128 devices in a mesh: grp: 4 (over x_hi, core), dp: 32 (over z, x_lo, y).
Axes of the slice: x: 4 (x_hi: 2, x_lo: 2; x = x_hi * 2 + x_lo), y: 4, z: 4, core: 2. Of those that a mesh axis runs over, the one named last changes fastest.
Arguments:
- normed: bfloat16 [65536, 1280], P(('grp', 'dp')), may hold values from -6 to 6
- w_in: bfloat16 [5120, 1280], replicated, may hold values from -0.15625 to 0.15625
- w_out: bfloat16 [1280, 2560], replicated, may hold values from -0.125 to 0.125
- cotangent: bfloat16 [65536, 1280], P(('grp', 'dp')), may hold values from -24 to 24
Outputs:
- grad_in: float32 [5120, 1280], P('dp')
- grad_out: float32 [1280, 2560], P('dp')
- grad_normed: bfloat16 [65536, 1280], P(('grp', 'dp'))
The draws below stay inside these ranges and needn't reach their ends.
All inputs are finite; a program needn't handle non-finite values.
Results may differ from the reference program's by a relative error of at most 0.005.
Values sent between devices are 32-bit elements; how exact they have to be, the bound alone decides.
No kernel may reach another device: no remote copies, remote signals or barrier semaphores. Data moves between devices by JAX's collectives and lax.ppermute only.
A program may use at most 192 MiB of HBM per device.

```python
import jax
import jax.numpy as jnp
from jax import lax

D = 1280
FW = 2560
TOK_DEV = 512
TOKENS = 65536


def strengthened(values, key, source, target, shards_of, factor):
    owner, partner = [(jnp.arange(values.shape[axis_at]) // (values.shape[axis_at] // shards_of)).reshape([-1 if axis == axis_at else 1 for axis in range(values.ndim)]) for axis_at in (source, target)]
    chosen = jax.random.permutation(key, shards_of)[partner]
    strong = (owner == chosen) | (owner == (partner + shards_of // 2) % shards_of)
    return jnp.where(strong, factor * values, values)


def shard_levels(key, extent, pieces, least, high):
    def one(axis_at, shards_of):
        draws = jax.random.uniform(jax.random.fold_in(jax.random.fold_in(key, 6), axis_at), (shards_of,), jnp.float32, least / len(pieces), high / len(pieces))
        return jnp.repeat(jnp.exp(draws), extent[axis_at] // shards_of).reshape((-1,) + (1,) * (len(extent) - axis_at - 1))

    factor_of = one(*pieces[0])
    for cut in pieces[1:]:
        factor_of = factor_of * one(*cut)
    return factor_of


def scatter_about(rng, extent, deviation, limit, split=(), dtype=jnp.bfloat16):
    values = jax.random.normal(rng, extent, jnp.float32) * deviation
    if len(split) > 0:
        values = shard_levels(rng, extent, split, -0.22, 0.18) * values
    return jnp.clip(values, min=-limit, max=limit).astype(dtype)


def bell_draw_with(rng, dims, deviation, reach, cuts, heavy, kind=jnp.bfloat16):
    array = deviation * jax.random.normal(rng, dims, jnp.float32)
    if cuts:
        array = array * shard_levels(rng, dims, cuts, -0.22, 0.18)
    return jnp.clip(strengthened(array, jax.random.fold_in(rng, 3), *heavy), -reach, reach).astype(kind)


def setup_inputs(seed: int = 0) -> dict:
    arg_keys = jax.random.split(jax.random.key(seed), 5)
    normed = scatter_about(arg_keys[0], (TOKENS, D), 1.0, 6.0, ((0, 128),))
    w_in = scatter_about(arg_keys[1], (2 * FW, D), D ** -0.5, 0.15625)
    w_out = scatter_about(arg_keys[2], (D, FW), FW ** -0.5, 0.125)
    cotangent = bell_draw_with(arg_keys[3], (TOKENS, D), 1.0, 24.0, ((0, 128),), (0, 1, 128, 5.5))
    return {"normed": normed, "w_in": w_in, "w_out": w_out, "cotangent": cotangent}


def cross_dot(left, right):
    return lax.dot_general(left, right, (((0,), (0,)), ((), ())), preferred_element_type=jnp.float32)


def block_terms(normed, w_in, w_out, cotangent):
    width = w_out.shape[1]
    proj = lax.dot_general(normed, w_in, (((1,), (1,)), ((), ())), preferred_element_type=jnp.float32)
    value = proj[:, :width]
    gate = proj[:, width:]
    cdf = 0.5 * (1.0 + lax.erf(gate * (2.0 ** -0.5)))
    density = jnp.exp(-0.5 * gate * gate) * ((2.0 * jnp.pi) ** -0.5)
    act = (value * gate * cdf).astype(jnp.bfloat16)
    dact = jnp.dot(cotangent, w_out, preferred_element_type=jnp.float32)
    d_value = dact * gate * cdf
    d_gate = dact * value * (cdf + gate * density)
    dproj = jnp.concatenate([d_value, d_gate], axis=1).astype(jnp.bfloat16)
    grad_normed = jnp.dot(dproj, w_in, preferred_element_type=jnp.float32).astype(jnp.bfloat16)
    return cross_dot(dproj, normed), cross_dot(cotangent, act), grad_normed


def reference(normed, w_in, w_out, cotangent):
    blocks = TOKENS // TOK_DEV
    normed_blocks = normed.reshape(blocks, TOK_DEV, D)
    cot_blocks = cotangent.reshape(blocks, TOK_DEV, D)

    def step(carry, pair):
        sum_in, sum_out = carry
        term_in, term_out, grad_block = block_terms(pair[0], w_in, w_out, pair[1])
        return (sum_in + term_in, sum_out + term_out), grad_block

    start = (jnp.zeros((2 * FW, D), jnp.float32), jnp.zeros((D, FW), jnp.float32))
    (sum_in, sum_out), grads = lax.scan(step, start, (normed_blocks, cot_blocks))
    factor = TOKENS ** -0.5
    return sum_in * factor, sum_out * factor, grads.reshape(TOKENS, D)
```

```python
import functools

import jax
import jax.numpy as jnp
from jax import lax
from jax.experimental import pallas as pl
from jax.experimental.pallas import tpu as pltpu
from jax.sharding import PartitionSpec as P

AXES = ("grp", "dp")
BF = jnp.bfloat16
F32 = jnp.float32
VMEM_LIMIT = 56 * 1024 * 1024


def place(x, y, z, c):
    return ((x // 2) * 2 + c) * 32 + z * 8 + (x % 2) * 4 + y


EVERY = [(x, y, z, c) for x in range(4) for y in range(4) for z in range(4) for c in range(2)]


def halving_pairs(axis, step):
    pairs = []
    for x, y, z, c in EVERY:
        at = [x, y, z]
        phase = (c + step) % 2
        at[axis] = (at[axis] + (1 if at[axis] % 2 == phase else -1)) % 4
        pairs.append((place(x, y, z, c), place(*at, c)))
    return pairs


CORE_PAIRS = [(place(x, y, z, c), place(x, y, z, 1 - c)) for x, y, z, c in EVERY]
FAR_PAIRS = [(place(x, y, z, c), place((x + 2) % 4, y, z, c)) for x, y, z, c in EVERY]


def owner_pairs(shift):
    return [
        (place((x + shift) % 4, y, z, c), place(x, y, z, c))
        for x, y, z, c in EVERY
        if x % 2 == c
    ]


def halves(at, core):
    keep0 = jnp.where(core == 0, jnp.where((at == 1) | (at == 2), 1, 0), jnp.where(at >= 2, 2, 0))
    keep1 = jnp.where(core == 0, 3 - keep0, keep0 + 1)
    send0 = jnp.where(core == 0, 1 - keep0, 2 - keep0)
    send1 = jnp.where(core == 0, 3 - send0, send0 + 1)
    own = jnp.where(core == 0, at // 2, at % 2)
    return (keep0, keep1), (send0, send1), own


def terms_kernel(core_ref, normed_ref, cot_ref, win_ref, wout_ref, dproj_ref, dproj_t_ref, act_ref, cot_t_ref):
    width = wout_ref.shape[1]
    normed = normed_ref[...].astype(BF)
    cot = cot_ref[...].astype(BF)
    w = win_ref[...].reshape(2 * width, win_ref.shape[-1])
    proj = lax.dot_general(normed, w, (((1,), (1,)), ((), ())), preferred_element_type=F32)
    dact = jnp.dot(cot, wout_ref[...], preferred_element_type=F32)
    value = proj[:, :width]
    gate = proj[:, width:]
    cdf = 0.5 * (1.0 + lax.erf(gate * (2.0 ** -0.5)))
    density = jnp.exp(-0.5 * gate * gate) * ((2.0 * jnp.pi) ** -0.5)
    gated = gate * cdf
    act_ref[0] = (value * gated).astype(BF)
    d_value = (dact * gated).astype(BF)
    d_gate = (dact * value * (cdf + gate * density)).astype(BF)
    dproj_ref[0, :, :width] = d_value
    dproj_ref[0, :, width:] = d_gate
    dproj_t_ref[0, 0] = d_value.T
    dproj_t_ref[0, 1] = d_gate.T

    @pl.when(pl.program_id(0) == 0)
    def _():
        cot_t_ref[...] = cot.T


def terms(core, normed, cot, win, wout, tile=256):
    tokens, dim = normed.shape
    width = win.shape[3]
    steps = tokens // tile
    last = steps - 1
    return pl.pallas_call(
        terms_kernel,
        grid_spec=pltpu.PrefetchScalarGridSpec(
            num_scalar_prefetch=1,
            grid=(2, steps),
            in_specs=[
                pl.BlockSpec((tile, dim), lambda k, t, c: (t, 0)),
                pl.BlockSpec((tile, dim), lambda k, t, c: (t, 0)),
                pl.BlockSpec((2, None, None, width, dim), lambda k, t, c: (0, k, c[0], 0, 0)),
                pl.BlockSpec((dim, width), lambda k, t, c: (0, k * 2 + c[0])),
            ],
            out_specs=[
                pl.BlockSpec((1, tile, 2 * width), lambda k, t, c: (k, t, 0)),
                pl.BlockSpec((1, 2, width, tile), lambda k, t, c: (k, 0, 0, t)),
                pl.BlockSpec((1, tile, width), lambda k, t, c: (k, t, 0)),
                pl.BlockSpec((dim, tile), lambda k, t, c: (0, jnp.where(k == 0, t, last))),
            ],
        ),
        out_shape=[
            jax.ShapeDtypeStruct((2, tokens, 2 * width), BF),
            jax.ShapeDtypeStruct((2, 2, width, tokens), BF),
            jax.ShapeDtypeStruct((2, tokens, width), BF),
            jax.ShapeDtypeStruct((dim, tokens), BF),
        ],
        compiler_params=pltpu.CompilerParams(vmem_limit_bytes=VMEM_LIMIT),
        cost_estimate=pl.CostEstimate(
            flops=2 * tokens * dim * width * 6, bytes_accessed=20 * 2**20, transcendentals=0
        ),
        name="terms",
    )(core, normed, cot, win, wout)


def grad_in_kernel(
    tab, d_own, d_oth, n_own, n_oth, a_send, a_keep, b_send, b_keep, a_buf, b_buf, n_bf, sems
):
    half = a_buf.shape[-1]
    block = b_buf.shape[2]
    n_bf[...] = n_oth[...].astype(BF)
    kept = tab[0]
    copies = []
    for slot, (which, out) in enumerate(((1 - kept, a_send), (kept, a_keep))):
        a_buf[slot] = jnp.dot(
            d_own[which], n_own[:, :half], preferred_element_type=F32
        ) + jnp.dot(d_oth[which], n_bf[:, :half], preferred_element_type=F32)
        copy = pltpu.make_async_copy(a_buf.at[slot], out, sems.at[slot])
        copy.start()
        copies.append(copy)
    at = 2
    for which in range(2):
        total = jnp.dot(d_own[which], n_own[:, half:], preferred_element_type=F32) + jnp.dot(
            d_oth[which], n_bf[:, half:], preferred_element_type=F32
        )
        b_buf[which] = total.reshape(4, block, half)
        for i, (quarter, out) in enumerate(
            ((tab[3], b_send), (tab[4], b_send), (tab[1], b_keep), (tab[2], b_keep))
        ):
            copy = pltpu.make_async_copy(b_buf.at[which, quarter], out.at[which, i % 2], sems.at[at])
            at += 1
            copy.start()
            copies.append(copy)
    for copy in copies:
        copy.wait()


def grad_in_chunk(tab, d_own, d_oth, n_own, n_oth, chunk):
    tokens, dim = n_own.shape
    width = d_own.shape[2]
    half = dim // 2
    block = width // 4
    one = jax.ShapeDtypeStruct((width, half), F32)
    two = jax.ShapeDtypeStruct((2, 2, block, half), F32)
    d_spec = pl.BlockSpec((None, 2, width, tokens), lambda i, t: (chunk, 0, 0, 0))
    n_spec = pl.BlockSpec((tokens, dim), lambda i, t: (0, 0))
    return pl.pallas_call(
        grad_in_kernel,
        grid_spec=pltpu.PrefetchScalarGridSpec(
            num_scalar_prefetch=1,
            grid=(1,),
            in_specs=[d_spec, d_spec, n_spec, n_spec],
            out_specs=[pl.BlockSpec(memory_space=pl.ANY)] * 4,
            scratch_shapes=[
                pltpu.VMEM((2, width, half), F32),
                pltpu.VMEM((2, 4, block, half), F32),
                pltpu.VMEM((tokens, dim), BF),
                pltpu.SemaphoreType.DMA((10,)),
            ],
        ),
        out_shape=[one, one, two, two],
        compiler_params=pltpu.CompilerParams(vmem_limit_bytes=VMEM_LIMIT),
        cost_estimate=pl.CostEstimate(
            flops=2 * 2 * tokens * dim * width * 2, bytes_accessed=12 * 2**20, transcendentals=0
        ),
        name="grad_in_chunk",
    )(tab, d_own, d_oth, n_own, n_oth)


def grad_out_kernel(tab, c_own, c_oth, act_own, act_oth, send, keep, buf, sems):
    total = jnp.dot(c_own[...], act_own[...], preferred_element_type=F32) + jnp.dot(
        c_oth[...], act_oth[...], preferred_element_type=F32
    )
    buf[...] = total.reshape(buf.shape)
    kept = tab[0]
    copies = []
    for i in range(4):
        copies.append(pltpu.make_async_copy(buf.at[i, 1 - kept], send.at[i], sems.at[0, i]))
        copies.append(pltpu.make_async_copy(buf.at[i, kept], keep.at[i], sems.at[1, i]))
    for copy in copies:
        copy.start()
    for copy in copies:
        copy.wait()


def grad_out_chunk(tab, c_own, c_oth, act_own, act_oth, chunk):
    dim, tokens = c_own.shape
    width = act_own.shape[2]
    block = dim // 8
    one = jax.ShapeDtypeStruct((4, block, width), F32)
    c_spec = pl.BlockSpec((dim, tokens), lambda i, t: (0, 0))
    a_spec = pl.BlockSpec((None, tokens, width), lambda i, t: (chunk, 0, 0))
    return pl.pallas_call(
        grad_out_kernel,
        grid_spec=pltpu.PrefetchScalarGridSpec(
            num_scalar_prefetch=1,
            grid=(1,),
            in_specs=[c_spec, c_spec, a_spec, a_spec],
            out_specs=[pl.BlockSpec(memory_space=pl.ANY)] * 2,
            scratch_shapes=[
                pltpu.VMEM((4, 2, block, width), F32),
                pltpu.SemaphoreType.DMA((2, 4)),
            ],
        ),
        out_shape=[one, one],
        compiler_params=pltpu.CompilerParams(vmem_limit_bytes=VMEM_LIMIT),
        cost_estimate=pl.CostEstimate(
            flops=2 * 2 * tokens * dim * width, bytes_accessed=8 * 2**20, transcendentals=0
        ),
        name="grad_out_chunk",
    )(tab, c_own, c_oth, act_own, act_oth)


def back_kernel(core_ref, d_ref, w_ref, *rest):
    rest, total = rest[:-1], rest[-1]
    out = rest[-1]
    w = w_ref[...].reshape(2 * w_ref.shape[1], w_ref.shape[2])
    part = jnp.dot(d_ref[...], w, preferred_element_type=F32)

    @pl.when(pl.program_id(0) == 0)
    def _():
        total[...] = part

    @pl.when(pl.program_id(0) == 1)
    def _():
        whole = total[...] + part
        if len(rest) > 1:
            whole = whole + rest[0][...]
        out[...] = whole.astype(out.dtype)


def back(core, dproj, win, dtype, *more):
    _, tokens, both = dproj.shape
    width, dim = win.shape[3:]
    whole = pl.BlockSpec((tokens, dim), lambda k, c: (0, 0))
    return pl.pallas_call(
        back_kernel,
        grid_spec=pltpu.PrefetchScalarGridSpec(
            num_scalar_prefetch=1,
            grid=(2,),
            in_specs=[
                pl.BlockSpec((None, tokens, both), lambda k, c: (k, 0, 0)),
                pl.BlockSpec((2, None, None, width, dim), lambda k, c: (0, k, c[0], 0, 0)),
            ]
            + [whole] * len(more),
            out_specs=whole,
            scratch_shapes=[pltpu.VMEM((tokens, dim), F32)],
        ),
        out_shape=jax.ShapeDtypeStruct((tokens, dim), dtype),
        compiler_params=pltpu.CompilerParams(vmem_limit_bytes=VMEM_LIMIT),
        cost_estimate=pl.CostEstimate(
            flops=2 * tokens * dim * both * 2, bytes_accessed=12 * 2**20, transcendentals=0
        ),
        name="back",
    )(core, dproj, win, *more)


def move(array, pairs):
    return lax.ppermute(array, AXES, pairs)


def pick(array, axis, index):
    return lax.dynamic_index_in_dim(array, index, axis, keepdims=False)


def pick_two(array, axis, indices):
    return jnp.concatenate([lax.dynamic_slice_in_dim(array, i, 1, axis) for i in indices], axis)


def halve(array, axis_at, mesh_axis, at, core):
    keep, send, own = halves(at, core)
    got = move(pick_two(array, axis_at, send), halving_pairs(mesh_axis, 0))
    array = pick_two(array, axis_at, keep) + got
    return finish(array, axis_at, mesh_axis, own)


def finish(array, axis_at, mesh_axis, own):
    got = move(pick(array, axis_at, 1 - own), halving_pairs(mesh_axis, 1))
    return pick(array, axis_at, own) + got


def local(normed, w_in, w_out, cotangent):
    dim = normed.shape[1]
    width = w_out.shape[1] // 4
    factor = (normed.shape[0] * lax.axis_size("dp") * lax.axis_size("grp")) ** (-0.5)
    grp, dp = lax.axis_index("grp"), lax.axis_index("dp")
    core = grp % 2
    z, x, y = dp // 8, (grp // 2) * 2 + (dp % 8) // 4, dp % 4
    win = w_in.reshape(2, 2, 2, width, dim)
    core_1 = core.reshape(1).astype(jnp.int32)

    wide = lax.optimization_barrier((normed.astype(F32), cotangent.astype(F32)))
    n_oth = move(wide[0], CORE_PAIRS)
    c_oth = move(wide[1], CORE_PAIRS)
    d_own, dt_own, act_own, ct_own = terms(core_1, normed, cotangent, win, w_out)
    d_oth, dt_oth, act_oth, ct_oth = terms(core_1, n_oth, c_oth, win, w_out)

    keep_z, _, own_z = halves(z, core)
    keep_x, _, own_x = halves(x, core)
    keep_y, send_y, own_y = halves(y, core)
    own_z_chunk = z % 2
    own_x_chunk = jnp.where(core == 0, x // 2, (x // 2) ^ (x % 2))

    a, b, c = [], [], []
    for chunk in range(2):
        kept_gate = jnp.where(core == 0, keep_z[0] ^ chunk, keep_z[0] // 2)
        tab = jnp.stack([kept_gate, *keep_y, *send_y]).astype(jnp.int32)
        kept_x = jnp.where(core == 0, keep_x[0] ^ chunk, (keep_x[0] // 2) ^ chunk)
        c_send, c_keep = grad_out_chunk(
            kept_x.reshape(1).astype(jnp.int32), ct_own, ct_oth, act_own, act_oth, chunk
        )
        a_send, a_keep, b_send, b_keep = grad_in_chunk(tab, dt_own, dt_oth, normed, n_oth, chunk)
        c.append(c_keep + move(c_send, halving_pairs(0, 0)))
        a.append(a_keep + move(a_send, halving_pairs(2, 0)))
        b.append(b_keep + move(b_send, halving_pairs(1, 0)))

    back_oth = back(core_1, d_oth, win, F32)
    grad_normed = back(core_1, d_own, win, BF, move(back_oth, CORE_PAIRS))

    half = dim // 2
    a = finish(jnp.stack(a), 0, 2, own_z_chunk).reshape(4, 4, width // 16, half)
    b = finish(jnp.stack(b), 2, 1, own_y).reshape(2, 2, 4, width // 16, half)
    c = finish(jnp.stack(c), 0, 0, own_x_chunk).reshape(4, 4, dim // 32, width)

    a = halve(a, 0, 1, y, core)
    b = halve(b, 2, 0, x, core)
    c = halve(c, 0, 2, z, core)
    b = b.transpose(1, 0, 2, 3).reshape(4, width // 16, half)

    a = halve(a, 0, 0, x, core)
    b = halve(b, 0, 2, z, core)
    c = halve(c, 0, 1, y, core)

    piece_in = jnp.concatenate([a, b], axis=1) * factor
    piece_out = c * factor
    far_out = move(piece_out, FAR_PAIRS)
    mine_in = [piece_in] + [move(piece_in, owner_pairs(s)) for s in (1, 2, 3)]
    stacked = jnp.stack(mine_in + mine_in)
    rows_in = lax.dynamic_slice_in_dim(stacked, (4 - x) % 4, 4, 0).reshape(width // 4, dim)
    pair_out = jnp.stack([piece_out, far_out, piece_out])
    rows_out = lax.dynamic_slice_in_dim(pair_out, own_x_chunk, 2, 0)

    other_in = move(rows_in, CORE_PAIRS)
    other_out = move(rows_out, CORE_PAIRS)
    grad_in = jnp.where(x % 2 == core, rows_in, other_in)
    first = jnp.where(core == 0, rows_out, other_out)
    second = jnp.where(core == 0, other_out, rows_out)
    grad_out = jnp.concatenate([first[0], second[0], first[1], second[1]], axis=1)
    return (grad_in, grad_out, grad_normed)


def solution(mesh):
    placed = (P(AXES, None), P(), P(), P(AXES, None))
    return jax.shard_map(
        local,
        mesh=mesh,
        in_specs=placed,
        out_specs=(P("dp", None), P("dp", None), P(AXES, None)),
        check_vma=False,
    )
```

```python
import functools

import jax
import jax.numpy as jnp
import numpy as np
from jax import lax
from jax.experimental import pallas as pl
from jax.experimental.pallas import tpu as pltpu
from jax.sharding import PartitionSpec as P

AXES = ("grp", "dp")
BF = jnp.bfloat16
F32 = jnp.float32
VMEM_LIMIT = 56 * 1024 * 1024


def place(x, y, z, c):
    return ((x // 2) * 2 + c) * 32 + z * 8 + (x % 2) * 4 + y


EVERY = [(x, y, z, c) for x in range(4) for y in range(4) for z in range(4) for c in range(2)]


def partner(i, core, step):
    return (i + (1 if i % 2 == (core + step) % 2 else -1)) % 4


def halving_pairs(axis, step):
    pairs = []
    for x, y, z, c in EVERY:
        at = [x, y, z]
        at[axis] = partner(at[axis], c, step)
        pairs.append((place(x, y, z, c), place(*at, c)))
    return pairs


X0, X1 = halving_pairs(0, 0), halving_pairs(0, 1)
Y0, Y1 = halving_pairs(1, 0), halving_pairs(1, 1)
Z0, Z1 = halving_pairs(2, 0), halving_pairs(2, 1)
CORE_PAIRS = [(place(x, y, z, c), place(x, y, z, 1 - c)) for x, y, z, c in EVERY]
FAR_PAIRS = [(place(x, y, z, c), place((x + 2) % 4, y, z, c)) for x, y, z, c in EVERY]


def owner_pairs(shift):
    return [
        (place((x + shift) % 4, y, z, c), place(x, y, z, c))
        for x, y, z, c in EVERY
        if x % 2 == c
    ]


def ring_order(i, core):
    first, second = partner(i, core, 0), partner(i, core, 1)
    return [partner(first, core, 1), first, second, i]


CORE, CHUNK, KIND, HALF, XAT, YAT, ZAT = 0, 1, 3, 7, 9, 13, 17
OWN_X, OWN_HALF, ROLL, IS_OWNER, WIDTH = 21, 22, 23, 24, 32


def table():
    rows = np.zeros((len(EVERY), WIDTH), np.int32)
    for x, y, z, c in EVERY:
        row = rows[place(x, y, z, c)]
        row[CORE] = c
        xs, ys, zs = ring_order(x, c), ring_order(y, c), ring_order(z, c)
        row[CHUNK], row[CHUNK + 1] = 1 - z % 2, z % 2
        row[KIND : KIND + 4] = [zs[1] // 2, zs[2] // 2, zs[0] // 2, zs[3] // 2]
        labels = {i: (i % 2, i // 2 if c == 0 else (i // 2) ^ (i % 2)) for i in range(4)}
        for k in range(2):
            (row[HALF + k],) = [labels[i][0] for i in xs[2:] if labels[i][1] == row[CHUNK + k]]
        for at, order in ((XAT, xs), (YAT, ys), (ZAT, zs)):
            for rank, i in enumerate(order):
                row[at + rank] = i
        row[OWN_X] = int(row[CHUNK + 1] == labels[x][1])
        row[OWN_HALF] = labels[x][1]
        row[ROLL] = (4 - x) % 4
        row[IS_OWNER] = int(x % 2 == c)
    return rows


TABLE = table()


NT = (((1,), (1,)), ((), ()))
TN = (((0,), (0,)), ((), ()))


def chunk_kernel(chunk, sources, begin, final, tab, *refs):
    refs = list(refs)
    take = lambda n: [refs.pop(0) for _ in range(n)]
    win, wout = take(2)
    tokens = [take(2) for _ in range(sources)]
    start = take(2) if begin else None
    outs = take(6 if final else 2)
    d_outs = take(sources)
    w, wo = take(2)
    raw = [take(2) for _ in range(sources)]
    nb, cb, d, act, gin, gout, sems = take(7)
    width, dim = w.shape[1:]
    half = dim // 2
    core, block = tab[CORE], tab[CHUNK + chunk]

    loads = []

    def load(source, target):
        copy = pltpu.make_async_copy(source, target, sems.at[len(loads)])
        loads.append(copy)
        copy.start()
        return copy

    load_w = [load(win.at[kind, block, core], w.at[kind]) for kind in range(2)]
    load_n = [load(tokens[s][0], raw[s][0]) for s in range(sources)]
    load_c = [load(tokens[s][1], raw[s][1]) for s in range(sources)]
    column = pl.multiple_of((block * 2 + core) * width, 128)
    load_wo = load(wout.at[:, pl.ds(column, width)], wo)
    load_begin = [load(start[0], gin), load(start[1], gout)] if begin else []

    stores = []

    def store(source, target, sem):
        pltpu.make_async_copy(source, target, sems.at[sem]).start()

    for copy in load_w:
        copy.wait()
    for s in range(sources):
        load_n[s].wait()
        nb[s] = raw[s][0][...].astype(BF)
        proj = lax.dot_general(
            nb[s], w[...].reshape(2 * width, dim), NT, preferred_element_type=F32
        )
        load_c[s].wait()
        cb[s] = raw[s][1][...].astype(BF)
        if s == 0:
            load_wo.wait()
        dact = jnp.dot(cb[s], wo[...], preferred_element_type=F32)
        value = proj[:, :width]
        gate = proj[:, width:]
        cdf = 0.5 * (1.0 + lax.erf(gate * (2.0 ** -0.5)))
        density = jnp.exp(-0.5 * gate * gate) * ((2.0 * jnp.pi) ** -0.5)
        gated = gate * cdf
        act[s] = (value * gated).astype(BF)
        d[s, 0] = (dact * gated).astype(BF)
        d[s, 1] = (dact * value * (cdf + gate * density)).astype(BF)
        store(d.at[s], d_outs[s], 16 + s)
        stores.append(pltpu.make_async_copy(d.at[s], d_outs[s], sems.at[16 + s]))

    def total(left, right, place_at):
        parts = [
            lax.dot_general(left(s), right(s), TN, preferred_element_type=F32)
            for s in range(sources)
        ]
        whole = functools.reduce(lambda p, q: p + q, parts)
        if begin:
            whole = whole + place_at[...]
        place_at[...] = whole

    for copy in load_begin:
        copy.wait()
    small = width // 16
    for slot in range(2):
        kind = tab[KIND + 2 * chunk + slot]
        total(lambda s: d[s, kind], lambda s: nb[s], gin.at[slot])
        if final:
            for y in range(4):
                for x in range(4):
                    at = (tab[YAT + y] * 4 + tab[XAT + x]) * small
                    rows = pl.ds(pl.multiple_of(at, 8), small)
                    store(gin.at[slot, rows, pl.ds(0, half)], outs[slot].at[y, x], 18 + slot)
                    store(
                        gin.at[slot, rows, pl.ds(half, half)],
                        outs[2 + y // 2].at[slot, y % 2, x],
                        20 + y // 2,
                    )
    total(lambda s: cb[s], lambda s: act[s], gout)
    if final:
        tiny = dim // 32
        kept = tab[HALF + chunk]
        for slot, x in ((0, 1 - kept), (1, kept)):
            for z in range(4):
                for y in range(4):
                    at = ((tab[ZAT + z] * 2 + x) * 4 + tab[YAT + y]) * tiny
                    rows = pl.ds(pl.multiple_of(at, 8), tiny)
                    store(gout.at[rows], outs[4 + slot].at[z, y], 22 + slot)
    else:
        store(gin, outs[0], 18)
        store(gout, outs[1], 19)
    for copy in stores:
        copy.wait()
    if final:
        for i in range(6):
            pltpu.make_async_copy(outs[i], outs[i], sems.at[18 + i]).wait()
    else:
        pltpu.make_async_copy(gin, outs[0], sems.at[18]).wait()
        pltpu.make_async_copy(gout, outs[1], sems.at[19]).wait()


def chunk_call(tab, win, wout, tokens, chunk, begin=None, final=True):
    count, dim = tokens[0][0].shape
    width = win.shape[3]
    sources = len(tokens)
    if final:
        a = jax.ShapeDtypeStruct((4, 4, width // 16, dim // 2), F32)
        b = jax.ShapeDtypeStruct((2, 2, 4, width // 16, dim // 2), F32)
        c = jax.ShapeDtypeStruct((4, 4, dim // 32, width), F32)
        outs = [a, a, b, b, c, c]
    else:
        outs = [
            jax.ShapeDtypeStruct((2, width, dim), F32),
            jax.ShapeDtypeStruct((dim, width), F32),
        ]
    outs = outs + [jax.ShapeDtypeStruct((2, count, width), BF)] * sources
    operands = [win, wout] + [t for pair in tokens for t in pair] + list(begin or ())
    anywhere = pl.BlockSpec(memory_space=pl.ANY)
    scratch = [pltpu.VMEM((2, width, dim), BF), pltpu.VMEM((dim, width), BF)]
    scratch += [pltpu.VMEM((count, dim), t.dtype) for pair in tokens for t in pair]
    scratch += [
        pltpu.VMEM((sources, count, dim), BF),
        pltpu.VMEM((sources, count, dim), BF),
        pltpu.VMEM((sources, 2, count, width), BF),
        pltpu.VMEM((sources, count, width), BF),
        pltpu.VMEM((2, width, dim), F32),
        pltpu.VMEM((dim, width), F32),
        pltpu.SemaphoreType.DMA((24,)),
    ]
    return pl.pallas_call(
        functools.partial(chunk_kernel, chunk, sources, begin is not None, final),
        grid_spec=pltpu.PrefetchScalarGridSpec(
            num_scalar_prefetch=1,
            grid=(1,),
            in_specs=[anywhere] * len(operands),
            out_specs=[anywhere] * len(outs),
            scratch_shapes=scratch,
        ),
        out_shape=outs,
        compiler_params=pltpu.CompilerParams(vmem_limit_bytes=VMEM_LIMIT),
        cost_estimate=pl.CostEstimate(
            flops=12 * count * sources * dim * width * 2,
            bytes_accessed=16 * 2**20,
            transcendentals=0,
        ),
        name="chunk",
    )(tab, *operands)


def back_kernel(tab, d0_ref, d1_ref, w_ref, *rest):
    rest, total = rest[:-1], rest[-1]
    out = rest[-1]
    w = w_ref[...].reshape(2 * w_ref.shape[1], w_ref.shape[2])
    straight = tab[CHUNK] == 0
    low = jnp.where(straight, d0_ref[...], d1_ref[...])
    high = jnp.where(straight, d1_ref[...], d0_ref[...])
    part = jnp.dot(jnp.concatenate([low, high], axis=1), w, preferred_element_type=F32)

    @pl.when(pl.program_id(0) == 0)
    def _():
        total[...] = part

    @pl.when(pl.program_id(0) == 1)
    def _():
        whole = total[...] + part
        if len(rest) > 1:
            whole = whole + rest[0][...]
        out[...] = whole.astype(out.dtype)


def back(tab, d0, d1, win, dtype, *more):
    _, tokens, width = d0.shape
    dim = win.shape[4]
    whole = pl.BlockSpec((tokens, dim), lambda k, t: (0, 0))
    d_spec = pl.BlockSpec((None, tokens, width), lambda k, t: (k, 0, 0))
    return pl.pallas_call(
        back_kernel,
        grid_spec=pltpu.PrefetchScalarGridSpec(
            num_scalar_prefetch=1,
            grid=(2,),
            in_specs=[
                d_spec,
                d_spec,
                pl.BlockSpec((None, 2, None, width, dim), lambda k, t: (k, 0, t[CORE], 0, 0)),
            ]
            + [whole] * len(more),
            out_specs=whole,
            scratch_shapes=[pltpu.VMEM((tokens, dim), F32)],
        ),
        out_shape=jax.ShapeDtypeStruct((tokens, dim), dtype),
        compiler_params=pltpu.CompilerParams(vmem_limit_bytes=VMEM_LIMIT),
        cost_estimate=pl.CostEstimate(
            flops=8 * tokens * dim * width, bytes_accessed=12 * 2**20, transcendentals=0
        ),
        name="back",
    )(tab, d0, d1, win, *more)


def move(array, pairs):
    return lax.ppermute(array, AXES, pairs)


def local(normed, w_in, w_out, cotangent):
    dim = normed.shape[1]
    width = w_out.shape[1] // 4
    factor = (normed.shape[0] * lax.axis_size("dp") * lax.axis_size("grp")) ** (-0.5)
    tab = lax.dynamic_index_in_dim(jnp.asarray(TABLE), lax.axis_index(AXES), 0, keepdims=False)
    win = w_in.reshape(2, 2, 2, width, dim)

    wide = lax.optimization_barrier((normed.astype(F32), cotangent.astype(F32)))
    own = normed, cotangent
    other = move(wide[0], CORE_PAIRS), move(wide[1], CORE_PAIRS)
    gin, gout, d0_own = chunk_call(tab, win, w_out, [own], 0, final=False)
    *first, d0_oth = chunk_call(tab, win, w_out, [other], 0, begin=(gin, gout))
    got_a0, got_b0, got_c0 = move(first[0], Z0), move(first[2], Y0), move(first[4], X0)
    tab, _ = lax.optimization_barrier((tab, first[0]))
    *second, d1_oth, d1_own = chunk_call(tab, win, w_out, [other, own], 1)
    got_a1, got_b1, got_c1 = move(second[0], Z0), move(second[2], Y0), move(second[4], X0)

    d0_oth, got_a0, got_b0, got_c0 = lax.optimization_barrier((d0_oth, got_a0, got_b0, got_c0))
    back_oth = back(tab, d0_oth, d1_oth, win, F32)
    grad_normed = back(tab, d0_own, d1_own, win, BF, move(back_oth, CORE_PAIRS))

    a0, a1 = first[1] + got_a1, second[1] + got_a0
    b = jnp.stack([first[3] + got_b0, second[3] + got_b1])
    c0, c1 = first[5] + got_c0, second[5] + got_c1
    own_first = tab[OWN_X] == 0

    a = a1 + move(a0, Z1)
    b = b[:, :, 1] + move(b[:, :, 0], Y1)
    c = jnp.where(own_first, c0, c1) + move(jnp.where(own_first, c1, c0), X1)

    a = a[2:] + move(a[:2], Y0)
    b = b[:, :, 2:] + move(b[:, :, :2], X0)
    c = c[2:] + move(c[:2], Z0)

    a = a[1] + move(a[0], Y1)
    b = b[:, :, 1] + move(b[:, :, 0], X1)
    c = c[1] + move(c[0], Z1)

    a = a[2:] + move(a[:2], X0)
    b = b[:, 1] + move(b[::-1, 0], Z0)
    c = c[2:] + move(c[:2], Y0)

    a = a[1] + move(a[0], X1)
    b = b[1] + move(b[0], Z1)
    c = c[1] + move(c[0], Y1)

    piece_in = jnp.concatenate([a, b], axis=1) * factor
    piece_out = c * factor
    far_out = move(piece_out, FAR_PAIRS)
    mine_in = [piece_in] + [move(piece_in, owner_pairs(s)) for s in (1, 2, 3)]
    stacked = jnp.stack(mine_in + mine_in)
    rows_in = lax.dynamic_slice_in_dim(stacked, tab[ROLL], 4, 0).reshape(width // 4, dim)
    low_half = tab[OWN_HALF] == 0
    rows_out = jnp.stack(
        [jnp.where(low_half, piece_out, far_out), jnp.where(low_half, far_out, piece_out)]
    )

    other_in = move(rows_in, CORE_PAIRS)
    other_out = move(rows_out, CORE_PAIRS)
    grad_in = jnp.where(tab[IS_OWNER] == 1, rows_in, other_in)
    core_zero = tab[CORE] == 0
    low = jnp.where(core_zero, rows_out, other_out)
    high = jnp.where(core_zero, other_out, rows_out)
    grad_out = jnp.concatenate([low[0], high[0], low[1], high[1]], axis=1)
    return (grad_in, grad_out, grad_normed)


def solution(mesh):
    placed = (P(AXES, None), P(), P(), P(AXES, None))
    return jax.shard_map(
        local,
        mesh=mesh,
        in_specs=placed,
        out_specs=(P("dp", None), P("dp", None), P(AXES, None)),
        check_vma=False,
    )
```

```python
import functools

import jax
import jax.numpy as jnp
import numpy as np
from jax import lax
from jax.experimental import pallas as pl
from jax.experimental.pallas import tpu as pltpu
from jax.sharding import PartitionSpec as P

AXES = ("grp", "dp")
BF = jnp.bfloat16
F32 = jnp.float32
VMEM_LIMIT = 56 * 1024 * 1024


def place(x, y, z, c):
    return ((x // 2) * 2 + c) * 32 + z * 8 + (x % 2) * 4 + y


EVERY = [(x, y, z, c) for x in range(4) for y in range(4) for z in range(4) for c in range(2)]


def partner(i, core, step):
    return (i + (1 if i % 2 == (core + step) % 2 else -1)) % 4


def halving_pairs(axis, step):
    pairs = []
    for x, y, z, c in EVERY:
        at = [x, y, z]
        at[axis] = partner(at[axis], c, step)
        pairs.append((place(x, y, z, c), place(*at, c)))
    return pairs


X0, X1 = halving_pairs(0, 0), halving_pairs(0, 1)
Y0, Y1 = halving_pairs(1, 0), halving_pairs(1, 1)
Z0, Z1 = halving_pairs(2, 0), halving_pairs(2, 1)
CORE_PAIRS = [(place(x, y, z, c), place(x, y, z, 1 - c)) for x, y, z, c in EVERY]
FAR_PAIRS = [(place(x, y, z, c), place((x + 2) % 4, y, z, c)) for x, y, z, c in EVERY]


def owner_pairs(shift):
    return [
        (place((x + shift) % 4, y, z, c), place(x, y, z, c))
        for x, y, z, c in EVERY
        if x % 2 == c
    ]


def ring_order(i, core):
    first, second = partner(i, core, 0), partner(i, core, 1)
    return [partner(first, core, 1), first, second, i]


CORE, CHUNK, KIND, HALF, XAT, YAT, ZAT = 0, 1, 3, 7, 9, 13, 17
OWN_X, OWN_HALF, X, IS_OWNER, WIDTH = 21, 22, 23, 24, 32


def table():
    rows = np.zeros((len(EVERY), WIDTH), np.int32)
    for x, y, z, c in EVERY:
        row = rows[place(x, y, z, c)]
        row[CORE] = c
        xs, ys, zs = ring_order(x, c), ring_order(y, c), ring_order(z, c)
        row[CHUNK], row[CHUNK + 1] = 1 - z % 2, z % 2
        row[KIND : KIND + 4] = [zs[1] // 2, zs[2] // 2, zs[0] // 2, zs[3] // 2]
        labels = {i: (i % 2, i // 2 if c == 0 else (i // 2) ^ (i % 2)) for i in range(4)}
        for k in range(2):
            (row[HALF + k],) = [labels[i][0] for i in xs[2:] if labels[i][1] == row[CHUNK + k]]
        for at, order in ((XAT, xs), (YAT, ys), (ZAT, zs)):
            for rank, i in enumerate(order):
                row[at + rank] = i
        row[OWN_X] = int(row[CHUNK + 1] == labels[x][1])
        row[OWN_HALF] = labels[x][1]
        row[X] = x
        row[IS_OWNER] = int(x % 2 == c)
    return rows


TABLE = table()


NT = (((1,), (1,)), ((), ()))
TN = (((0,), (0,)), ((), ()))


def row_of(index, table):
    class Row:
        def __getitem__(self, at):
            return table[index[0] * WIDTH + at]

    return Row()


def chunk_kernel(chunk, sources, begin, final, index, table, *refs):
    tab = row_of(index, table)
    refs = list(refs)
    take = lambda n: [refs.pop(0) for _ in range(n)]
    win, wout = take(2)
    tokens = [take(2) for _ in range(sources)]
    start = take(2) if begin else None
    outs = take(6 if final else 2)
    (d_out,) = take(1)
    w, wo = take(2)
    raw = [take(2) for _ in range(sources)]
    nb, cb, d, act, gin, gout, sems = take(7)
    width, dim = w.shape[1:]
    half = dim // 2
    count = raw[0][0].shape[0]
    core, block = tab[CORE], tab[CHUNK + chunk]

    loads = []

    def load(source, target):
        copy = pltpu.make_async_copy(source, target, sems.at[len(loads)])
        loads.append(copy)
        copy.start()
        return copy

    column = pl.multiple_of((block * 2 + core) * width, 128)
    load_wo = load(wout.at[:, pl.ds(column, width)], wo)
    load_c = [load(tokens[s][1], raw[s][1]) for s in range(sources)]
    load_w = [load(win.at[kind, block, core], w.at[kind]) for kind in range(2)]
    load_n = [load(tokens[s][0], raw[s][0]) for s in range(sources)]
    load_begin = [load(start[0], gin), load(start[1], gout)] if begin else []

    stores = []

    def store(source, target, sem):
        pltpu.make_async_copy(source, target, sems.at[sem]).start()

    load_wo.wait()
    for s in range(sources):
        here = pl.ds(s * count, count)
        load_c[s].wait()
        cb[here] = raw[s][1][...].astype(BF)
        dact = jnp.dot(cb[here], wo[...], preferred_element_type=F32)
        load_n[s].wait()
        nb[here] = raw[s][0][...].astype(BF)
        if s == 0:
            for copy in load_w:
                copy.wait()
        proj = lax.dot_general(
            nb[here], w[...].reshape(2 * width, dim), NT, preferred_element_type=F32
        )
        value = proj[:, :width]
        gate = proj[:, width:]
        cdf = 0.5 * (1.0 + lax.erf(gate * (2.0 ** -0.5)))
        density = jnp.exp(-0.5 * gate * gate) * ((2.0 * jnp.pi) ** -0.5)
        gated = gate * cdf
        act[here] = (value * gated).astype(BF)
        d[0, here] = (dact * gated).astype(BF)
        d[1, here] = (dact * value * (cdf + gate * density)).astype(BF)
    for kind in range(2):
        store(d.at[kind], d_out.at[kind], 16 + kind)
        stores.append(pltpu.make_async_copy(d.at[kind], d_out.at[kind], sems.at[16 + kind]))

    def total(left, right, place_at):
        whole = lax.dot_general(left, right, TN, preferred_element_type=F32)
        if begin:
            whole = whole + place_at[...]
        place_at[...] = whole

    for copy in load_begin:
        copy.wait()
    small = width // 16
    for slot in range(2):
        kind = tab[KIND + 2 * chunk + slot]
        total(d[kind], nb[...], gin.at[slot])
        if final:
            for y in range(4):
                for x in range(4):
                    at = (tab[YAT + y] * 4 + tab[XAT + x]) * small
                    rows = pl.ds(pl.multiple_of(at, 8), small)
                    store(gin.at[slot, rows, pl.ds(0, half)], outs[slot].at[y, x], 18 + slot)
                    store(
                        gin.at[slot, rows, pl.ds(half, half)],
                        outs[2 + y // 2].at[y % 2, x, slot],
                        20 + y // 2,
                    )
    total(cb[...], act[...], gout)
    if final:
        tiny = dim // 32
        kept = tab[HALF + chunk]
        for slot, x in ((0, 1 - kept), (1, kept)):
            for z in range(4):
                for y in range(4):
                    at = ((tab[ZAT + z] * 2 + x) * 4 + tab[YAT + y]) * tiny
                    rows = pl.ds(pl.multiple_of(at, 8), tiny)
                    store(gout.at[rows], outs[4 + slot].at[z, y], 22 + slot)
    else:
        store(gin, outs[0], 18)
        store(gout, outs[1], 19)
    for copy in stores:
        copy.wait()
    if final:
        for i in range(6):
            pltpu.make_async_copy(outs[i], outs[i], sems.at[18 + i]).wait()
    else:
        pltpu.make_async_copy(gin, outs[0], sems.at[18]).wait()
        pltpu.make_async_copy(gout, outs[1], sems.at[19]).wait()


def chunk_call(place_at, win, wout, tokens, chunk, begin=None, final=True):
    count, dim = tokens[0][0].shape
    width = win.shape[3]
    sources = len(tokens)
    if final:
        a = jax.ShapeDtypeStruct((4, 4, width // 16, dim // 2), F32)
        b = jax.ShapeDtypeStruct((2, 4, 2, width // 16, dim // 2), F32)
        c = jax.ShapeDtypeStruct((4, 4, dim // 32, width), F32)
        outs = [a, a, b, b, c, c]
    else:
        outs = [
            jax.ShapeDtypeStruct((2, width, dim), F32),
            jax.ShapeDtypeStruct((dim, width), F32),
        ]
    outs = outs + [jax.ShapeDtypeStruct((2, sources * count, width), BF)]
    operands = [win, wout] + [t for pair in tokens for t in pair] + list(begin or ())
    anywhere = pl.BlockSpec(memory_space=pl.ANY)
    scratch = [pltpu.VMEM((2, width, dim), BF), pltpu.VMEM((dim, width), BF)]
    scratch += [pltpu.VMEM((count, dim), t.dtype) for pair in tokens for t in pair]
    scratch += [
        pltpu.VMEM((sources * count, dim), BF),
        pltpu.VMEM((sources * count, dim), BF),
        pltpu.VMEM((2, sources * count, width), BF),
        pltpu.VMEM((sources * count, width), BF),
        pltpu.VMEM((2, width, dim), F32),
        pltpu.VMEM((dim, width), F32),
        pltpu.SemaphoreType.DMA((24,)),
    ]
    return pl.pallas_call(
        functools.partial(chunk_kernel, chunk, sources, begin is not None, final),
        grid_spec=pltpu.PrefetchScalarGridSpec(
            num_scalar_prefetch=2,
            grid=(1,),
            in_specs=[anywhere] * len(operands),
            out_specs=[anywhere] * len(outs),
            scratch_shapes=scratch,
        ),
        out_shape=outs,
        compiler_params=pltpu.CompilerParams(vmem_limit_bytes=VMEM_LIMIT),
        cost_estimate=pl.CostEstimate(
            flops=12 * count * sources * dim * width * 2,
            bytes_accessed=16 * 2**20,
            transcendentals=0,
        ),
        name="chunk",
    )(*place_at, *operands)


def back_kernel(index, table, own0_ref, oth0_ref, d1_ref, w_ref, oth_ref, own_ref):
    tab = row_of(index, table)
    count = own_ref.shape[0]
    w = w_ref[...].reshape(2 * w_ref.shape[1], w_ref.shape[2])
    straight = tab[CHUNK] == 0
    for d0_ref, out, at in ((oth0_ref, oth_ref, 0), (own0_ref, own_ref, count)):
        d0, d1 = d0_ref[...], d1_ref[at : at + count]
        low = jnp.where(straight, d0, d1)
        high = jnp.where(straight, d1, d0)
        part = jnp.dot(jnp.concatenate([low, high], axis=1), w, preferred_element_type=F32)

        @pl.when(pl.program_id(0) == 0)
        def _():
            out[...] = part

        @pl.when(pl.program_id(0) == 1)
        def _():
            out[...] += part


def back(place_at, own0, oth0, d1, win):
    _, count, width = own0.shape
    dim = win.shape[4]
    whole = pl.BlockSpec((count, dim), lambda k, i, t: (0, 0))
    d_spec = pl.BlockSpec((None, count, width), lambda k, i, t: (k, 0, 0))
    return pl.pallas_call(
        back_kernel,
        grid_spec=pltpu.PrefetchScalarGridSpec(
            num_scalar_prefetch=2,
            grid=(2,),
            in_specs=[
                d_spec,
                d_spec,
                pl.BlockSpec((None, 2 * count, width), lambda k, i, t: (k, 0, 0)),
                pl.BlockSpec(
                    (None, 2, None, width, dim),
                    lambda k, i, t: (k, 0, t[i[0] * WIDTH + CORE], 0, 0),
                ),
            ],
            out_specs=[whole, whole],
        ),
        out_shape=[jax.ShapeDtypeStruct((count, dim), F32)] * 2,
        compiler_params=pltpu.CompilerParams(vmem_limit_bytes=VMEM_LIMIT),
        cost_estimate=pl.CostEstimate(
            flops=16 * count * dim * width, bytes_accessed=16 * 2**20, transcendentals=0
        ),
        name="back",
    )(*place_at, own0, oth0, d1, win)


def small_call(kernel, out_shape, name, place_at, *operands):
    return pl.pallas_call(
        kernel,
        grid_spec=pltpu.PrefetchScalarGridSpec(
            num_scalar_prefetch=2,
            grid=(1,),
            in_specs=[
                pl.BlockSpec(o.shape, functools.partial(lambda n, *_: (0,) * n, o.ndim))
                for o in operands
            ],
            out_specs=[
                pl.BlockSpec(o.shape, functools.partial(lambda n, *_: (0,) * n, len(o.shape)))
                for o in out_shape
            ],
        ),
        out_shape=out_shape,
        cost_estimate=pl.CostEstimate(flops=2**20, bytes_accessed=2**20, transcendentals=0),
        name=name,
    )(*place_at, *operands)


def sums_kernel(sizes, *refs):
    out = refs[-1]
    at = 0
    for i, size in enumerate(sizes):
        out[i, 0] = functools.reduce(lambda p, q: p + q, [r[0] for r in refs[at : at + size]])
        at += size


def sums(groups, rows, count, stride=1):
    lanes = groups[0][0][0].shape[-1]
    tile = min(rows, 160)
    operands, specs = [], []
    for group in groups:
        for array, first in group:
            operands.append(array.reshape(-1, rows, lanes))
            specs.append(
                pl.BlockSpec((1, tile, lanes), functools.partial(lambda f, i, j: (f + i * stride, j, 0), first))
            )
    return pl.pallas_call(
        functools.partial(sums_kernel, [len(group) for group in groups]),
        grid=(count, rows // tile),
        in_specs=specs,
        out_specs=pl.BlockSpec((len(groups), 1, tile, lanes), lambda i, j: (0, i, j, 0)),
        out_shape=jax.ShapeDtypeStruct((len(groups), count, rows, lanes), F32),
        cost_estimate=pl.CostEstimate(
            flops=2**20, bytes_accessed=4 * 2**20, transcendentals=0
        ),
        name="sums",
    )(*operands)


def pieces_kernel(factor, counts, index, table, *refs):
    refs, (all_ref, in_ref) = refs[:-2], refs[-2:]
    at = 0
    for i, picks in enumerate(counts):
        terms = []
        for pick in picks:
            terms.append(refs[at][pick])
            at += 1
        whole = functools.reduce(lambda p, q: p + q, terms) * factor
        all_ref[i] = whole
        if i < 2:
            in_ref[i] = whole


def gather_kernel(index, table, all_ref, next_ref, far_ref, last_ref, out):
    tab = row_of(index, table)
    rows, half = all_ref.shape[1:]
    for i, ref in enumerate((all_ref, next_ref, far_ref, last_ref)):
        place_at = lax.rem(tab[X] + i, 4) * rows
        here = pl.ds(pl.multiple_of(place_at, 8), rows)
        out[here, :half] = ref[0]
        out[here, half:] = ref[1]
    low = tab[OWN_HALF] == 0
    out[4 * rows :, :half] = jnp.where(low, all_ref[2], far_ref[2])
    out[4 * rows :, half:] = jnp.where(low, far_ref[2], all_ref[2])


def last_kernel(index, table, own_ref, oth_ref, in_ref, out_ref):
    tab = row_of(index, table)
    count, half = in_ref.shape[0], in_ref.shape[1] // 2
    owner, zero = tab[IS_OWNER] == 1, tab[CORE] == 0
    in_ref[...] = jnp.where(owner, own_ref[:count], oth_ref[:count])
    own, oth = own_ref[count:], oth_ref[count:]
    for i in range(2):
        cut = slice(i * half, (i + 1) * half)
        out_ref[:, 2 * i * half : (2 * i + 1) * half] = jnp.where(zero, own[:, cut], oth[:, cut])
        out_ref[:, (2 * i + 1) * half : (2 * i + 2) * half] = jnp.where(
            zero, oth[:, cut], own[:, cut]
        )


def move(array, pairs):
    return lax.ppermute(array, AXES, pairs)


def total(terms):
    return functools.reduce(lambda p, q: p + q, terms)


def settle(array):
    return lax.optimization_barrier(array)


def local(normed, w_in, w_out, cotangent):
    dim = normed.shape[1]
    width = w_out.shape[1] // 4
    factor = (normed.shape[0] * lax.axis_size("dp") * lax.axis_size("grp")) ** (-0.5)
    index = lax.axis_index(AXES).reshape(1)
    place_at = index, jnp.asarray(TABLE.reshape(-1))
    win = w_in.reshape(2, 2, 2, width, dim)

    wide = lax.optimization_barrier((normed.astype(F32), cotangent.astype(F32)))
    own = normed, cotangent
    other = move(wide[0], CORE_PAIRS), move(wide[1], CORE_PAIRS)
    gin, gout, own0 = chunk_call(place_at, win, w_out, [own], 0, final=False)
    *first, oth0 = chunk_call(place_at, win, w_out, [other], 0, begin=(gin, gout))
    got_a0, got_b0, got_c0 = move(first[0], Z0), move(first[2], Y0), move(first[4], X0)
    index, _ = lax.optimization_barrier((index, first[0]))
    place_at = index, place_at[1]
    *second, d1 = chunk_call(place_at, win, w_out, [other, own], 1)
    got_a1, got_b1, got_c1 = move(second[0], Z0), move(second[2], Y0), move(second[4], X0)

    oth0, index, got_a0, got_b0, got_c0 = lax.optimization_barrier(
        (oth0, index, got_a0, got_b0, got_c0)
    )
    back_oth, back_own = back(place_at, own0, oth0, d1, win)
    got_a1, got_b1, got_c1, back_own = lax.optimization_barrier(
        (got_a1, got_b1, got_c1, back_own)
    )
    grad_normed = (back_own + move(back_oth, CORE_PAIRS)).astype(BF)

    number = lax.dynamic_index_in_dim(jnp.asarray(TABLE[:, OWN_X]), index[0], 0, keepdims=False)
    own_first = number == 0

    a = [second[1], got_a0]
    b = [[first[3], got_b0], [second[3], got_b1]]
    c = [first[5], got_c0], [second[5], got_c1]
    a += [move(total([first[1], got_a1]), Z1)]
    rows = width // 2
    got = move(sums([[(t, 0) for t in chunk] for chunk in b], rows, 1), Y1)
    b = [[(t, 4) for t in chunk] + [(got, 4 * k)] for k, chunk in enumerate(b)]
    got = move(jnp.where(own_first, total(c[1]), total(c[0])), X1)
    c = [settle(jnp.where(own_first, total(c[0]), total(c[1]))), got]

    def step(terms, pairs, cut_send, cut_keep, keep_whole=False):
        got = move(total([t[cut_send] for t in terms]), pairs)
        kept = [t[cut_keep] for t in terms]
        if keep_whole:
            kept = [settle(total(kept))]
        return kept + [got]

    front, back_half = slice(None, 2), slice(2, None)
    a = step(a, Y0, front, back_half, True)
    rows = width // 8
    kept = [[(t, at + 2) for t, at in chunk] for chunk in b]
    b = [sums(kept, rows, 2), move(sums(b, rows, 2), X0)]
    c = step(c, Z0, front, back_half, True)

    a = step(a, Y1, 0, 1)
    got = move(sums([[(t, 0) for t in b]], rows, 2, 2), X1)
    b = [sums([[(t, 1) for t in b]], rows, 2, 2), got]
    c = step(c, Z1, 0, 1)

    a = step(a, X0, front, back_half)
    rows = width // 16
    got = move(sums([[(t, 2) for t in b]], rows, 2, -2), Z0)
    b = [sums([[(t, 1) for t in b]], rows, 2, 2), got]
    b = [t[0] for t in b]
    c = step(c, Y0, front, back_half)

    a = step(a, X1, 0, 1)
    b = step(b, Z1, 0, 1)
    c = step(c, Y1, 0, 1)

    half = dim // 2
    piece = jax.ShapeDtypeStruct((3, dim // 32, half), F32)
    piece_in = jax.ShapeDtypeStruct((2, dim // 32, half), F32)
    a, b, c = total(a), total(b), total(c)
    mine, mine_in = small_call(
        functools.partial(pieces_kernel, factor, [[Ellipsis]] * 3),
        [piece, piece_in],
        "pieces",
        place_at,
        a,
        b,
        c,
    )
    after = move(mine_in, owner_pairs(1))
    before = move(mine_in, owner_pairs(3))
    far = move(mine, FAR_PAIRS)
    (rows,) = small_call(
        gather_kernel,
        [jax.ShapeDtypeStruct((5 * (dim // 32), dim), F32)],
        "gather",
        place_at,
        mine,
        after,
        far,
        before,
    )
    grad_in, grad_out = small_call(
        last_kernel,
        [
            jax.ShapeDtypeStruct((width // 4, dim), F32),
            jax.ShapeDtypeStruct((dim // 32, 4 * width), F32),
        ],
        "last",
        place_at,
        rows,
        move(rows, CORE_PAIRS),
    )
    return (grad_in, grad_out, grad_normed)


def solution(mesh):
    placed = (P(AXES, None), P(), P(), P(AXES, None))
    return jax.shard_map(
        local,
        mesh=mesh,
        in_specs=placed,
        out_specs=(P("dp", None), P("dp", None), P(AXES, None)),
        check_vma=False,
    )
```

```python
import functools

import jax
import jax.numpy as jnp
import numpy as np
from jax import lax
from jax.experimental import pallas as pl
from jax.experimental.pallas import tpu as pltpu
from jax.sharding import PartitionSpec as P

AXES = ("grp", "dp")
BF = jnp.bfloat16
F32 = jnp.float32
VMEM_LIMIT = 56 * 1024 * 1024
SMALL_LIMIT = 8 * 1024 * 1024


def place(x, y, z, c):
    return ((x // 2) * 2 + c) * 32 + z * 8 + (x % 2) * 4 + y


EVERY = [(x, y, z, c) for x in range(4) for y in range(4) for z in range(4) for c in range(2)]


def partner(i, core, step):
    return (i + (1 if i % 2 == (core + step) % 2 else -1)) % 4


def halving_pairs(axis, step):
    pairs = []
    for x, y, z, c in EVERY:
        at = [x, y, z]
        at[axis] = partner(at[axis], c, step)
        pairs.append((place(x, y, z, c), place(*at, c)))
    return pairs


X0, X1 = halving_pairs(0, 0), halving_pairs(0, 1)
Y0, Y1 = halving_pairs(1, 0), halving_pairs(1, 1)
Z0, Z1 = halving_pairs(2, 0), halving_pairs(2, 1)
CORE_PAIRS = [(place(x, y, z, c), place(x, y, z, 1 - c)) for x, y, z, c in EVERY]
FAR_PAIRS = [(place(x, y, z, c), place((x + 2) % 4, y, z, c)) for x, y, z, c in EVERY]


def owner_pairs(shift):
    return [
        (place((x + shift) % 4, y, z, c), place(x, y, z, c))
        for x, y, z, c in EVERY
        if x % 2 == c
    ]


def ring_order(i, core):
    first, second = partner(i, core, 0), partner(i, core, 1)
    return [partner(first, core, 1), first, second, i]


CORE, CHUNK, KIND, HALF, XAT, YAT, ZAT = 0, 1, 3, 7, 9, 13, 17
OWN_X, OWN_HALF, X, IS_OWNER, WIDTH = 21, 22, 23, 24, 32


def table():
    rows = np.zeros((len(EVERY), WIDTH), np.int32)
    for x, y, z, c in EVERY:
        row = rows[place(x, y, z, c)]
        row[CORE] = c
        xs, ys, zs = ring_order(x, c), ring_order(y, c), ring_order(z, c)
        row[CHUNK], row[CHUNK + 1] = 1 - z % 2, z % 2
        row[KIND : KIND + 4] = [zs[1] // 2, zs[2] // 2, zs[0] // 2, zs[3] // 2]
        labels = {i: (i % 2, i // 2 if c == 0 else (i // 2) ^ (i % 2)) for i in range(4)}
        for k in range(2):
            (row[HALF + k],) = [labels[i][0] for i in xs[2:] if labels[i][1] == row[CHUNK + k]]
        for at, order in ((XAT, xs), (YAT, ys), (ZAT, zs)):
            for rank, i in enumerate(order):
                row[at + rank] = i
        row[OWN_X] = int(row[CHUNK + 1] == labels[x][1])
        row[OWN_HALF] = labels[x][1]
        row[X] = x
        row[IS_OWNER] = int(x % 2 == c)
    return rows


TABLE = table()


NT = (((1,), (1,)), ((), ()))
TN = (((0,), (0,)), ((), ()))


def row_of(index, table):
    class Row:
        def __getitem__(self, at):
            return table[index[0] * WIDTH + at]

    return Row()


def chunk_kernel(chunk, sources, begin, final, index, table, *refs):
    tab = row_of(index, table)
    refs = list(refs)
    take = lambda n: [refs.pop(0) for _ in range(n)]
    win, wout = take(2)
    tokens = [take(2) for _ in range(sources)]
    start = take(2) if begin else None
    outs = take(6 if final else 2)
    (d_out,) = take(1)
    w, wo = take(2)
    raw = [take(2) for _ in range(sources)]
    nb, cb, d, act, gin, gout, sems = take(7)
    width, dim = w.shape[1:]
    half = dim // 2
    count = raw[0][0].shape[0]
    core, block = tab[CORE], tab[CHUNK + chunk]

    loads = []

    def load(source, target):
        copy = pltpu.make_async_copy(source, target, sems.at[len(loads)])
        loads.append(copy)
        copy.start()
        return copy

    column = pl.multiple_of((block * 2 + core) * width, 128)
    load_wo = load(wout.at[:, pl.ds(column, width)], wo)
    load_c = [load(tokens[s][1], raw[s][1]) for s in range(sources)]
    load_w = [load(win.at[kind, block, core], w.at[kind]) for kind in range(2)]
    load_n = [load(tokens[s][0], raw[s][0]) for s in range(sources)]
    load_begin = [load(start[0], gin), load(start[1], gout)] if begin else []

    stores = []

    def store(source, target, sem):
        pltpu.make_async_copy(source, target, sems.at[sem]).start()

    load_wo.wait()
    for s in range(sources):
        here = pl.ds(s * count, count)
        load_c[s].wait()
        cb[here] = raw[s][1][...].astype(BF)
        dact = jnp.dot(cb[here], wo[...], preferred_element_type=F32)
        load_n[s].wait()
        nb[here] = raw[s][0][...].astype(BF)
        if s == 0:
            for copy in load_w:
                copy.wait()
        proj = lax.dot_general(
            nb[here], w[...].reshape(2 * width, dim), NT, preferred_element_type=F32
        )
        value = proj[:, :width]
        gate = proj[:, width:]
        cdf = 0.5 * (1.0 + lax.erf(gate * (2.0 ** -0.5)))
        density = jnp.exp(-0.5 * gate * gate) * ((2.0 * jnp.pi) ** -0.5)
        gated = gate * cdf
        act[here] = (value * gated).astype(BF)
        d[0, here] = (dact * gated).astype(BF)
        d[1, here] = (dact * value * (cdf + gate * density)).astype(BF)
    for kind in range(2):
        store(d.at[kind], d_out.at[kind], 16 + kind)
        stores.append(pltpu.make_async_copy(d.at[kind], d_out.at[kind], sems.at[16 + kind]))

    def total(left, right, place_at):
        whole = lax.dot_general(left, right, TN, preferred_element_type=F32)
        if begin:
            whole = whole + place_at[...]
        place_at[...] = whole

    for copy in load_begin:
        copy.wait()
    small = width // 16
    for slot in range(2):
        kind = tab[KIND + 2 * chunk + slot]
        total(d[kind], nb[...], gin.at[slot])
        if final:
            for y in range(4):
                for x in range(4):
                    at = (tab[YAT + y] * 4 + tab[XAT + x]) * small
                    rows = pl.ds(pl.multiple_of(at, 8), small)
                    store(gin.at[slot, rows, pl.ds(0, half)], outs[slot].at[y, x], 18 + slot)
                    store(
                        gin.at[slot, rows, pl.ds(half, half)],
                        outs[2 + y // 2].at[y % 2, x, slot],
                        20 + y // 2,
                    )
    total(cb[...], act[...], gout)
    if final:
        tiny = dim // 32
        kept = tab[HALF + chunk]
        for slot, x in ((0, 1 - kept), (1, kept)):
            for z in range(4):
                for y in range(4):
                    at = ((tab[ZAT + z] * 2 + x) * 4 + tab[YAT + y]) * tiny
                    rows = pl.ds(pl.multiple_of(at, 8), tiny)
                    store(gout.at[rows], outs[4 + slot].at[z, y], 22 + slot)
    else:
        store(gin, outs[0], 18)
        store(gout, outs[1], 19)
    for copy in stores:
        copy.wait()
    if final:
        for i in range(6):
            pltpu.make_async_copy(outs[i], outs[i], sems.at[18 + i]).wait()
    else:
        pltpu.make_async_copy(gin, outs[0], sems.at[18]).wait()
        pltpu.make_async_copy(gout, outs[1], sems.at[19]).wait()


def chunk_call(place_at, win, wout, tokens, chunk, begin=None, final=True):
    count, dim = tokens[0][0].shape
    width = win.shape[3]
    sources = len(tokens)
    if final:
        a = jax.ShapeDtypeStruct((4, 4, width // 16, dim // 2), F32)
        b = jax.ShapeDtypeStruct((2, 4, 2, width // 16, dim // 2), F32)
        c = jax.ShapeDtypeStruct((4, 4, dim // 32, width), F32)
        outs = [a, a, b, b, c, c]
    else:
        outs = [
            jax.ShapeDtypeStruct((2, width, dim), F32),
            jax.ShapeDtypeStruct((dim, width), F32),
        ]
    outs = outs + [jax.ShapeDtypeStruct((2, sources * count, width), BF)]
    operands = [win, wout] + [t for pair in tokens for t in pair] + list(begin or ())
    anywhere = pl.BlockSpec(memory_space=pl.ANY)
    scratch = [pltpu.VMEM((2, width, dim), BF), pltpu.VMEM((dim, width), BF)]
    scratch += [pltpu.VMEM((count, dim), t.dtype) for pair in tokens for t in pair]
    scratch += [
        pltpu.VMEM((sources * count, dim), BF),
        pltpu.VMEM((sources * count, dim), BF),
        pltpu.VMEM((2, sources * count, width), BF),
        pltpu.VMEM((sources * count, width), BF),
        pltpu.VMEM((2, width, dim), F32),
        pltpu.VMEM((dim, width), F32),
        pltpu.SemaphoreType.DMA((24,)),
    ]
    return pl.pallas_call(
        functools.partial(chunk_kernel, chunk, sources, begin is not None, final),
        grid_spec=pltpu.PrefetchScalarGridSpec(
            num_scalar_prefetch=2,
            grid=(1,),
            in_specs=[anywhere] * len(operands),
            out_specs=[anywhere] * len(outs),
            scratch_shapes=scratch,
        ),
        out_shape=outs,
        compiler_params=pltpu.CompilerParams(vmem_limit_bytes=VMEM_LIMIT),
        cost_estimate=pl.CostEstimate(
            flops=12 * count * sources * dim * width * 2,
            bytes_accessed=16 * 2**20,
            transcendentals=0,
        ),
        name="chunk",
    )(*place_at, *operands)


def back_kernel(index, table, own0_ref, oth0_ref, d1_ref, w_ref, oth_ref, own_ref):
    tab = row_of(index, table)
    count = own_ref.shape[0]
    w = w_ref[...].reshape(2 * w_ref.shape[1], w_ref.shape[2])
    straight = tab[CHUNK] == 0
    for d0_ref, out, at in ((oth0_ref, oth_ref, 0), (own0_ref, own_ref, count)):
        d0, d1 = d0_ref[...], d1_ref[at : at + count]
        low = jnp.where(straight, d0, d1)
        high = jnp.where(straight, d1, d0)
        part = jnp.dot(jnp.concatenate([low, high], axis=1), w, preferred_element_type=F32)

        @pl.when(pl.program_id(0) == 0)
        def _():
            out[...] = part

        @pl.when(pl.program_id(0) == 1)
        def _():
            out[...] += part


def back(place_at, own0, oth0, d1, win):
    _, count, width = own0.shape
    dim = win.shape[4]
    whole = pl.BlockSpec((count, dim), lambda k, i, t: (0, 0))
    d_spec = pl.BlockSpec((None, count, width), lambda k, i, t: (k, 0, 0))
    return pl.pallas_call(
        back_kernel,
        grid_spec=pltpu.PrefetchScalarGridSpec(
            num_scalar_prefetch=2,
            grid=(2,),
            in_specs=[
                d_spec,
                d_spec,
                pl.BlockSpec((None, 2 * count, width), lambda k, i, t: (k, 0, 0)),
                pl.BlockSpec(
                    (None, 2, None, width, dim),
                    lambda k, i, t: (k, 0, t[i[0] * WIDTH + CORE], 0, 0),
                ),
            ],
            out_specs=[whole, whole],
        ),
        out_shape=[jax.ShapeDtypeStruct((count, dim), F32)] * 2,
        compiler_params=pltpu.CompilerParams(vmem_limit_bytes=VMEM_LIMIT),
        cost_estimate=pl.CostEstimate(
            flops=16 * count * dim * width, bytes_accessed=16 * 2**20, transcendentals=0
        ),
        name="back",
    )(*place_at, own0, oth0, d1, win)


def small_call(kernel, out_shape, name, place_at, *operands):
    return pl.pallas_call(
        kernel,
        grid_spec=pltpu.PrefetchScalarGridSpec(
            num_scalar_prefetch=2,
            grid=(1,),
            in_specs=[
                pl.BlockSpec(o.shape, functools.partial(lambda n, *_: (0,) * n, o.ndim))
                for o in operands
            ],
            out_specs=[
                pl.BlockSpec(o.shape, functools.partial(lambda n, *_: (0,) * n, len(o.shape)))
                for o in out_shape
            ],
        ),
        out_shape=out_shape,
        compiler_params=pltpu.CompilerParams(vmem_limit_bytes=SMALL_LIMIT),
        cost_estimate=pl.CostEstimate(flops=2**20, bytes_accessed=2**20, transcendentals=0),
        name=name,
    )(*place_at, *operands)


def sums_kernel(sizes, *refs):
    out = refs[-1]
    at = 0
    for i, size in enumerate(sizes):
        out[i, 0] = functools.reduce(lambda p, q: p + q, [r[0] for r in refs[at : at + size]])
        at += size


def sums(groups, rows, count, stride=1):
    lanes = groups[0][0][0].shape[-1]
    tile = min(rows, 160)
    operands, specs = [], []
    for group in groups:
        for array, first in group:
            operands.append(array.reshape(-1, rows, lanes))
            specs.append(
                pl.BlockSpec((1, tile, lanes), functools.partial(lambda f, i, j: (f + i * stride, j, 0), first))
            )
    return pl.pallas_call(
        functools.partial(sums_kernel, [len(group) for group in groups]),
        grid=(count, rows // tile),
        in_specs=specs,
        out_specs=pl.BlockSpec((len(groups), 1, tile, lanes), lambda i, j: (0, i, j, 0)),
        out_shape=jax.ShapeDtypeStruct((len(groups), count, rows, lanes), F32),
        compiler_params=pltpu.CompilerParams(vmem_limit_bytes=SMALL_LIMIT),
        cost_estimate=pl.CostEstimate(
            flops=2**20, bytes_accessed=4 * 2**20, transcendentals=0
        ),
        name="sums",
    )(*operands)


def pieces_kernel(factor, counts, index, table, *refs):
    refs, (all_ref, in_ref) = refs[:-2], refs[-2:]
    at = 0
    for i, picks in enumerate(counts):
        terms = []
        for pick in picks:
            terms.append(refs[at][pick])
            at += 1
        whole = functools.reduce(lambda p, q: p + q, terms) * factor
        all_ref[i] = whole
        if i < 2:
            in_ref[i] = whole


def gather_kernel(index, table, all_ref, next_ref, far_ref, last_ref, out):
    tab = row_of(index, table)
    rows, half = all_ref.shape[1:]
    for i, ref in enumerate((all_ref, next_ref, far_ref, last_ref)):
        place_at = lax.rem(tab[X] + i, 4) * rows
        here = pl.ds(pl.multiple_of(place_at, 8), rows)
        out[here, :half] = ref[0]
        out[here, half:] = ref[1]
    low = tab[OWN_HALF] == 0
    out[4 * rows :, :half] = jnp.where(low, all_ref[2], far_ref[2])
    out[4 * rows :, half:] = jnp.where(low, far_ref[2], all_ref[2])


def last_kernel(index, table, own_ref, oth_ref, in_ref, out_ref):
    tab = row_of(index, table)
    count, half = in_ref.shape[0], in_ref.shape[1] // 2
    owner, zero = tab[IS_OWNER] == 1, tab[CORE] == 0
    in_ref[...] = jnp.where(owner, own_ref[:count], oth_ref[:count])
    own, oth = own_ref[count:], oth_ref[count:]
    for i in range(2):
        cut = slice(i * half, (i + 1) * half)
        out_ref[:, 2 * i * half : (2 * i + 1) * half] = jnp.where(zero, own[:, cut], oth[:, cut])
        out_ref[:, (2 * i + 1) * half : (2 * i + 2) * half] = jnp.where(
            zero, oth[:, cut], own[:, cut]
        )


def move(array, pairs):
    return lax.ppermute(array, AXES, pairs)


def total(terms):
    return functools.reduce(lambda p, q: p + q, terms)


def settle(array):
    return lax.optimization_barrier(array)


def local(normed, w_in, w_out, cotangent):
    dim = normed.shape[1]
    width = w_out.shape[1] // 4
    factor = (normed.shape[0] * lax.axis_size("dp") * lax.axis_size("grp")) ** (-0.5)
    index = lax.axis_index(AXES).reshape(1)
    place_at = index, jnp.asarray(TABLE.reshape(-1))
    win = w_in.reshape(2, 2, 2, width, dim)

    wide = lax.optimization_barrier((normed.astype(F32), cotangent.astype(F32)))
    own = normed, cotangent
    other = move(wide[0], CORE_PAIRS), move(wide[1], CORE_PAIRS)
    gin, gout, own0 = chunk_call(place_at, win, w_out, [own], 0, final=False)
    *first, oth0 = chunk_call(place_at, win, w_out, [other], 0, begin=(gin, gout))
    got_a0, got_b0, got_c0 = move(first[0], Z0), move(first[2], Y0), move(first[4], X0)
    index, _ = lax.optimization_barrier((index, first[0]))
    place_at = index, place_at[1]
    *second, d1 = chunk_call(place_at, win, w_out, [other, own], 1)
    got_a1, got_b1, got_c1 = move(second[0], Z0), move(second[2], Y0), move(second[4], X0)

    oth0, index, got_a0, got_b0, got_c0 = lax.optimization_barrier(
        (oth0, index, got_a0, got_b0, got_c0)
    )
    back_oth, back_own = back(place_at, own0, oth0, d1, win)
    got_a1, got_b1, got_c1, back_own = lax.optimization_barrier(
        (got_a1, got_b1, got_c1, back_own)
    )
    grad_normed = (back_own + move(back_oth, CORE_PAIRS)).astype(BF)

    number = lax.dynamic_index_in_dim(jnp.asarray(TABLE[:, OWN_X]), index[0], 0, keepdims=False)
    own_first = number == 0

    a = [second[1], got_a0]
    b = [[first[3], got_b0], [second[3], got_b1]]
    c = [first[5], got_c0], [second[5], got_c1]
    a += [move(total([first[1], got_a1]), Z1)]
    rows = width // 2
    got = move(sums([[(t, 0) for t in chunk] for chunk in b], rows, 1), Y1)
    b = [[(t, 4) for t in chunk] + [(got, 4 * k)] for k, chunk in enumerate(b)]
    got = move(jnp.where(own_first, total(c[1]), total(c[0])), X1)
    c = [settle(jnp.where(own_first, total(c[0]), total(c[1]))), got]

    def step(terms, pairs, cut_send, cut_keep, keep_whole=False):
        got = move(total([t[cut_send] for t in terms]), pairs)
        kept = [t[cut_keep] for t in terms]
        if keep_whole:
            kept = [settle(total(kept))]
        return kept + [got]

    front, back_half = slice(None, 2), slice(2, None)
    a = step(a, Y0, front, back_half, True)
    rows = width // 8
    kept = [[(t, at + 2) for t, at in chunk] for chunk in b]
    b = [sums(kept, rows, 2), move(sums(b, rows, 2), X0)]
    c = step(c, Z0, front, back_half, True)

    a = step(a, Y1, 0, 1)
    got = move(sums([[(t, 0) for t in b]], rows, 2, 2), X1)
    b = [sums([[(t, 1) for t in b]], rows, 2, 2), got]
    c = step(c, Z1, 0, 1)

    a = step(a, X0, front, back_half)
    rows = width // 16
    got = move(sums([[(t, 2) for t in b]], rows, 2, -2), Z0)
    b = [sums([[(t, 1) for t in b]], rows, 2, 2), got]
    b = [t[0] for t in b]
    c = step(c, Y0, front, back_half)

    a = step(a, X1, 0, 1)
    b = step(b, Z1, 0, 1)
    c = step(c, Y1, 0, 1)

    half = dim // 2
    piece = jax.ShapeDtypeStruct((3, dim // 32, half), F32)
    piece_in = jax.ShapeDtypeStruct((2, dim // 32, half), F32)
    a, b, c = total(a), total(b), total(c)
    mine, mine_in = small_call(
        functools.partial(pieces_kernel, factor, [[Ellipsis]] * 3),
        [piece, piece_in],
        "pieces",
        place_at,
        a,
        b,
        c,
    )
    after = move(mine_in, owner_pairs(1))
    before = move(mine_in, owner_pairs(3))
    far = move(mine, FAR_PAIRS)
    (rows,) = small_call(
        gather_kernel,
        [jax.ShapeDtypeStruct((5 * (dim // 32), dim), F32)],
        "gather",
        place_at,
        mine,
        after,
        far,
        before,
    )
    grad_in, grad_out = small_call(
        last_kernel,
        [
            jax.ShapeDtypeStruct((width // 4, dim), F32),
            jax.ShapeDtypeStruct((dim // 32, 4 * width), F32),
        ],
        "last",
        place_at,
        rows,
        move(rows, CORE_PAIRS),
    )
    return (grad_in, grad_out, grad_normed)


def solution(mesh):
    placed = (P(AXES, None), P(), P(), P(AXES, None))
    return jax.shard_map(
        local,
        mesh=mesh,
        in_specs=placed,
        out_specs=(P("dp", None), P("dp", None), P(AXES, None)),
        check_vma=False,
    )
```

```python
import functools

import jax
import jax.numpy as jnp
import numpy as np
from jax import lax
from jax.experimental import pallas as pl
from jax.experimental.pallas import tpu as pltpu
from jax.sharding import PartitionSpec as P

AXES = ("grp", "dp")
BF = jnp.bfloat16
F32 = jnp.float32
VMEM_LIMIT = 56 * 1024 * 1024
BACK_LIMIT = 36 * 1024 * 1024
SMALL_LIMIT = 8 * 1024 * 1024


def place(x, y, z, c):
    return ((x // 2) * 2 + c) * 32 + z * 8 + (x % 2) * 4 + y


EVERY = [(x, y, z, c) for x in range(4) for y in range(4) for z in range(4) for c in range(2)]


def partner(i, core, step):
    return (i + (1 if i % 2 == (core + step) % 2 else -1)) % 4


def halving_pairs(axis, step):
    pairs = []
    for x, y, z, c in EVERY:
        at = [x, y, z]
        at[axis] = partner(at[axis], c, step)
        pairs.append((place(x, y, z, c), place(*at, c)))
    return pairs


X0, X1 = halving_pairs(0, 0), halving_pairs(0, 1)
Y0, Y1 = halving_pairs(1, 0), halving_pairs(1, 1)
Z0, Z1 = halving_pairs(2, 0), halving_pairs(2, 1)
CORE_PAIRS = [(place(x, y, z, c), place(x, y, z, 1 - c)) for x, y, z, c in EVERY]
FAR_PAIRS = [(place(x, y, z, c), place((x + 2) % 4, y, z, c)) for x, y, z, c in EVERY]


def owner_pairs(shift):
    return [
        (place((x + shift) % 4, y, z, c), place(x, y, z, c))
        for x, y, z, c in EVERY
        if x % 2 == c
    ]


def ring_order(i, core):
    first, second = partner(i, core, 0), partner(i, core, 1)
    return [partner(first, core, 1), first, second, i]


CORE, CHUNK, KIND, HALF, XAT, YAT, ZAT = 0, 1, 3, 7, 9, 13, 17
OWN_HALF, X, IS_OWNER, WIDTH = 22, 23, 24, 32


def table():
    rows = np.zeros((len(EVERY), WIDTH), np.int32)
    for x, y, z, c in EVERY:
        row = rows[place(x, y, z, c)]
        row[CORE] = c
        xs, ys, zs = ring_order(x, c), ring_order(y, c), ring_order(z, c)
        row[CHUNK], row[CHUNK + 1] = 1 - z % 2, z % 2
        row[KIND : KIND + 4] = [zs[1] // 2, zs[2] // 2, zs[0] // 2, zs[3] // 2]
        labels = {i: (i % 2, i // 2 if c == 0 else (i // 2) ^ (i % 2)) for i in range(4)}
        for k in range(2):
            (row[HALF + k],) = [labels[i][0] for i in xs[2:] if labels[i][1] == row[CHUNK + k]]
        for at, order in ((XAT, xs), (YAT, ys), (ZAT, zs)):
            for rank, i in enumerate(order):
                row[at + rank] = i
        row[OWN_HALF] = labels[x][1]
        row[X] = x
        row[IS_OWNER] = int(x % 2 == c)
    return rows


TABLE = table()


NT = (((1,), (1,)), ((), ()))
TN = (((0,), (0,)), ((), ()))


def row_of(index, table):
    class Row:
        def __getitem__(self, at):
            return table[index[0] * WIDTH + at]

    return Row()


def chunk_kernel(chunk, sources, begin, final, index, table, *refs):
    tab = row_of(index, table)
    refs = list(refs)
    take = lambda n: [refs.pop(0) for _ in range(n)]
    win, wout = take(2)
    tokens = [take(2) for _ in range(sources)]
    start = take(2) if begin else None
    outs = take(6 if final else 2)
    (d_out,) = take(1)
    w, wo = take(2)
    raw = [take(2) for _ in range(sources)]
    nb, cb, d, act, gin, gout, sems = take(7)
    width, dim = w.shape[1:]
    half = dim // 2
    count = raw[0][0].shape[0]
    core, block = tab[CORE], tab[CHUNK + chunk]

    loads = []

    def load(source, target):
        copy = pltpu.make_async_copy(source, target, sems.at[len(loads)])
        loads.append(copy)
        copy.start()
        return copy

    column = pl.multiple_of((block * 2 + core) * width, 128)
    load_wo = load(wout.at[:, pl.ds(column, width)], wo)
    load_c = [load(tokens[s][1], raw[s][1]) for s in range(sources)]
    load_w = [load(win.at[kind, block, core], w.at[kind]) for kind in range(2)]
    load_n = [load(tokens[s][0], raw[s][0]) for s in range(sources)]
    load_begin = [load(start[0], gin), load(start[1], gout)] if begin else []

    stores = []

    def store(source, target, sem):
        pltpu.make_async_copy(source, target, sems.at[sem]).start()

    load_wo.wait()
    for s in range(sources):
        here = pl.ds(s * count, count)
        load_c[s].wait()
        cb[here] = raw[s][1][...].astype(BF)
        dact = jnp.dot(cb[here], wo[...], preferred_element_type=F32)
        load_n[s].wait()
        nb[here] = raw[s][0][...].astype(BF)
        if s == 0:
            for copy in load_w:
                copy.wait()
        proj = lax.dot_general(
            nb[here], w[...].reshape(2 * width, dim), NT, preferred_element_type=F32
        )
        value = proj[:, :width]
        gate = proj[:, width:]
        cdf = 0.5 * (1.0 + lax.erf(gate * (2.0 ** -0.5)))
        density = jnp.exp(-0.5 * gate * gate) * ((2.0 * jnp.pi) ** -0.5)
        gated = gate * cdf
        act[here] = (value * gated).astype(BF)
        d[0, here] = (dact * gated).astype(BF)
        d[1, here] = (dact * value * (cdf + gate * density)).astype(BF)
    for kind in range(2):
        store(d.at[kind], d_out.at[kind], 16 + kind)
        stores.append(pltpu.make_async_copy(d.at[kind], d_out.at[kind], sems.at[16 + kind]))

    def total(left, right, place_at):
        whole = lax.dot_general(left, right, TN, preferred_element_type=F32)
        if begin:
            whole = whole + place_at[...]
        place_at[...] = whole

    for copy in load_begin:
        copy.wait()
    small = width // 16
    for slot in range(2):
        kind = tab[KIND + 2 * chunk + slot]
        total(d[kind], nb[...], gin.at[slot])
        if final:
            for y in range(4):
                for x in range(4):
                    at = (tab[YAT + y] * 4 + tab[XAT + x]) * small
                    rows = pl.ds(pl.multiple_of(at, 8), small)
                    store(gin.at[slot, rows, pl.ds(0, half)], outs[slot].at[y, x], 18 + slot)
                    store(
                        gin.at[slot, rows, pl.ds(half, half)],
                        outs[2 + y // 2].at[y % 2, x, slot],
                        20 + y // 2,
                    )
    total(cb[...], act[...], gout)
    if final:
        tiny = dim // 32
        kept = tab[HALF + chunk]
        for slot, x in ((0, 1 - kept), (1, kept)):
            for z in range(4):
                for y in range(4):
                    at = ((tab[ZAT + z] * 2 + x) * 4 + tab[YAT + y]) * tiny
                    rows = pl.ds(pl.multiple_of(at, 8), tiny)
                    store(gout.at[rows], outs[4 + slot].at[z, y], 22 + slot)
    else:
        store(gin, outs[0], 18)
        store(gout, outs[1], 19)
    for copy in stores:
        copy.wait()
    if final:
        for i in range(6):
            pltpu.make_async_copy(outs[i], outs[i], sems.at[18 + i]).wait()
    else:
        pltpu.make_async_copy(gin, outs[0], sems.at[18]).wait()
        pltpu.make_async_copy(gout, outs[1], sems.at[19]).wait()


def chunk_call(place_at, win, wout, tokens, chunk, begin=None, final=True):
    count, dim = tokens[0][0].shape
    width = win.shape[3]
    sources = len(tokens)
    if final:
        a = jax.ShapeDtypeStruct((4, 4, width // 16, dim // 2), F32)
        b = jax.ShapeDtypeStruct((2, 4, 2, width // 16, dim // 2), F32)
        c = jax.ShapeDtypeStruct((4, 4, dim // 32, width), F32)
        outs = [a, a, b, b, c, c]
    else:
        outs = [
            jax.ShapeDtypeStruct((2, width, dim), F32),
            jax.ShapeDtypeStruct((dim, width), F32),
        ]
    outs = outs + [jax.ShapeDtypeStruct((2, sources * count, width), BF)]
    operands = [win, wout] + [t for pair in tokens for t in pair] + list(begin or ())
    anywhere = pl.BlockSpec(memory_space=pl.ANY)
    scratch = [pltpu.VMEM((2, width, dim), BF), pltpu.VMEM((dim, width), BF)]
    scratch += [pltpu.VMEM((count, dim), t.dtype) for pair in tokens for t in pair]
    scratch += [
        pltpu.VMEM((sources * count, dim), BF),
        pltpu.VMEM((sources * count, dim), BF),
        pltpu.VMEM((2, sources * count, width), BF),
        pltpu.VMEM((sources * count, width), BF),
        pltpu.VMEM((2, width, dim), F32),
        pltpu.VMEM((dim, width), F32),
        pltpu.SemaphoreType.DMA((24,)),
    ]
    return pl.pallas_call(
        functools.partial(chunk_kernel, chunk, sources, begin is not None, final),
        grid_spec=pltpu.PrefetchScalarGridSpec(
            num_scalar_prefetch=2,
            grid=(1,),
            in_specs=[anywhere] * len(operands),
            out_specs=[anywhere] * len(outs),
            scratch_shapes=scratch,
        ),
        out_shape=outs,
        compiler_params=pltpu.CompilerParams(vmem_limit_bytes=VMEM_LIMIT),
        cost_estimate=pl.CostEstimate(
            flops=12 * count * sources * dim * width * 2,
            bytes_accessed=16 * 2**20,
            transcendentals=0,
        ),
        name="chunk",
    )(*place_at, *operands)


def back_kernel(index, table, own0_ref, oth0_ref, d1_ref, w_ref, oth_ref, own_ref):
    tab = row_of(index, table)
    count = own_ref.shape[0]
    w = w_ref[...].reshape(2 * w_ref.shape[1], w_ref.shape[2])
    straight = tab[CHUNK] == 0
    for d0_ref, out, at in ((oth0_ref, oth_ref, 0), (own0_ref, own_ref, count)):
        d0, d1 = d0_ref[...], d1_ref[at : at + count]
        low = jnp.where(straight, d0, d1)
        high = jnp.where(straight, d1, d0)
        part = jnp.dot(jnp.concatenate([low, high], axis=1), w, preferred_element_type=F32)

        @pl.when(pl.program_id(0) == 0)
        def _():
            out[...] = part

        @pl.when(pl.program_id(0) == 1)
        def _():
            out[...] += part


def back(place_at, own0, oth0, d1, win):
    _, count, width = own0.shape
    dim = win.shape[4]
    whole = pl.BlockSpec((count, dim), lambda k, i, t: (0, 0))
    d_spec = pl.BlockSpec((None, count, width), lambda k, i, t: (k, 0, 0))
    return pl.pallas_call(
        back_kernel,
        grid_spec=pltpu.PrefetchScalarGridSpec(
            num_scalar_prefetch=2,
            grid=(2,),
            in_specs=[
                d_spec,
                d_spec,
                pl.BlockSpec((None, 2 * count, width), lambda k, i, t: (k, 0, 0)),
                pl.BlockSpec(
                    (None, 2, None, width, dim),
                    lambda k, i, t: (k, 0, t[i[0] * WIDTH + CORE], 0, 0),
                ),
            ],
            out_specs=[whole, whole],
        ),
        out_shape=[jax.ShapeDtypeStruct((count, dim), F32)] * 2,
        compiler_params=pltpu.CompilerParams(vmem_limit_bytes=BACK_LIMIT),
        cost_estimate=pl.CostEstimate(
            flops=16 * count * dim * width, bytes_accessed=16 * 2**20, transcendentals=0
        ),
        name="back",
    )(*place_at, own0, oth0, d1, win)


def small_call(kernel, out_shape, name, place_at, *operands):
    return pl.pallas_call(
        kernel,
        grid_spec=pltpu.PrefetchScalarGridSpec(
            num_scalar_prefetch=2,
            grid=(1,),
            in_specs=[
                pl.BlockSpec(o.shape, functools.partial(lambda n, *_: (0,) * n, o.ndim))
                for o in operands
            ],
            out_specs=[
                pl.BlockSpec(o.shape, functools.partial(lambda n, *_: (0,) * n, len(o.shape)))
                for o in out_shape
            ],
        ),
        out_shape=out_shape,
        compiler_params=pltpu.CompilerParams(vmem_limit_bytes=SMALL_LIMIT),
        cost_estimate=pl.CostEstimate(flops=2**20, bytes_accessed=2**20, transcendentals=0),
        name=name,
    )(*place_at, *operands)


def sums_kernel(sizes, *refs):
    out = refs[-1]
    at = 0
    for i, size in enumerate(sizes):
        out[i, 0] = functools.reduce(lambda p, q: p + q, [r[0] for r in refs[at : at + size]])
        at += size


def sums(groups, rows, count, stride=1):
    lanes = groups[0][0][0].shape[-1]
    tile = min(rows, 160)
    operands, specs = [], []
    for group in groups:
        for array, first in group:
            operands.append(array.reshape(-1, rows, lanes))
            specs.append(
                pl.BlockSpec((1, tile, lanes), functools.partial(lambda f, i, j: (f + i * stride, j, 0), first))
            )
    return pl.pallas_call(
        functools.partial(sums_kernel, [len(group) for group in groups]),
        grid=(count, rows // tile),
        in_specs=specs,
        out_specs=pl.BlockSpec((len(groups), 1, tile, lanes), lambda i, j: (0, i, j, 0)),
        out_shape=jax.ShapeDtypeStruct((len(groups), count, rows, lanes), F32),
        compiler_params=pltpu.CompilerParams(vmem_limit_bytes=SMALL_LIMIT),
        cost_estimate=pl.CostEstimate(
            flops=2**20, bytes_accessed=4 * 2**20, transcendentals=0
        ),
        name="sums",
    )(*operands)


def pieces_kernel(factor, counts, index, table, *refs):
    refs, (all_ref, in_ref) = refs[:-2], refs[-2:]
    at = 0
    for i, picks in enumerate(counts):
        terms = []
        for pick in picks:
            terms.append(refs[at][pick])
            at += 1
        whole = functools.reduce(lambda p, q: p + q, terms) * factor
        all_ref[i] = whole
        if i < 2:
            in_ref[i] = whole


def gather_kernel(index, table, all_ref, next_ref, far_ref, last_ref, out):
    tab = row_of(index, table)
    rows, half = all_ref.shape[1:]
    for i, ref in enumerate((all_ref, next_ref, far_ref, last_ref)):
        place_at = lax.rem(tab[X] + i, 4) * rows
        here = pl.ds(pl.multiple_of(place_at, 8), rows)
        out[here, :half] = ref[0]
        out[here, half:] = ref[1]
    low = tab[OWN_HALF] == 0
    out[4 * rows :, :half] = jnp.where(low, all_ref[2], far_ref[2])
    out[4 * rows :, half:] = jnp.where(low, far_ref[2], all_ref[2])


def last_kernel(index, table, own_ref, oth_ref, in_ref, out_ref):
    tab = row_of(index, table)
    count, half = in_ref.shape[0], in_ref.shape[1] // 2
    owner, zero = tab[IS_OWNER] == 1, tab[CORE] == 0
    in_ref[...] = jnp.where(owner, own_ref[:count], oth_ref[:count])
    own, oth = own_ref[count:], oth_ref[count:]
    for i in range(2):
        cut = slice(i * half, (i + 1) * half)
        out_ref[:, 2 * i * half : (2 * i + 1) * half] = jnp.where(zero, own[:, cut], oth[:, cut])
        out_ref[:, (2 * i + 1) * half : (2 * i + 2) * half] = jnp.where(
            zero, oth[:, cut], own[:, cut]
        )


def move(array, pairs):
    return lax.ppermute(array, AXES, pairs)


def total(terms):
    return functools.reduce(lambda p, q: p + q, terms)


def settle(array):
    return lax.optimization_barrier(array)


def send_all(*pairs):
    sent = [array for array, _ in pairs]
    got = [move(array, way) for array, way in pairs]
    return [lax.optimization_barrier((g, *sent))[0] for g in got]


def local(normed, w_in, w_out, cotangent):
    dim = normed.shape[1]
    width = w_out.shape[1] // 4
    factor = (normed.shape[0] * lax.axis_size("dp") * lax.axis_size("grp")) ** (-0.5)
    index = lax.axis_index(AXES).reshape(1)
    place_at = index, jnp.asarray(TABLE.reshape(-1))
    win = w_in.reshape(2, 2, 2, width, dim)

    wide = lax.optimization_barrier((normed.astype(F32), cotangent.astype(F32)))
    own = normed, cotangent
    other = move(wide[0], CORE_PAIRS), move(wide[1], CORE_PAIRS)
    gin, gout, own0 = chunk_call(place_at, win, w_out, [own], 0, final=False)
    *first, oth0 = chunk_call(place_at, win, w_out, [other], 0, begin=(gin, gout))
    got_a0, got_b0, got_c0 = move(first[0], Z0), move(first[2], Y0), move(first[4], X0)
    index, _ = lax.optimization_barrier((index, first[0]))
    place_at = index, place_at[1]
    *second, d1 = chunk_call(place_at, win, w_out, [other, own], 1)
    got_a1, got_b1, got_c1 = move(second[0], Z0), move(second[2], Y0), move(second[4], X0)

    oth0, index, got_a0, got_b0, early_c = lax.optimization_barrier(
        (oth0, index, got_a0, got_b0, first[5] + got_c0)
    )
    back_oth, back_own = back(place_at, own0, oth0, d1, win)
    got_a1, got_b1, got_c1, back_own = lax.optimization_barrier(
        (got_a1, got_b1, got_c1, back_own)
    )
    grad_normed = (back_own + move(back_oth, CORE_PAIRS)).astype(BF)

    grp, dp = lax.axis_index("grp"), lax.axis_index("dp")
    own_first = ((dp >> 3) & 1) != ((grp >> 1) ^ (grp & (dp >> 2) & 1))

    rows = width // 2
    a = [second[1], got_a0]
    b = [first[3], got_b0], [second[3], got_b1]
    c = [early_c], [second[5], got_c1]
    to_b = sums([[(t, 0) for t in chunk] for chunk in b], rows, 1)
    to_a = total([first[1], got_a1])
    to_c = jnp.where(own_first, total(c[1]), total(c[0]))
    got_b, got_a, got_c = send_all((to_b, Y1), (to_a, Z1), (to_c, X1))
    rows = width // 8
    a = [settle(total(a)), got_a]
    b = [[(t, 4) for t in chunk] + [(got_b, 4 * k)] for k, chunk in enumerate(b)]
    kept, grad_normed = settle((jnp.where(own_first, total(c[0]), total(c[1])), grad_normed))
    c = [kept, got_c]

    to_b = sums(b, rows, 2)
    to_a, to_c = total([t[:2] for t in a]), total([t[:2] for t in c])
    got_b, got_a, got_c = send_all((to_b, X0), (to_a, Y0), (to_c, Z0))
    a = [settle(total([t[2:] for t in a])), got_a]
    b = [sums([[(t, at + 2) for t, at in chunk] for chunk in b], rows, 2), got_b]
    c = [settle(total([t[2:] for t in c])), got_c]

    to_b = sums([[(t, 0) for t in b]], rows, 2, 2)
    to_a, to_c = total([t[0] for t in a]), total([t[0] for t in c])
    got_b, got_a, got_c = send_all((to_b, X1), (to_a, Y1), (to_c, Z1))
    a = [t[1] for t in a] + [got_a]
    b = [sums([[(t, 1) for t in b]], rows, 2, 2), got_b]
    c = [t[1] for t in c] + [got_c]

    rows = width // 16
    to_b = sums([[(t, 2) for t in b]], rows, 2, -2)
    to_a, to_c = total([t[:2] for t in a]), total([t[:2] for t in c])
    got_b, got_a, got_c = send_all((to_b, Z0), (to_a, X0), (to_c, Y0))
    a = [t[2:] for t in a] + [got_a]
    b = [sums([[(t, 1) for t in b]], rows, 2, 2)[0], got_b[0]]
    c = [t[2:] for t in c] + [got_c]

    to_a, to_b, to_c = (total([t[0] for t in terms]) for terms in (a, b, c))
    got_b, got_a, got_c = send_all((to_b, Z1), (to_a, X1), (to_c, Y1))
    a, b, c = (
        total([t[1] for t in terms] + [got])
        for terms, got in ((a, got_a), (b, got_b), (c, got_c))
    )

    half = dim // 2
    piece = jax.ShapeDtypeStruct((3, dim // 32, half), F32)
    piece_in = jax.ShapeDtypeStruct((2, dim // 32, half), F32)
    mine, mine_in = small_call(
        functools.partial(pieces_kernel, factor, [[Ellipsis]] * 3),
        [piece, piece_in],
        "pieces",
        place_at,
        a,
        b,
        c,
    )
    after = move(mine_in, owner_pairs(1))
    before = move(mine_in, owner_pairs(3))
    far = move(mine, FAR_PAIRS)
    (rows,) = small_call(
        gather_kernel,
        [jax.ShapeDtypeStruct((5 * (dim // 32), dim), F32)],
        "gather",
        place_at,
        mine,
        after,
        far,
        before,
    )
    grad_in, grad_out = small_call(
        last_kernel,
        [
            jax.ShapeDtypeStruct((width // 4, dim), F32),
            jax.ShapeDtypeStruct((dim // 32, 4 * width), F32),
        ],
        "last",
        place_at,
        rows,
        move(rows, CORE_PAIRS),
    )
    return (grad_in, grad_out, grad_normed)


def solution(mesh):
    placed = (P(AXES, None), P(), P(), P(AXES, None))
    return jax.shard_map(
        local,
        mesh=mesh,
        in_specs=placed,
        out_specs=(P("dp", None), P("dp", None), P(AXES, None)),
        check_vma=False,
    )
```

```python
import functools

import jax
import jax.numpy as jnp
import numpy as np
from jax import lax
from jax.experimental import pallas as pl
from jax.experimental.pallas import tpu as pltpu
from jax.sharding import PartitionSpec as P

AXES = ("grp", "dp")
BF = jnp.bfloat16
F32 = jnp.float32
OWN_LIMIT = 24 * 2**20
CHUNK_LIMIT = 32 * 2**20
BACK_LIMIT = 22 * 2**20
SMALL_LIMIT = 8 * 2**20


def place(x, y, z, c):
    return ((x // 2) * 2 + c) * 32 + z * 8 + (x % 2) * 4 + y


EVERY = [(x, y, z, c) for x in range(4) for y in range(4) for z in range(4) for c in range(2)]


def partner(i, core, step):
    return (i + (1 if i % 2 == (core + step) % 2 else -1)) % 4


def halving_pairs(axis, step):
    pairs = []
    for x, y, z, c in EVERY:
        at = [x, y, z]
        at[axis] = partner(at[axis], c, step)
        pairs.append((place(x, y, z, c), place(*at, c)))
    return pairs


X0, X1 = halving_pairs(0, 0), halving_pairs(0, 1)
Y0, Y1 = halving_pairs(1, 0), halving_pairs(1, 1)
Z0, Z1 = halving_pairs(2, 0), halving_pairs(2, 1)
CORE_PAIRS = [(place(x, y, z, c), place(x, y, z, 1 - c)) for x, y, z, c in EVERY]
FAR_PAIRS = [(place(x, y, z, c), place((x + 2) % 4, y, z, c)) for x, y, z, c in EVERY]


def owner_pairs(shift):
    return [
        (place((x + shift) % 4, y, z, c), place(x, y, z, c))
        for x, y, z, c in EVERY
        if x % 2 == c
    ]


def ring_order(i, core):
    first, second = partner(i, core, 0), partner(i, core, 1)
    return [partner(first, core, 1), first, second, i]


CORE, CHUNK, KIND, HALF, XAT, YAT, ZAT = 0, 1, 3, 7, 9, 13, 17
OWN_HALF, X, IS_OWNER, WIDTH = 22, 23, 24, 32


def table():
    rows = np.zeros((len(EVERY), WIDTH), np.int32)
    for x, y, z, c in EVERY:
        row = rows[place(x, y, z, c)]
        row[CORE] = c
        xs, ys, zs = ring_order(x, c), ring_order(y, c), ring_order(z, c)
        row[CHUNK], row[CHUNK + 1] = 1 - z % 2, z % 2
        row[KIND : KIND + 4] = [zs[1] // 2, zs[2] // 2, zs[0] // 2, zs[3] // 2]
        labels = {i: (i % 2, i // 2 if c == 0 else (i // 2) ^ (i % 2)) for i in range(4)}
        for k in range(2):
            (row[HALF + k],) = [labels[i][0] for i in xs[2:] if labels[i][1] == row[CHUNK + k]]
        for at, order in ((XAT, xs), (YAT, ys), (ZAT, zs)):
            for rank, i in enumerate(order):
                row[at + rank] = i
        row[OWN_HALF] = labels[x][1]
        row[X] = x
        row[IS_OWNER] = int(x % 2 == c)
    return rows


TWO_BITS = [*range(XAT, ZAT + 4), X]
FIELDS = {at: (0, 2 * i, 3) for i, at in enumerate(TWO_BITS)}
ONE_BIT = [CORE, CHUNK, CHUNK + 1, *range(KIND, KIND + 4), HALF, HALF + 1, OWN_HALF, IS_OWNER]
FIELDS.update({at: (1, i, 1) for i, at in enumerate(ONE_BIT)})


def packed():
    rows = table()
    words = np.zeros((len(EVERY), 2), np.int32)
    for at, (word, shift, _) in FIELDS.items():
        words[:, word] |= rows[:, at] << shift
    return words


TABLE = packed()


def field(index, table, at):
    word, shift, mask = FIELDS[at]
    return (table[index[0] * 2 + word] >> shift) & mask


NT = (((1,), (1,)), ((), ()))
TN = (((0,), (0,)), ((), ()))


def row_of(index, table):
    class Row:
        def __getitem__(self, at):
            return field(index, table, at)

    return Row()


def gated(value, gate, dact):
    cdf = 0.5 * (1.0 + lax.erf(gate * (2.0 ** -0.5)))
    density = jnp.exp(-0.5 * gate * gate) * ((2.0 * jnp.pi) ** -0.5)
    share = gate * cdf
    return (
        (value * share).astype(BF),
        (dact * share).astype(BF),
        (dact * value * (cdf + gate * density)).astype(BF),
    )


class Copies:
    def __init__(self, sems):
        self.sems, self.used = sems, 0

    def start(self, source, target):
        copy = pltpu.make_async_copy(source, target, self.sems.at[self.used])
        self.used += 1
        copy.start()
        return copy


def own_kernel(index, table, win, wout, n_in, c_in, d_out, act_out, w, wo, n, c, d, act, sems):
    tab = row_of(index, table)
    width = w.shape[2]
    copies = Copies(sems)
    load_w, load_wo = [], []
    for k in range(2):
        block, core = tab[CHUNK + k], tab[CORE]
        column = pl.multiple_of((block * 2 + core) * width, 128)
        load_wo.append(copies.start(wout.at[:, pl.ds(column, width)], wo.at[k]))
        if k == 0:
            load_c = copies.start(c_in, c)
        load_w.append([copies.start(win.at[i, block, core], w.at[k, i]) for i in range(2)])
        if k == 0:
            load_n = copies.start(n_in, n)
    stores = []
    for k in range(2):
        load_wo[k].wait()
        if k == 0:
            load_c.wait()
        dact = jnp.dot(c[...], wo[k], preferred_element_type=F32)
        for copy in load_w[k]:
            copy.wait()
        if k == 0:
            load_n.wait()
        proj = lax.dot_general(
            n[...], w[k].reshape(2 * width, w.shape[3]), NT, preferred_element_type=F32
        )
        act[k], d[k, 0], d[k, 1] = gated(proj[:, :width], proj[:, width:], dact)
        stores.append(copies.start(act.at[k], act_out.at[k]))
        stores.append(copies.start(d.at[k], d_out.at[k]))
    for copy in stores:
        copy.wait()


def own_call(place_at, win, wout, normed, cot):
    count, dim = normed.shape
    width = win.shape[3]
    anywhere = pl.BlockSpec(memory_space=pl.ANY)
    return pl.pallas_call(
        own_kernel,
        grid_spec=pltpu.PrefetchScalarGridSpec(
            num_scalar_prefetch=2,
            grid=(1,),
            in_specs=[anywhere] * 4,
            out_specs=[anywhere] * 2,
            scratch_shapes=[
                pltpu.VMEM((2, 2, width, dim), BF),
                pltpu.VMEM((2, dim, width), BF),
                pltpu.VMEM((count, dim), BF),
                pltpu.VMEM((count, dim), BF),
                pltpu.VMEM((2, 2, count, width), BF),
                pltpu.VMEM((2, count, width), BF),
                pltpu.SemaphoreType.DMA((12,)),
            ],
        ),
        out_shape=[
            jax.ShapeDtypeStruct((2, 2, count, width), BF),
            jax.ShapeDtypeStruct((2, count, width), BF),
        ],
        compiler_params=pltpu.CompilerParams(vmem_limit_bytes=OWN_LIMIT),
        cost_estimate=pl.CostEstimate(
            flops=12 * count * dim * width, bytes_accessed=16 * 2**20, transcendentals=0
        ),
        name="own_terms",
    )(*place_at, win, wout, normed, cot)


def chunk_kernel(
    chunk, index, table, win, wout, n_in, c_in, n_own, c_own, d_own, act_own,
    a_send, a_keep, b_send, b_keep, c_send, c_keep, d_out,
    w, wo, nb, cb, d, act, gin, gout, load_sems, sems,
):
    tab = row_of(index, table)
    width, dim = w.shape[1:]
    count = n_in.shape[0]
    half = dim // 2
    core, block = tab[CORE], tab[CHUNK + chunk]
    own, oth = pl.ds(count, count), pl.ds(0, count)
    loads = Copies(load_sems)
    column = pl.multiple_of((block * 2 + core) * width, 128)
    load_wo = loads.start(wout.at[:, pl.ds(column, width)], wo)
    lanes = [pl.ds(part * half, half) for part in range(2)]
    raw = gin.at[:, :, oth]
    load_c = [loads.start(c_in.at[:, lanes[i]], raw.at[0, i]) for i in range(2)]
    load_w = [loads.start(win.at[i, block, core], w.at[i]) for i in range(2)]
    load_n = [loads.start(n_in.at[:, lanes[i]], raw.at[1, i]) for i in range(2)]
    load_own = [loads.start(c_own, cb.at[own]), loads.start(act_own.at[chunk], act.at[own])]
    load_own += [loads.start(d_own.at[chunk, i], d.at[i, own]) for i in range(2)]
    load_own += [loads.start(n_own, nb.at[own])]

    def store(source, target, sem):
        pltpu.make_async_copy(source, target, sems.at[sem]).start()

    load_wo.wait()
    for i in range(2):
        load_c[i].wait()
        cb[oth, i * half : (i + 1) * half] = raw[0, i].astype(BF)
    dact = jnp.dot(cb[oth], wo[...], preferred_element_type=F32)
    for i in range(2):
        load_n[i].wait()
        nb[oth, i * half : (i + 1) * half] = raw[1, i].astype(BF)
    for copy in load_w:
        copy.wait()
    proj = lax.dot_general(
        nb[oth], w[...].reshape(2 * width, dim), NT, preferred_element_type=F32
    )
    act[oth], d[0, oth], d[1, oth] = gated(proj[:, :width], proj[:, width:], dact)
    for i in range(2):
        store(d.at[i, oth], d_out.at[i], 0)
    for copy in load_own:
        copy.wait()

    gout[...] = lax.dot_general(cb[...], act[...], TN, preferred_element_type=F32)
    tiny = dim // 32
    kept = tab[HALF + chunk]
    for out, x, sem in ((c_send, 1 - kept, 1), (c_keep, kept, 2)):
        for z in range(4):
            for y in range(4):
                at = ((tab[ZAT + z] * 2 + x) * 4 + tab[YAT + y]) * tiny
                store(gout.at[pl.ds(pl.multiple_of(at, 8), tiny)], out.at[z, y], sem)
    small = width // 16
    for slot, out in enumerate((a_send, a_keep)):
        kind = tab[KIND + 2 * chunk + slot]
        for part in range(2):
            cut = slice(part * half, (part + 1) * half)
            gin[slot, part] = lax.dot_general(
                d[kind], nb[:, cut], TN, preferred_element_type=F32
            )
            for y in range(4):
                for x in range(4):
                    at = (tab[YAT + y] * 4 + tab[XAT + x]) * small
                    rows = gin.at[slot, part, pl.ds(pl.multiple_of(at, 8), small)]
                    if part == 0:
                        store(rows, out.at[y, x], 3 + slot)
                    else:
                        store(rows, (b_send, b_keep)[y // 2].at[y % 2, x, slot], 5 + y // 2)
    outs = (d_out, c_send, c_keep, a_send, a_keep, b_send, b_keep)
    for i, out in enumerate(outs):
        pltpu.make_async_copy(out, out, sems.at[i]).wait()


def chunk_call(place_at, win, wout, other, own, terms, chunk):
    count, dim = own[0].shape
    width = win.shape[3]
    a = jax.ShapeDtypeStruct((4, 4, width // 16, dim // 2), F32)
    b = jax.ShapeDtypeStruct((2, 4, 2, width // 16, dim // 2), F32)
    c = jax.ShapeDtypeStruct((4, 4, dim // 32, width), F32)
    outs = [a, a, b, b, c, c, jax.ShapeDtypeStruct((2, count, width), BF)]
    operands = [win, wout, *other, *own, *terms]
    anywhere = pl.BlockSpec(memory_space=pl.ANY)
    return pl.pallas_call(
        functools.partial(chunk_kernel, chunk),
        grid_spec=pltpu.PrefetchScalarGridSpec(
            num_scalar_prefetch=2,
            grid=(1,),
            in_specs=[anywhere] * len(operands),
            out_specs=[anywhere] * len(outs),
            scratch_shapes=[
                pltpu.VMEM((2, width, dim), BF),
                pltpu.VMEM((dim, width), BF),
                pltpu.VMEM((2 * count, dim), BF),
                pltpu.VMEM((2 * count, dim), BF),
                pltpu.VMEM((2, 2 * count, width), BF),
                pltpu.VMEM((2 * count, width), BF),
                pltpu.VMEM((2, 2, width, dim // 2), F32),
                pltpu.VMEM((dim, width), F32),
                pltpu.SemaphoreType.DMA((12,)),
                pltpu.SemaphoreType.DMA((7,)),
            ],
        ),
        out_shape=outs,
        compiler_params=pltpu.CompilerParams(vmem_limit_bytes=CHUNK_LIMIT),
        cost_estimate=pl.CostEstimate(
            flops=16 * count * dim * width, bytes_accessed=16 * 2**20, transcendentals=0
        ),
        name="chunk",
    )(*place_at, *operands)


def back_kernel(index, table, own_ref, oth0_ref, oth1_ref, w_ref, oth_out, own_out):
    tab = row_of(index, table)
    w = w_ref[...].reshape(2 * w_ref.shape[1], w_ref.shape[2])
    straight = tab[CHUNK] == 0
    for d0, d1, out in (
        (oth0_ref[...], oth1_ref[...], oth_out),
        (own_ref[0], own_ref[1], own_out),
    ):
        low = jnp.where(straight, d0, d1)
        high = jnp.where(straight, d1, d0)
        part = jnp.dot(jnp.concatenate([low, high], axis=1), w, preferred_element_type=F32)

        @pl.when(pl.program_id(0) == 0)
        def _():
            out[...] = part

        @pl.when(pl.program_id(0) == 1)
        def _():
            out[...] += part


def back(place_at, own, oth0, oth1, win):
    _, count, width = oth0.shape
    dim = win.shape[4]
    whole = pl.BlockSpec((count, dim), lambda k, i, t: (0, 0))
    d_spec = pl.BlockSpec((None, count, width), lambda k, i, t: (k, 0, 0))
    return pl.pallas_call(
        back_kernel,
        grid_spec=pltpu.PrefetchScalarGridSpec(
            num_scalar_prefetch=2,
            grid=(2,),
            in_specs=[
                pl.BlockSpec((2, None, count, width), lambda k, i, t: (0, k, 0, 0)),
                d_spec,
                d_spec,
                pl.BlockSpec(
                    (None, 2, None, width, dim),
                    lambda k, i, t: (k, 0, field(i, t, CORE), 0, 0),
                ),
            ],
            out_specs=[whole, whole],
        ),
        out_shape=[jax.ShapeDtypeStruct((count, dim), F32)] * 2,
        compiler_params=pltpu.CompilerParams(vmem_limit_bytes=BACK_LIMIT),
        cost_estimate=pl.CostEstimate(
            flops=16 * count * dim * width, bytes_accessed=16 * 2**20, transcendentals=0
        ),
        name="back",
    )(*place_at, own, oth0, oth1, win)


def small_call(kernel, out_shape, name, place_at, *operands):
    return pl.pallas_call(
        kernel,
        grid_spec=pltpu.PrefetchScalarGridSpec(
            num_scalar_prefetch=2,
            grid=(1,),
            in_specs=[
                pl.BlockSpec(o.shape, functools.partial(lambda n, *_: (0,) * n, o.ndim))
                for o in operands
            ],
            out_specs=[
                pl.BlockSpec(o.shape, functools.partial(lambda n, *_: (0,) * n, len(o.shape)))
                for o in out_shape
            ],
        ),
        out_shape=out_shape,
        compiler_params=pltpu.CompilerParams(vmem_limit_bytes=SMALL_LIMIT),
        cost_estimate=pl.CostEstimate(flops=2**20, bytes_accessed=2**20, transcendentals=0),
        name=name,
    )(*place_at, *operands)


def sums_kernel(sizes, *refs):
    out = refs[-1]
    at = 0
    for i, size in enumerate(sizes):
        out[i, 0] = functools.reduce(lambda p, q: p + q, [r[0] for r in refs[at : at + size]])
        at += size


def sums(groups, rows, count, stride=1):
    lanes = groups[0][0][0].shape[-1]
    tile = min(rows, 160)
    operands, specs = [], []
    for group in groups:
        for array, first in group:
            operands.append(array.reshape(-1, rows, lanes))
            specs.append(
                pl.BlockSpec((1, tile, lanes), functools.partial(lambda f, i, j: (f + i * stride, j, 0), first))
            )
    return pl.pallas_call(
        functools.partial(sums_kernel, [len(group) for group in groups]),
        grid=(count, rows // tile),
        in_specs=specs,
        out_specs=pl.BlockSpec((len(groups), 1, tile, lanes), lambda i, j: (0, i, j, 0)),
        out_shape=jax.ShapeDtypeStruct((len(groups), count, rows, lanes), F32),
        compiler_params=pltpu.CompilerParams(vmem_limit_bytes=SMALL_LIMIT),
        cost_estimate=pl.CostEstimate(
            flops=2**20, bytes_accessed=4 * 2**20, transcendentals=0
        ),
        name="sums",
    )(*operands)


def pieces_kernel(factor, counts, index, table, *refs):
    refs, (all_ref, in_ref) = refs[:-2], refs[-2:]
    at = 0
    for i, picks in enumerate(counts):
        terms = []
        for pick in picks:
            terms.append(refs[at][pick])
            at += 1
        whole = functools.reduce(lambda p, q: p + q, terms) * factor
        all_ref[i] = whole
        if i < 2:
            in_ref[i] = whole


def gather_kernel(index, table, all_ref, next_ref, far_ref, last_ref, out):
    tab = row_of(index, table)
    rows, half = all_ref.shape[1:]
    for i, ref in enumerate((all_ref, next_ref, far_ref, last_ref)):
        place_at = lax.rem(tab[X] + i, 4) * rows
        here = pl.ds(pl.multiple_of(place_at, 8), rows)
        out[here, :half] = ref[0]
        out[here, half:] = ref[1]
    low = tab[OWN_HALF] == 0
    out[4 * rows :, :half] = jnp.where(low, all_ref[2], far_ref[2])
    out[4 * rows :, half:] = jnp.where(low, far_ref[2], all_ref[2])


def last_kernel(index, table, own_ref, oth_ref, in_ref, out_ref):
    tab = row_of(index, table)
    count, half = in_ref.shape[0], in_ref.shape[1] // 2
    owner, zero = tab[IS_OWNER] == 1, tab[CORE] == 0
    in_ref[...] = jnp.where(owner, own_ref[:count], oth_ref[:count])
    own, oth = own_ref[count:], oth_ref[count:]
    for i in range(2):
        cut = slice(i * half, (i + 1) * half)
        out_ref[:, 2 * i * half : (2 * i + 1) * half] = jnp.where(zero, own[:, cut], oth[:, cut])
        out_ref[:, (2 * i + 1) * half : (2 * i + 2) * half] = jnp.where(
            zero, oth[:, cut], own[:, cut]
        )


def move(array, pairs):
    return lax.ppermute(array, AXES, pairs)


def total(terms):
    return functools.reduce(lambda p, q: p + q, terms)


def settle(array):
    return lax.optimization_barrier(array)


def send_all(*pairs):
    sent = [array for array, _ in pairs]
    got = [move(array, way) for array, way in pairs]
    return [lax.optimization_barrier((g, *sent))[0] for g in got]


def local(normed, w_in, w_out, cotangent):
    dim = normed.shape[1]
    width = w_out.shape[1] // 4
    factor = (normed.shape[0] * lax.axis_size("dp") * lax.axis_size("grp")) ** (-0.5)
    index = lax.axis_index(AXES).reshape(1)
    place_at = index, jnp.asarray(TABLE.reshape(-1))
    win = w_in.reshape(2, 2, 2, width, dim)

    wide = lax.optimization_barrier((normed.astype(F32), cotangent.astype(F32)))
    own = normed, cotangent
    other = move(wide[0], CORE_PAIRS), move(wide[1], CORE_PAIRS)
    terms = own_call(place_at, win, w_out, normed, cotangent)
    *first, oth0 = chunk_call(place_at, win, w_out, other, own, terms, 0)
    got_a0, got_b0, got_c0 = move(first[0], Z0), move(first[2], Y0), move(first[4], X0)
    index, _ = lax.optimization_barrier((index, first[0]))
    place_at = index, place_at[1]
    *second, oth1 = chunk_call(place_at, win, w_out, other, own, terms, 1)
    got_a1, got_b1, got_c1 = move(second[0], Z0), move(second[2], Y0), move(second[4], X0)

    oth0, index, got_a0, got_b0, early_c = lax.optimization_barrier(
        (oth0, index, got_a0, got_b0, first[5] + got_c0)
    )
    back_oth, back_own = back(place_at, terms[0], oth0, oth1, win)
    got_a1, got_b1, got_c1, back_own = lax.optimization_barrier(
        (got_a1, got_b1, got_c1, back_own)
    )
    grad_normed = (back_own + move(back_oth, CORE_PAIRS)).astype(BF)

    grp, dp = lax.axis_index("grp"), lax.axis_index("dp")
    own_first = ((dp >> 3) & 1) != ((grp >> 1) ^ (grp & (dp >> 2) & 1))

    rows = width // 2
    a = [second[1], got_a0]
    b = [first[3], got_b0], [second[3], got_b1]
    c = [early_c], [second[5], got_c1]
    to_b = sums([[(t, 0) for t in chunk] for chunk in b], rows, 1)
    to_a = total([first[1], got_a1])
    to_c = jnp.where(own_first, total(c[1]), total(c[0]))
    got_b, got_a, got_c = send_all((to_b, Y1), (to_a, Z1), (to_c, X1))
    rows = width // 8
    a = [settle(total(a)), got_a]
    b = [[(t, 4) for t in chunk] + [(got_b, 4 * k)] for k, chunk in enumerate(b)]
    kept, grad_normed = settle((jnp.where(own_first, total(c[0]), total(c[1])), grad_normed))
    c = [kept, got_c]

    to_b = sums(b, rows, 2)
    to_a, to_c = total([t[:2] for t in a]), total([t[:2] for t in c])
    got_b, got_a, got_c = send_all((to_b, X0), (to_a, Y0), (to_c, Z0))
    a = [settle(total([t[2:] for t in a])), got_a]
    b = [sums([[(t, at + 2) for t, at in chunk] for chunk in b], rows, 2), got_b]
    c = [settle(total([t[2:] for t in c])), got_c]

    to_b = sums([[(t, 0) for t in b]], rows, 2, 2)
    to_a, to_c = total([t[0] for t in a]), total([t[0] for t in c])
    got_b, got_a, got_c = send_all((to_b, X1), (to_a, Y1), (to_c, Z1))
    a = [t[1] for t in a] + [got_a]
    b = [sums([[(t, 1) for t in b]], rows, 2, 2), got_b]
    c = [t[1] for t in c] + [got_c]

    rows = width // 16
    to_b = sums([[(t, 2) for t in b]], rows, 2, -2)
    to_a, to_c = total([t[:2] for t in a]), total([t[:2] for t in c])
    got_b, got_a, got_c = send_all((to_b, Z0), (to_a, X0), (to_c, Y0))
    a = [t[2:] for t in a] + [got_a]
    b = [sums([[(t, 1) for t in b]], rows, 2, 2)[0], got_b[0]]
    c = [t[2:] for t in c] + [got_c]

    to_a, to_b, to_c = (total([t[0] for t in terms]) for terms in (a, b, c))
    got_b, got_a, got_c = send_all((to_b, Z1), (to_a, X1), (to_c, Y1))
    a, b, c = (
        total([t[1] for t in terms] + [got])
        for terms, got in ((a, got_a), (b, got_b), (c, got_c))
    )

    half = dim // 2
    piece = jax.ShapeDtypeStruct((3, dim // 32, half), F32)
    piece_in = jax.ShapeDtypeStruct((2, dim // 32, half), F32)
    mine, mine_in = small_call(
        functools.partial(pieces_kernel, factor, [[Ellipsis]] * 3),
        [piece, piece_in],
        "pieces",
        place_at,
        a,
        b,
        c,
    )
    after = move(mine_in, owner_pairs(1))
    before = move(mine_in, owner_pairs(3))
    far = move(mine, FAR_PAIRS)
    (rows,) = small_call(
        gather_kernel,
        [jax.ShapeDtypeStruct((5 * (dim // 32), dim), F32)],
        "gather",
        place_at,
        mine,
        after,
        far,
        before,
    )
    grad_in, grad_out = small_call(
        last_kernel,
        [
            jax.ShapeDtypeStruct((width // 4, dim), F32),
            jax.ShapeDtypeStruct((dim // 32, 4 * width), F32),
        ],
        "last",
        place_at,
        rows,
        move(rows, CORE_PAIRS),
    )
    return (grad_in, grad_out, grad_normed)


def solution(mesh):
    placed = (P(AXES, None), P(), P(), P(AXES, None))
    return jax.shard_map(
        local,
        mesh=mesh,
        in_specs=placed,
        out_specs=(P("dp", None), P("dp", None), P(AXES, None)),
        check_vma=False,
    )
```

```python
import functools

import jax
import jax.numpy as jnp
import numpy as np
from jax import lax
from jax.experimental import pallas as pl
from jax.experimental.pallas import tpu as pltpu
from jax.sharding import PartitionSpec as P

AXES = ("grp", "dp")
BF = jnp.bfloat16
F32 = jnp.float32
OWN_LIMIT = 56 * 2**20
CHUNK_LIMIT = 56 * 2**20
BACK_LIMIT = 22 * 2**20
SMALL_LIMIT = 8 * 2**20


def place(x, y, z, c):
    return ((x // 2) * 2 + c) * 32 + z * 8 + (x % 2) * 4 + y


EVERY = [(x, y, z, c) for x in range(4) for y in range(4) for z in range(4) for c in range(2)]


def partner(i, core, step):
    return (i + (1 if i % 2 == (core + step) % 2 else -1)) % 4


def halving_pairs(axis, step):
    pairs = []
    for x, y, z, c in EVERY:
        at = [x, y, z]
        at[axis] = partner(at[axis], c, step)
        pairs.append((place(x, y, z, c), place(*at, c)))
    return pairs


X0, X1 = halving_pairs(0, 0), halving_pairs(0, 1)
Y0, Y1 = halving_pairs(1, 0), halving_pairs(1, 1)
Z0, Z1 = halving_pairs(2, 0), halving_pairs(2, 1)
CORE_PAIRS = [(place(x, y, z, c), place(x, y, z, 1 - c)) for x, y, z, c in EVERY]
FAR_PAIRS = [(place(x, y, z, c), place((x + 2) % 4, y, z, c)) for x, y, z, c in EVERY]


def owner_pairs(shift):
    return [
        (place((x + shift) % 4, y, z, c), place(x, y, z, c))
        for x, y, z, c in EVERY
        if x % 2 == c
    ]


def ring_order(i, core):
    first, second = partner(i, core, 0), partner(i, core, 1)
    return [partner(first, core, 1), first, second, i]


CORE, CHUNK, KIND, HALF, XAT, YAT, ZAT = 0, 1, 3, 7, 9, 13, 17
OWN_HALF, X, IS_OWNER, WIDTH = 22, 23, 24, 32


def table():
    rows = np.zeros((len(EVERY), WIDTH), np.int32)
    for x, y, z, c in EVERY:
        row = rows[place(x, y, z, c)]
        row[CORE] = c
        xs, ys, zs = ring_order(x, c), ring_order(y, c), ring_order(z, c)
        row[CHUNK], row[CHUNK + 1] = 1 - z % 2, z % 2
        row[KIND : KIND + 4] = [zs[1] // 2, zs[2] // 2, zs[0] // 2, zs[3] // 2]
        labels = {i: (i % 2, i // 2 if c == 0 else (i // 2) ^ (i % 2)) for i in range(4)}
        for k in range(2):
            (row[HALF + k],) = [labels[i][0] for i in xs[2:] if labels[i][1] == row[CHUNK + k]]
        for at, order in ((XAT, xs), (YAT, ys), (ZAT, zs)):
            for rank, i in enumerate(order):
                row[at + rank] = i
        row[OWN_HALF] = labels[x][1]
        row[X] = x
        row[IS_OWNER] = int(x % 2 == c)
    return rows


TWO_BITS = [*range(XAT, ZAT + 4), X]
FIELDS = {at: (0, 2 * i, 3) for i, at in enumerate(TWO_BITS)}
ONE_BIT = [CORE, CHUNK, CHUNK + 1, *range(KIND, KIND + 4), HALF, HALF + 1, OWN_HALF, IS_OWNER]
FIELDS.update({at: (1, i, 1) for i, at in enumerate(ONE_BIT)})


def packed():
    rows = table()
    words = np.zeros((len(EVERY), 2), np.int32)
    for at, (word, shift, _) in FIELDS.items():
        words[:, word] |= rows[:, at] << shift
    return words


TABLE = packed()


def field(index, table, at):
    word, shift, mask = FIELDS[at]
    return (table[index[0] * 2 + word] >> shift) & mask


NT = (((1,), (1,)), ((), ()))
TN = (((0,), (0,)), ((), ()))


def row_of(index, table):
    class Row:
        def __getitem__(self, at):
            return field(index, table, at)

    return Row()


def gated(value, gate, dact):
    cdf = 0.5 * (1.0 + lax.erf(gate * (2.0 ** -0.5)))
    density = jnp.exp(-0.5 * gate * gate) * ((2.0 * jnp.pi) ** -0.5)
    share = gate * cdf
    return (
        (value * share).astype(BF),
        (dact * share).astype(BF),
        (dact * value * (cdf + gate * density)).astype(BF),
    )


class Copies:
    def __init__(self, sems):
        self.sems, self.used = sems, 0

    def start(self, source, target):
        copy = pltpu.make_async_copy(source, target, self.sems.at[self.used])
        self.used += 1
        copy.start()
        return copy


def own_kernel(index, table, win, wout, n_in, c_in, d_out, act_out, w, wo, n, c, d, act, sems):
    tab = row_of(index, table)
    width = w.shape[2]
    copies = Copies(sems)
    load_w, load_wo = [], []
    for k in range(2):
        block, core = tab[CHUNK + k], tab[CORE]
        column = pl.multiple_of((block * 2 + core) * width, 128)
        load_wo.append(copies.start(wout.at[:, pl.ds(column, width)], wo.at[k]))
        if k == 0:
            load_c = copies.start(c_in, c)
        load_w.append([copies.start(win.at[i, block, core], w.at[k, i]) for i in range(2)])
        if k == 0:
            load_n = copies.start(n_in, n)
    stores = []
    for k in range(2):
        load_wo[k].wait()
        if k == 0:
            load_c.wait()
        dact = jnp.dot(c[...], wo[k], preferred_element_type=F32)
        for copy in load_w[k]:
            copy.wait()
        if k == 0:
            load_n.wait()
        proj = lax.dot_general(
            n[...], w[k].reshape(2 * width, w.shape[3]), NT, preferred_element_type=F32
        )
        act[k], d[k, 0], d[k, 1] = gated(proj[:, :width], proj[:, width:], dact)
        stores.append(copies.start(act.at[k], act_out.at[k]))
        stores.append(copies.start(d.at[k], d_out.at[k]))
    for copy in stores:
        copy.wait()


def own_call(place_at, win, wout, normed, cot):
    count, dim = normed.shape
    width = win.shape[3]
    anywhere = pl.BlockSpec(memory_space=pl.ANY)
    return pl.pallas_call(
        own_kernel,
        grid_spec=pltpu.PrefetchScalarGridSpec(
            num_scalar_prefetch=2,
            grid=(1,),
            in_specs=[anywhere] * 4,
            out_specs=[anywhere] * 2,
            scratch_shapes=[
                pltpu.VMEM((2, 2, width, dim), BF),
                pltpu.VMEM((2, dim, width), BF),
                pltpu.VMEM((count, dim), BF),
                pltpu.VMEM((count, dim), BF),
                pltpu.VMEM((2, 2, count, width), BF),
                pltpu.VMEM((2, count, width), BF),
                pltpu.SemaphoreType.DMA((12,)),
            ],
        ),
        out_shape=[
            jax.ShapeDtypeStruct((2, 2, count, width), BF),
            jax.ShapeDtypeStruct((2, count, width), BF),
        ],
        compiler_params=pltpu.CompilerParams(vmem_limit_bytes=OWN_LIMIT),
        cost_estimate=pl.CostEstimate(
            flops=12 * count * dim * width, bytes_accessed=16 * 2**20, transcendentals=0
        ),
        name="own_terms",
    )(*place_at, win, wout, normed, cot)


def chunk_kernel(
    chunk, index, table, win, wout, n_in, c_in, n_own, c_own, d_own, act_own,
    a_send, a_keep, b_send, b_keep, c_send, c_keep, d_out,
    w, wo, nb, cb, d, act, gin, gout, load_sems, sems,
):
    tab = row_of(index, table)
    width, dim = w.shape[1:]
    count = n_in.shape[0]
    half = dim // 2
    core, block = tab[CORE], tab[CHUNK + chunk]
    own, oth = pl.ds(count, count), pl.ds(0, count)
    loads = Copies(load_sems)
    column = pl.multiple_of((block * 2 + core) * width, 128)
    load_wo = loads.start(wout.at[:, pl.ds(column, width)], wo)
    lanes = [pl.ds(part * half, half) for part in range(2)]
    raw = gin.at[:, :, oth]
    load_c = [loads.start(c_in.at[:, lanes[i]], raw.at[0, i]) for i in range(2)]
    load_w = [loads.start(win.at[i, block, core], w.at[i]) for i in range(2)]
    load_n = [loads.start(n_in.at[:, lanes[i]], raw.at[1, i]) for i in range(2)]
    load_own = [loads.start(c_own, cb.at[own]), loads.start(act_own.at[chunk], act.at[own])]
    load_own += [loads.start(d_own.at[chunk, i], d.at[i, own]) for i in range(2)]
    load_own += [loads.start(n_own, nb.at[own])]

    def store(source, target, sem):
        pltpu.make_async_copy(source, target, sems.at[sem]).start()

    load_wo.wait()
    for i in range(2):
        load_c[i].wait()
        cb[oth, i * half : (i + 1) * half] = raw[0, i].astype(BF)
    dact = jnp.dot(cb[oth], wo[...], preferred_element_type=F32)
    for i in range(2):
        load_n[i].wait()
        nb[oth, i * half : (i + 1) * half] = raw[1, i].astype(BF)
    for copy in load_w:
        copy.wait()
    proj = lax.dot_general(
        nb[oth], w[...].reshape(2 * width, dim), NT, preferred_element_type=F32
    )
    act[oth], d[0, oth], d[1, oth] = gated(proj[:, :width], proj[:, width:], dact)
    for i in range(2):
        store(d.at[i, oth], d_out.at[i], 0)
    for copy in load_own:
        copy.wait()

    gout[...] = lax.dot_general(cb[...], act[...], TN, preferred_element_type=F32)
    tiny = dim // 32
    kept = tab[HALF + chunk]
    for out, x, sem in ((c_send, 1 - kept, 1), (c_keep, kept, 2)):
        for z in range(4):
            for y in range(4):
                at = ((tab[ZAT + z] * 2 + x) * 4 + tab[YAT + y]) * tiny
                store(gout.at[pl.ds(pl.multiple_of(at, 8), tiny)], out.at[z, y], sem)
    small = width // 16
    for slot, out in enumerate((a_send, a_keep)):
        kind = tab[KIND + 2 * chunk + slot]
        for part in range(2):
            cut = slice(part * half, (part + 1) * half)
            gin[slot, part] = lax.dot_general(
                d[kind], nb[:, cut], TN, preferred_element_type=F32
            )
            for y in range(4):
                for x in range(4):
                    at = (tab[YAT + y] * 4 + tab[XAT + x]) * small
                    rows = gin.at[slot, part, pl.ds(pl.multiple_of(at, 8), small)]
                    if part == 0:
                        store(rows, out.at[y, x], 3 + slot)
                    else:
                        store(rows, (b_send, b_keep)[y // 2].at[y % 2, x, slot], 5 + y // 2)
    outs = (d_out, c_send, c_keep, a_send, a_keep, b_send, b_keep)
    for i, out in enumerate(outs):
        pltpu.make_async_copy(out, out, sems.at[i]).wait()


def chunk_call(place_at, win, wout, other, own, terms, chunk):
    count, dim = own[0].shape
    width = win.shape[3]
    a = jax.ShapeDtypeStruct((4, 4, width // 16, dim // 2), F32)
    b = jax.ShapeDtypeStruct((2, 4, 2, width // 16, dim // 2), F32)
    c = jax.ShapeDtypeStruct((4, 4, dim // 32, width), F32)
    outs = [a, a, b, b, c, c, jax.ShapeDtypeStruct((2, count, width), BF)]
    operands = [win, wout, *other, *own, *terms]
    anywhere = pl.BlockSpec(memory_space=pl.ANY)
    return pl.pallas_call(
        functools.partial(chunk_kernel, chunk),
        grid_spec=pltpu.PrefetchScalarGridSpec(
            num_scalar_prefetch=2,
            grid=(1,),
            in_specs=[anywhere] * len(operands),
            out_specs=[anywhere] * len(outs),
            scratch_shapes=[
                pltpu.VMEM((2, width, dim), BF),
                pltpu.VMEM((dim, width), BF),
                pltpu.VMEM((2 * count, dim), BF),
                pltpu.VMEM((2 * count, dim), BF),
                pltpu.VMEM((2, 2 * count, width), BF),
                pltpu.VMEM((2 * count, width), BF),
                pltpu.VMEM((2, 2, width, dim // 2), F32),
                pltpu.VMEM((dim, width), F32),
                pltpu.SemaphoreType.DMA((12,)),
                pltpu.SemaphoreType.DMA((7,)),
            ],
        ),
        out_shape=outs,
        compiler_params=pltpu.CompilerParams(vmem_limit_bytes=CHUNK_LIMIT),
        cost_estimate=pl.CostEstimate(
            flops=16 * count * dim * width, bytes_accessed=16 * 2**20, transcendentals=0
        ),
        name="chunk",
    )(*place_at, *operands)


def back_kernel(index, table, own_ref, oth0_ref, oth1_ref, w_ref, oth_out, own_out):
    tab = row_of(index, table)
    w = w_ref[...].reshape(2 * w_ref.shape[1], w_ref.shape[2])
    straight = tab[CHUNK] == 0
    for d0, d1, out in (
        (oth0_ref[...], oth1_ref[...], oth_out),
        (own_ref[0], own_ref[1], own_out),
    ):
        low = jnp.where(straight, d0, d1)
        high = jnp.where(straight, d1, d0)
        part = jnp.dot(jnp.concatenate([low, high], axis=1), w, preferred_element_type=F32)

        @pl.when(pl.program_id(0) == 0)
        def _():
            out[...] = part

        @pl.when(pl.program_id(0) == 1)
        def _():
            out[...] += part


def back(place_at, own, oth0, oth1, win):
    _, count, width = oth0.shape
    dim = win.shape[4]
    whole = pl.BlockSpec((count, dim), lambda k, i, t: (0, 0))
    d_spec = pl.BlockSpec((None, count, width), lambda k, i, t: (k, 0, 0))
    return pl.pallas_call(
        back_kernel,
        grid_spec=pltpu.PrefetchScalarGridSpec(
            num_scalar_prefetch=2,
            grid=(2,),
            in_specs=[
                pl.BlockSpec((2, None, count, width), lambda k, i, t: (0, k, 0, 0)),
                d_spec,
                d_spec,
                pl.BlockSpec(
                    (None, 2, None, width, dim),
                    lambda k, i, t: (k, 0, field(i, t, CORE), 0, 0),
                ),
            ],
            out_specs=[whole, whole],
        ),
        out_shape=[jax.ShapeDtypeStruct((count, dim), F32)] * 2,
        compiler_params=pltpu.CompilerParams(vmem_limit_bytes=BACK_LIMIT),
        cost_estimate=pl.CostEstimate(
            flops=16 * count * dim * width, bytes_accessed=16 * 2**20, transcendentals=0
        ),
        name="back",
    )(*place_at, own, oth0, oth1, win)


def small_call(kernel, out_shape, name, place_at, *operands):
    return pl.pallas_call(
        kernel,
        grid_spec=pltpu.PrefetchScalarGridSpec(
            num_scalar_prefetch=2,
            grid=(1,),
            in_specs=[
                pl.BlockSpec(o.shape, functools.partial(lambda n, *_: (0,) * n, o.ndim))
                for o in operands
            ],
            out_specs=[
                pl.BlockSpec(o.shape, functools.partial(lambda n, *_: (0,) * n, len(o.shape)))
                for o in out_shape
            ],
        ),
        out_shape=out_shape,
        compiler_params=pltpu.CompilerParams(vmem_limit_bytes=SMALL_LIMIT),
        cost_estimate=pl.CostEstimate(flops=2**20, bytes_accessed=2**20, transcendentals=0),
        name=name,
    )(*place_at, *operands)


def sums_kernel(sizes, *refs):
    out = refs[-1]
    at = 0
    for i, size in enumerate(sizes):
        out[i, 0] = functools.reduce(lambda p, q: p + q, [r[0] for r in refs[at : at + size]])
        at += size


def sums(groups, rows, count, stride=1):
    lanes = groups[0][0][0].shape[-1]
    tile = min(rows, 160)
    operands, specs = [], []
    for group in groups:
        for array, first in group:
            operands.append(array.reshape(-1, rows, lanes))
            specs.append(
                pl.BlockSpec((1, tile, lanes), functools.partial(lambda f, i, j: (f + i * stride, j, 0), first))
            )
    return pl.pallas_call(
        functools.partial(sums_kernel, [len(group) for group in groups]),
        grid=(count, rows // tile),
        in_specs=specs,
        out_specs=pl.BlockSpec((len(groups), 1, tile, lanes), lambda i, j: (0, i, j, 0)),
        out_shape=jax.ShapeDtypeStruct((len(groups), count, rows, lanes), F32),
        compiler_params=pltpu.CompilerParams(vmem_limit_bytes=SMALL_LIMIT),
        cost_estimate=pl.CostEstimate(
            flops=2**20, bytes_accessed=4 * 2**20, transcendentals=0
        ),
        name="sums",
    )(*operands)


def pieces_kernel(factor, counts, index, table, *refs):
    refs, (all_ref, in_ref) = refs[:-2], refs[-2:]
    at = 0
    for i, picks in enumerate(counts):
        terms = []
        for pick in picks:
            terms.append(refs[at][pick])
            at += 1
        whole = functools.reduce(lambda p, q: p + q, terms) * factor
        all_ref[i] = whole
        if i < 2:
            in_ref[i] = whole


def gather_kernel(index, table, all_ref, next_ref, far_ref, last_ref, out):
    tab = row_of(index, table)
    rows, half = all_ref.shape[1:]
    for i, ref in enumerate((all_ref, next_ref, far_ref, last_ref)):
        place_at = lax.rem(tab[X] + i, 4) * rows
        here = pl.ds(pl.multiple_of(place_at, 8), rows)
        out[here, :half] = ref[0]
        out[here, half:] = ref[1]
    low = tab[OWN_HALF] == 0
    out[4 * rows :, :half] = jnp.where(low, all_ref[2], far_ref[2])
    out[4 * rows :, half:] = jnp.where(low, far_ref[2], all_ref[2])


def last_kernel(index, table, own_ref, oth_ref, in_ref, out_ref):
    tab = row_of(index, table)
    count, half = in_ref.shape[0], in_ref.shape[1] // 2
    owner, zero = tab[IS_OWNER] == 1, tab[CORE] == 0
    in_ref[...] = jnp.where(owner, own_ref[:count], oth_ref[:count])
    own, oth = own_ref[count:], oth_ref[count:]
    for i in range(2):
        cut = slice(i * half, (i + 1) * half)
        out_ref[:, 2 * i * half : (2 * i + 1) * half] = jnp.where(zero, own[:, cut], oth[:, cut])
        out_ref[:, (2 * i + 1) * half : (2 * i + 2) * half] = jnp.where(
            zero, oth[:, cut], own[:, cut]
        )


def move(array, pairs):
    return lax.ppermute(array, AXES, pairs)


def total(terms):
    return functools.reduce(lambda p, q: p + q, terms)


def settle(array):
    return lax.optimization_barrier(array)


def send_all(*pairs):
    sent = [array for array, _ in pairs]
    got = [move(array, way) for array, way in pairs]
    return [lax.optimization_barrier((g, *sent))[0] for g in got]


def local(normed, w_in, w_out, cotangent):
    dim = normed.shape[1]
    width = w_out.shape[1] // 4
    factor = (normed.shape[0] * lax.axis_size("dp") * lax.axis_size("grp")) ** (-0.5)
    index = lax.axis_index(AXES).reshape(1)
    place_at = index, jnp.asarray(TABLE.reshape(-1))
    win = w_in.reshape(2, 2, 2, width, dim)

    wide = lax.optimization_barrier((normed.astype(F32), cotangent.astype(F32)))
    own = normed, cotangent
    other = move(wide[0], CORE_PAIRS), move(wide[1], CORE_PAIRS)
    terms = own_call(place_at, win, w_out, normed, cotangent)
    *first, oth0 = chunk_call(place_at, win, w_out, other, own, terms, 0)
    got_a0, got_b0, got_c0 = move(first[0], Z0), move(first[2], Y0), move(first[4], X0)
    index, _ = lax.optimization_barrier((index, first[0]))
    place_at = index, place_at[1]
    *second, oth1 = chunk_call(place_at, win, w_out, other, own, terms, 1)
    got_a1, got_b1, got_c1 = move(second[0], Z0), move(second[2], Y0), move(second[4], X0)

    oth0, index, got_a0, got_b0, early_c = lax.optimization_barrier(
        (oth0, index, got_a0, got_b0, first[5] + got_c0)
    )
    back_oth, back_own = back(place_at, terms[0], oth0, oth1, win)
    got_a1, got_b1, got_c1, back_own = lax.optimization_barrier(
        (got_a1, got_b1, got_c1, back_own)
    )
    grad_normed = (back_own + move(back_oth, CORE_PAIRS)).astype(BF)

    grp, dp = lax.axis_index("grp"), lax.axis_index("dp")
    own_first = ((dp >> 3) & 1) != ((grp >> 1) ^ (grp & (dp >> 2) & 1))

    rows = width // 2
    a = [second[1], got_a0]
    b = [first[3], got_b0], [second[3], got_b1]
    c = [early_c], [second[5], got_c1]
    to_b = sums([[(t, 0) for t in chunk] for chunk in b], rows, 1)
    to_a = total([first[1], got_a1])
    to_c = jnp.where(own_first, total(c[1]), total(c[0]))
    got_b, got_a, got_c = send_all((to_b, Y1), (to_a, Z1), (to_c, X1))
    rows = width // 8
    a = [settle(total(a)), got_a]
    b = [[(t, 4) for t in chunk] + [(got_b, 4 * k)] for k, chunk in enumerate(b)]
    c = [settle(jnp.where(own_first, total(c[0]), total(c[1]))), got_c]

    to_b = sums(b, rows, 2)
    to_a, to_c = total([t[:2] for t in a]), total([t[:2] for t in c])
    got_b, got_a, got_c = send_all((to_b, X0), (to_a, Y0), (to_c, Z0))
    a = [settle(total([t[2:] for t in a])), got_a]
    b = [sums([[(t, at + 2) for t, at in chunk] for chunk in b], rows, 2), got_b]
    kept, grad_normed = settle((total([t[2:] for t in c]), grad_normed))
    c = [kept, got_c]

    to_b = sums([[(t, 0) for t in b]], rows, 2, 2)
    to_a, to_c = total([t[0] for t in a]), total([t[0] for t in c])
    got_b, got_a, got_c = send_all((to_b, X1), (to_a, Y1), (to_c, Z1))
    a = [t[1] for t in a] + [got_a]
    b = [sums([[(t, 1) for t in b]], rows, 2, 2), got_b]
    c = [t[1] for t in c] + [got_c]

    rows = width // 16
    to_b = sums([[(t, 2) for t in b]], rows, 2, -2)
    to_a, to_c = total([t[:2] for t in a]), total([t[:2] for t in c])
    got_b, got_a, got_c = send_all((to_b, Z0), (to_a, X0), (to_c, Y0))
    a = [t[2:] for t in a] + [got_a]
    b = [sums([[(t, 1) for t in b]], rows, 2, 2)[0], got_b[0]]
    c = [t[2:] for t in c] + [got_c]

    to_a, to_b, to_c = (total([t[0] for t in terms]) for terms in (a, b, c))
    got_b, got_a, got_c = send_all((to_b, Z1), (to_a, X1), (to_c, Y1))
    a, b, c = (
        total([t[1] for t in terms] + [got])
        for terms, got in ((a, got_a), (b, got_b), (c, got_c))
    )

    half = dim // 2
    piece = jax.ShapeDtypeStruct((3, dim // 32, half), F32)
    piece_in = jax.ShapeDtypeStruct((2, dim // 32, half), F32)
    mine, mine_in = small_call(
        functools.partial(pieces_kernel, factor, [[Ellipsis]] * 3),
        [piece, piece_in],
        "pieces",
        place_at,
        a,
        b,
        c,
    )
    after = move(mine_in, owner_pairs(1))
    before = move(mine_in, owner_pairs(3))
    far = move(mine, FAR_PAIRS)
    (rows,) = small_call(
        gather_kernel,
        [jax.ShapeDtypeStruct((5 * (dim // 32), dim), F32)],
        "gather",
        place_at,
        mine,
        after,
        far,
        before,
    )
    grad_in, grad_out = small_call(
        last_kernel,
        [
            jax.ShapeDtypeStruct((width // 4, dim), F32),
            jax.ShapeDtypeStruct((dim // 32, 4 * width), F32),
        ],
        "last",
        place_at,
        rows,
        move(rows, CORE_PAIRS),
    )
    return (grad_in, grad_out, grad_normed)


def solution(mesh):
    placed = (P(AXES, None), P(), P(), P(AXES, None))
    return jax.shard_map(
        local,
        mesh=mesh,
        in_specs=placed,
        out_specs=(P("dp", None), P("dp", None), P(AXES, None)),
        check_vma=False,
    )
```

```python
import functools

import jax
import jax.numpy as jnp
import numpy as np
from jax import lax
from jax.experimental import pallas as pl
from jax.experimental.pallas import tpu as pltpu
from jax.sharding import PartitionSpec as P

AXES = ("grp", "dp")
BF = jnp.bfloat16
F32 = jnp.float32
OWN_LIMIT = 62 * 2**20
CHUNK_LIMIT = 62 * 2**20
BACK_LIMIT = 36 * 2**20
SMALL_LIMIT = 8 * 2**20


def place(x, y, z, c):
    return ((x // 2) * 2 + c) * 32 + z * 8 + (x % 2) * 4 + y


EVERY = [(x, y, z, c) for x in range(4) for y in range(4) for z in range(4) for c in range(2)]


def partner(i, core, step):
    return (i + (1 if i % 2 == (core + step) % 2 else -1)) % 4


def halving_pairs(axis, step):
    pairs = []
    for x, y, z, c in EVERY:
        at = [x, y, z]
        at[axis] = partner(at[axis], c, step)
        pairs.append((place(x, y, z, c), place(*at, c)))
    return pairs


X0, X1 = halving_pairs(0, 0), halving_pairs(0, 1)
Y0, Y1 = halving_pairs(1, 0), halving_pairs(1, 1)
Z0, Z1 = halving_pairs(2, 0), halving_pairs(2, 1)
CORE_PAIRS = [(place(x, y, z, c), place(x, y, z, 1 - c)) for x, y, z, c in EVERY]
FAR_PAIRS = [(place(x, y, z, c), place((x + 2) % 4, y, z, c)) for x, y, z, c in EVERY]


def owner_pairs(shift):
    return [
        (place((x + shift) % 4, y, z, c), place(x, y, z, c))
        for x, y, z, c in EVERY
        if x % 2 == c
    ]


def ring_order(i, core):
    first, second = partner(i, core, 0), partner(i, core, 1)
    return [partner(first, core, 1), first, second, i]


CORE, CHUNK, KIND, HALF, XAT, YAT, ZAT = 0, 1, 3, 7, 9, 13, 17
OWN_HALF, X, IS_OWNER, WIDTH = 22, 23, 24, 32


def table():
    rows = np.zeros((len(EVERY), WIDTH), np.int32)
    for x, y, z, c in EVERY:
        row = rows[place(x, y, z, c)]
        row[CORE] = c
        xs, ys, zs = ring_order(x, c), ring_order(y, c), ring_order(z, c)
        row[CHUNK], row[CHUNK + 1] = 1 - z % 2, z % 2
        row[KIND : KIND + 4] = [zs[1] // 2, zs[2] // 2, zs[0] // 2, zs[3] // 2]
        labels = {i: (i % 2, i // 2 if c == 0 else (i // 2) ^ (i % 2)) for i in range(4)}
        for k in range(2):
            (row[HALF + k],) = [labels[i][0] for i in xs[2:] if labels[i][1] == row[CHUNK + k]]
        for at, order in ((XAT, xs), (YAT, ys), (ZAT, zs)):
            for rank, i in enumerate(order):
                row[at + rank] = i
        row[OWN_HALF] = labels[x][1]
        row[X] = x
        row[IS_OWNER] = int(x % 2 == c)
    return rows


TWO_BITS = [*range(XAT, ZAT + 4), X]
FIELDS = {at: (0, 2 * i, 3) for i, at in enumerate(TWO_BITS)}
ONE_BIT = [CORE, CHUNK, CHUNK + 1, *range(KIND, KIND + 4), HALF, HALF + 1, OWN_HALF, IS_OWNER]
FIELDS.update({at: (1, i, 1) for i, at in enumerate(ONE_BIT)})


def packed():
    rows = table()
    words = np.zeros((len(EVERY), 2), np.int32)
    for at, (word, shift, _) in FIELDS.items():
        words[:, word] |= rows[:, at] << shift
    return words


TABLE = packed()


def field(index, table, at):
    word, shift, mask = FIELDS[at]
    return (table[index[0] * 2 + word] >> shift) & mask


NT = (((1,), (1,)), ((), ()))
TN = (((0,), (0,)), ((), ()))


def row_of(index, table):
    class Row:
        def __getitem__(self, at):
            return field(index, table, at)

    return Row()


def gated(value, gate, dact):
    cdf = 0.5 * (1.0 + lax.erf(gate * (2.0 ** -0.5)))
    density = jnp.exp(-0.5 * gate * gate) * ((2.0 * jnp.pi) ** -0.5)
    share = gate * cdf
    return (
        (value * share).astype(BF),
        (dact * share).astype(BF),
        (dact * value * (cdf + gate * density)).astype(BF),
    )


class Copies:
    def __init__(self, sems):
        self.sems, self.used = sems, 0

    def start(self, source, target):
        copy = pltpu.make_async_copy(source, target, self.sems.at[self.used])
        self.used += 1
        copy.start()
        return copy


def own_kernel(index, table, win, wout, n_in, c_in, d_out, act_out, w, wo, n, c, d, act, sems):
    tab = row_of(index, table)
    width = w.shape[2]
    copies = Copies(sems)
    load_w, load_wo = [], []
    for k in range(2):
        block, core = tab[CHUNK + k], tab[CORE]
        column = pl.multiple_of((block * 2 + core) * width, 128)
        load_wo.append(copies.start(wout.at[:, pl.ds(column, width)], wo.at[k]))
        if k == 0:
            load_c = copies.start(c_in, c)
        load_w.append([copies.start(win.at[i, block, core], w.at[k, i]) for i in range(2)])
        if k == 0:
            load_n = copies.start(n_in, n)
    stores = []
    for k in range(2):
        load_wo[k].wait()
        if k == 0:
            load_c.wait()
        dact = jnp.dot(c[...], wo[k], preferred_element_type=F32)
        for copy in load_w[k]:
            copy.wait()
        if k == 0:
            load_n.wait()
        proj = lax.dot_general(
            n[...], w[k].reshape(2 * width, w.shape[3]), NT, preferred_element_type=F32
        )
        act[k], d[k, 0], d[k, 1] = gated(proj[:, :width], proj[:, width:], dact)
        stores.append(copies.start(act.at[k], act_out.at[k]))
        stores.append(copies.start(d.at[k], d_out.at[k]))
    for copy in stores:
        copy.wait()


def own_call(place_at, win, wout, normed, cot):
    count, dim = normed.shape
    width = win.shape[3]
    anywhere = pl.BlockSpec(memory_space=pl.ANY)
    return pl.pallas_call(
        own_kernel,
        grid_spec=pltpu.PrefetchScalarGridSpec(
            num_scalar_prefetch=2,
            grid=(1,),
            in_specs=[anywhere] * 4,
            out_specs=[anywhere] * 2,
            scratch_shapes=[
                pltpu.VMEM((2, 2, width, dim), BF),
                pltpu.VMEM((2, dim, width), BF),
                pltpu.VMEM((count, dim), BF),
                pltpu.VMEM((count, dim), BF),
                pltpu.VMEM((2, 2, count, width), BF),
                pltpu.VMEM((2, count, width), BF),
                pltpu.SemaphoreType.DMA((12,)),
            ],
        ),
        out_shape=[
            jax.ShapeDtypeStruct((2, 2, count, width), BF),
            jax.ShapeDtypeStruct((2, count, width), BF),
        ],
        compiler_params=pltpu.CompilerParams(vmem_limit_bytes=OWN_LIMIT),
        cost_estimate=pl.CostEstimate(
            flops=12 * count * dim * width, bytes_accessed=16 * 2**20, transcendentals=0
        ),
        name="own_terms",
    )(*place_at, win, wout, normed, cot)


def chunk_kernel(
    chunk, index, table, win, wout, n_in, c_in, n_own, c_own, d_own, act_own,
    a_send, a_keep, b_send, b_keep, c_send, c_keep, d_out,
    w, wo, nb, cb, d, act, gin, gout, load_sems, sems,
):
    tab = row_of(index, table)
    width, dim = w.shape[1:]
    count = n_in.shape[0]
    half = dim // 2
    core, block = tab[CORE], tab[CHUNK + chunk]
    own, oth = pl.ds(count, count), pl.ds(0, count)
    loads = Copies(load_sems)
    column = pl.multiple_of((block * 2 + core) * width, 128)
    load_wo = loads.start(wout.at[:, pl.ds(column, width)], wo)
    lanes = [pl.ds(part * half, half) for part in range(2)]
    raw = gin.at[:, :, oth]
    load_c = [loads.start(c_in.at[:, lanes[i]], raw.at[0, i]) for i in range(2)]
    load_w = [loads.start(win.at[i, block, core], w.at[i]) for i in range(2)]
    load_n = [loads.start(n_in.at[:, lanes[i]], raw.at[1, i]) for i in range(2)]
    load_own = [loads.start(c_own, cb.at[own]), loads.start(act_own.at[chunk], act.at[own])]
    load_own += [loads.start(d_own.at[chunk, i], d.at[i, own]) for i in range(2)]
    load_own += [loads.start(n_own, nb.at[own])]

    def store(source, target, sem):
        pltpu.make_async_copy(source, target, sems.at[sem]).start()

    load_wo.wait()
    for i in range(2):
        load_c[i].wait()
        cb[oth, i * half : (i + 1) * half] = raw[0, i].astype(BF)
    dact = jnp.dot(cb[oth], wo[...], preferred_element_type=F32)
    for i in range(2):
        load_n[i].wait()
        nb[oth, i * half : (i + 1) * half] = raw[1, i].astype(BF)
    for copy in load_w:
        copy.wait()
    proj = lax.dot_general(
        nb[oth], w[...].reshape(2 * width, dim), NT, preferred_element_type=F32
    )
    act[oth], d[0, oth], d[1, oth] = gated(proj[:, :width], proj[:, width:], dact)
    for i in range(2):
        store(d.at[i, oth], d_out.at[i], 0)
    for copy in load_own:
        copy.wait()

    gout[...] = lax.dot_general(cb[...], act[...], TN, preferred_element_type=F32)
    tiny = dim // 32
    kept = tab[HALF + chunk]
    for out, x, sem in ((c_send, 1 - kept, 1), (c_keep, kept, 2)):
        for z in range(4):
            for y in range(4):
                at = ((tab[ZAT + z] * 2 + x) * 4 + tab[YAT + y]) * tiny
                store(gout.at[pl.ds(pl.multiple_of(at, 8), tiny)], out.at[z, y], sem)
    small = width // 16
    for slot, out in enumerate((a_send, a_keep)):
        kind = tab[KIND + 2 * chunk + slot]
        for part in range(2):
            cut = slice(part * half, (part + 1) * half)
            gin[slot, part] = lax.dot_general(
                d[kind], nb[:, cut], TN, preferred_element_type=F32
            )
            for y in range(4):
                for x in range(4):
                    at = (tab[YAT + y] * 4 + tab[XAT + x]) * small
                    rows = gin.at[slot, part, pl.ds(pl.multiple_of(at, 8), small)]
                    if part == 0:
                        store(rows, out.at[y, x], 3 + slot)
                    else:
                        store(rows, (b_send, b_keep)[y // 2].at[y % 2, x, slot], 5 + y // 2)
    outs = (d_out, c_send, c_keep, a_send, a_keep, b_send, b_keep)
    for i, out in enumerate(outs):
        pltpu.make_async_copy(out, out, sems.at[i]).wait()


def chunk_call(place_at, win, wout, other, own, terms, chunk):
    count, dim = own[0].shape
    width = win.shape[3]
    a = jax.ShapeDtypeStruct((4, 4, width // 16, dim // 2), F32)
    b = jax.ShapeDtypeStruct((2, 4, 2, width // 16, dim // 2), F32)
    c = jax.ShapeDtypeStruct((4, 4, dim // 32, width), F32)
    outs = [a, a, b, b, c, c, jax.ShapeDtypeStruct((2, count, width), BF)]
    operands = [win, wout, *other, *own, *terms]
    anywhere = pl.BlockSpec(memory_space=pl.ANY)
    return pl.pallas_call(
        functools.partial(chunk_kernel, chunk),
        grid_spec=pltpu.PrefetchScalarGridSpec(
            num_scalar_prefetch=2,
            grid=(1,),
            in_specs=[anywhere] * len(operands),
            out_specs=[anywhere] * len(outs),
            scratch_shapes=[
                pltpu.VMEM((2, width, dim), BF),
                pltpu.VMEM((dim, width), BF),
                pltpu.VMEM((2 * count, dim), BF),
                pltpu.VMEM((2 * count, dim), BF),
                pltpu.VMEM((2, 2 * count, width), BF),
                pltpu.VMEM((2 * count, width), BF),
                pltpu.VMEM((2, 2, width, dim // 2), F32),
                pltpu.VMEM((dim, width), F32),
                pltpu.SemaphoreType.DMA((12,)),
                pltpu.SemaphoreType.DMA((7,)),
            ],
        ),
        out_shape=outs,
        compiler_params=pltpu.CompilerParams(vmem_limit_bytes=CHUNK_LIMIT),
        cost_estimate=pl.CostEstimate(
            flops=16 * count * dim * width, bytes_accessed=16 * 2**20, transcendentals=0
        ),
        name="chunk",
    )(*place_at, *operands)


def back_kernel(index, table, own_ref, oth0_ref, oth1_ref, w_ref, oth_out, own_out):
    tab = row_of(index, table)
    w = w_ref[...].reshape(2 * w_ref.shape[1], w_ref.shape[2])
    straight = tab[CHUNK] == 0
    for d0, d1, out in (
        (oth0_ref[...], oth1_ref[...], oth_out),
        (own_ref[0], own_ref[1], own_out),
    ):
        low = jnp.where(straight, d0, d1)
        high = jnp.where(straight, d1, d0)
        part = jnp.dot(jnp.concatenate([low, high], axis=1), w, preferred_element_type=F32)

        @pl.when(pl.program_id(0) == 0)
        def _():
            out[...] = part

        @pl.when(pl.program_id(0) == 1)
        def _():
            out[...] += part


def back(place_at, own, oth0, oth1, win):
    _, count, width = oth0.shape
    dim = win.shape[4]
    whole = pl.BlockSpec((count, dim), lambda k, i, t: (0, 0))
    d_spec = pl.BlockSpec((None, count, width), lambda k, i, t: (k, 0, 0))
    return pl.pallas_call(
        back_kernel,
        grid_spec=pltpu.PrefetchScalarGridSpec(
            num_scalar_prefetch=2,
            grid=(2,),
            in_specs=[
                pl.BlockSpec((2, None, count, width), lambda k, i, t: (0, k, 0, 0)),
                d_spec,
                d_spec,
                pl.BlockSpec(
                    (None, 2, None, width, dim),
                    lambda k, i, t: (k, 0, field(i, t, CORE), 0, 0),
                ),
            ],
            out_specs=[whole, whole],
        ),
        out_shape=[jax.ShapeDtypeStruct((count, dim), F32)] * 2,
        compiler_params=pltpu.CompilerParams(vmem_limit_bytes=BACK_LIMIT),
        cost_estimate=pl.CostEstimate(
            flops=16 * count * dim * width, bytes_accessed=16 * 2**20, transcendentals=0
        ),
        name="back",
    )(*place_at, own, oth0, oth1, win)


def small_call(kernel, out_shape, name, place_at, *operands):
    return pl.pallas_call(
        kernel,
        grid_spec=pltpu.PrefetchScalarGridSpec(
            num_scalar_prefetch=2,
            grid=(1,),
            in_specs=[
                pl.BlockSpec(o.shape, functools.partial(lambda n, *_: (0,) * n, o.ndim))
                for o in operands
            ],
            out_specs=[
                pl.BlockSpec(o.shape, functools.partial(lambda n, *_: (0,) * n, len(o.shape)))
                for o in out_shape
            ],
        ),
        out_shape=out_shape,
        compiler_params=pltpu.CompilerParams(vmem_limit_bytes=SMALL_LIMIT),
        cost_estimate=pl.CostEstimate(flops=2**20, bytes_accessed=2**20, transcendentals=0),
        name=name,
    )(*place_at, *operands)


def sums_kernel(sizes, *refs):
    out = refs[-1]
    at = 0
    for i, size in enumerate(sizes):
        out[i, 0] = functools.reduce(lambda p, q: p + q, [r[0] for r in refs[at : at + size]])
        at += size


def sums(groups, rows, count, stride=1):
    lanes = groups[0][0][0].shape[-1]
    tile = min(rows, 160)
    operands, specs = [], []
    for group in groups:
        for array, first in group:
            operands.append(array.reshape(-1, rows, lanes))
            specs.append(
                pl.BlockSpec((1, tile, lanes), functools.partial(lambda f, i, j: (f + i * stride, j, 0), first))
            )
    return pl.pallas_call(
        functools.partial(sums_kernel, [len(group) for group in groups]),
        grid=(count, rows // tile),
        in_specs=specs,
        out_specs=pl.BlockSpec((len(groups), 1, tile, lanes), lambda i, j: (0, i, j, 0)),
        out_shape=jax.ShapeDtypeStruct((len(groups), count, rows, lanes), F32),
        compiler_params=pltpu.CompilerParams(vmem_limit_bytes=SMALL_LIMIT),
        cost_estimate=pl.CostEstimate(
            flops=2**20, bytes_accessed=4 * 2**20, transcendentals=0
        ),
        name="sums",
    )(*operands)


def pieces_kernel(factor, counts, index, table, *refs):
    refs, (all_ref, in_ref) = refs[:-2], refs[-2:]
    at = 0
    for i, picks in enumerate(counts):
        terms = []
        for pick in picks:
            terms.append(refs[at][pick])
            at += 1
        whole = functools.reduce(lambda p, q: p + q, terms) * factor
        all_ref[i] = whole
        if i < 2:
            in_ref[i] = whole


def gather_kernel(index, table, all_ref, next_ref, far_ref, last_ref, out):
    tab = row_of(index, table)
    rows, half = all_ref.shape[1:]
    for i, ref in enumerate((all_ref, next_ref, far_ref, last_ref)):
        place_at = lax.rem(tab[X] + i, 4) * rows
        here = pl.ds(pl.multiple_of(place_at, 8), rows)
        out[here, :half] = ref[0]
        out[here, half:] = ref[1]
    low = tab[OWN_HALF] == 0
    out[4 * rows :, :half] = jnp.where(low, all_ref[2], far_ref[2])
    out[4 * rows :, half:] = jnp.where(low, far_ref[2], all_ref[2])


def last_kernel(index, table, own_ref, oth_ref, in_ref, out_ref):
    tab = row_of(index, table)
    count, half = in_ref.shape[0], in_ref.shape[1] // 2
    owner, zero = tab[IS_OWNER] == 1, tab[CORE] == 0
    in_ref[...] = jnp.where(owner, own_ref[:count], oth_ref[:count])
    own, oth = own_ref[count:], oth_ref[count:]
    for i in range(2):
        cut = slice(i * half, (i + 1) * half)
        out_ref[:, 2 * i * half : (2 * i + 1) * half] = jnp.where(zero, own[:, cut], oth[:, cut])
        out_ref[:, (2 * i + 1) * half : (2 * i + 2) * half] = jnp.where(
            zero, oth[:, cut], own[:, cut]
        )


def move(array, pairs):
    return lax.ppermute(array, AXES, pairs)


def total(terms):
    return functools.reduce(lambda p, q: p + q, terms)


def settle(array):
    return lax.optimization_barrier(array)


def after(array, other):
    return lax.optimization_barrier((array, other))[0]


def local(normed, w_in, w_out, cotangent):
    dim = normed.shape[1]
    width = w_out.shape[1] // 4
    factor = (normed.shape[0] * lax.axis_size("dp") * lax.axis_size("grp")) ** (-0.5)
    index = lax.axis_index(AXES).reshape(1)
    place_at = index, jnp.asarray(TABLE.reshape(-1))
    win = w_in.reshape(2, 2, 2, width, dim)

    wide = lax.optimization_barrier((normed.astype(F32), cotangent.astype(F32)))
    own = normed, cotangent
    other = move(wide[0], CORE_PAIRS), move(wide[1], CORE_PAIRS)
    terms = own_call(place_at, win, w_out, normed, cotangent)
    *first, oth0 = chunk_call(place_at, win, w_out, other, own, terms, 0)
    got_a0, got_b0, got_c0 = move(first[0], Z0), move(first[2], Y0), move(first[4], X0)
    index, _ = lax.optimization_barrier((index, first[0]))
    place_at = index, place_at[1]
    *second, oth1 = chunk_call(place_at, win, w_out, other, own, terms, 1)
    got_a1, got_b1, got_c1 = move(second[0], Z0), move(second[2], Y0), move(second[4], X0)

    oth0, index, got_a0, got_b0, early_c = lax.optimization_barrier(
        (oth0, index, got_a0, got_b0, first[5] + got_c0)
    )
    back_oth, back_own = back(place_at, terms[0], oth0, oth1, win)
    got_a1, got_b1, got_c1, back_own = lax.optimization_barrier(
        (got_a1, got_b1, got_c1, back_own)
    )
    grad_normed = (back_own + move(back_oth, CORE_PAIRS)).astype(BF)

    grp, dp = lax.axis_index("grp"), lax.axis_index("dp")
    own_first = ((dp >> 3) & 1) != ((grp >> 1) ^ (grp & (dp >> 2) & 1))

    rows = width // 2
    a = [second[1], got_a0]
    b = [first[3], got_b0], [second[3], got_b1]
    c = [early_c], [second[5], got_c1]
    to_b = sums([[(t, 0) for t in chunk] for chunk in b], rows, 1)
    got_b = move(to_b, Y1)
    to_c = jnp.where(own_first, total([after(second[5], to_b), got_c1]), early_c)
    got_c = move(to_c, X1)
    to_a = total([first[1], after(got_a1, to_c)])
    got_a = move(to_a, Z1)
    a = [settle(total(a)), got_a]
    b = [[(t, 4) for t in chunk] + [(got_b, 4 * k)] for k, chunk in enumerate(b)]
    c = [settle(jnp.where(own_first, total(c[0]), total(c[1]))), got_c]

    rows = width // 8
    to_b = sums(b, rows, 2)
    got_b = move(to_b, X0)
    b = [sums([[(t, at + 2) for t, at in chunk] for chunk in b], rows, 2), got_b]
    c[-1] = after(c[-1], to_b)
    to_c = total([t[:2] for t in c])
    got_c = move(to_c, Z0)
    c = [settle(total([t[2:] for t in c])), got_c]
    a[-1] = after(a[-1], to_c)
    to_a = total([t[:2] for t in a])
    got_a = move(to_a, Y0)
    kept, grad_normed = settle((total([t[2:] for t in a]), grad_normed))
    a = [kept, got_a]

    b[-1] = after(b[-1], to_a)
    to_b = sums([[(t, 0) for t in b]], rows, 2, 2)
    got_b = move(to_b, X1)
    b = [sums([[(t, 1) for t in b]], rows, 2, 2), got_b]
    c[-1] = after(c[-1], to_b)
    to_c = total([t[0] for t in c])
    got_c = move(to_c, Z1)
    c = [t[1] for t in c] + [got_c]
    a[-1] = after(a[-1], to_c)
    to_a = total([t[0] for t in a])
    got_a = move(to_a, Y1)
    a = [t[1] for t in a] + [got_a]

    rows = width // 16
    b[-1] = after(b[-1], to_a)
    to_b = sums([[(t, 2) for t in b]], rows, 2, -2)
    got_b = move(to_b, Z0)
    b = [sums([[(t, 1) for t in b]], rows, 2, 2)[0], got_b[0]]
    c[-1] = after(c[-1], to_b)
    to_c = total([t[:2] for t in c])
    got_c = move(to_c, Y0)
    c = [t[2:] for t in c] + [got_c]
    a[-1] = after(a[-1], to_c)
    to_a = total([t[:2] for t in a])
    got_a = move(to_a, X0)
    a = [t[2:] for t in a] + [got_a]

    b[-1] = after(b[-1], to_a)
    to_b = total([t[0] for t in b])
    got_b = move(to_b, Z1)
    c[-1] = after(c[-1], to_b)
    to_c = total([t[0] for t in c])
    got_c = move(to_c, Y1)
    a[-1] = after(a[-1], to_c)
    to_a = total([t[0] for t in a])
    got_a = move(to_a, X1)
    a, b, c = (
        total([t[1] for t in terms] + [got])
        for terms, got in ((a, got_a), (b, got_b), (c, got_c))
    )

    half = dim // 2
    piece = jax.ShapeDtypeStruct((3, dim // 32, half), F32)
    piece_in = jax.ShapeDtypeStruct((2, dim // 32, half), F32)
    mine, mine_in = small_call(
        functools.partial(pieces_kernel, factor, [[Ellipsis]] * 3),
        [piece, piece_in],
        "pieces",
        place_at,
        a,
        b,
        c,
    )
    higher = move(mine_in, owner_pairs(1))
    lower = move(mine_in, owner_pairs(3))
    far = move(mine, FAR_PAIRS)
    (rows,) = small_call(
        gather_kernel,
        [jax.ShapeDtypeStruct((5 * (dim // 32), dim), F32)],
        "gather",
        place_at,
        mine,
        higher,
        far,
        lower,
    )
    grad_in, grad_out = small_call(
        last_kernel,
        [
            jax.ShapeDtypeStruct((width // 4, dim), F32),
            jax.ShapeDtypeStruct((dim // 32, 4 * width), F32),
        ],
        "last",
        place_at,
        rows,
        move(rows, CORE_PAIRS),
    )
    return (grad_in, grad_out, grad_normed)


def solution(mesh):
    placed = (P(AXES, None), P(), P(), P(AXES, None))
    return jax.shard_map(
        local,
        mesh=mesh,
        in_specs=placed,
        out_specs=(P("dp", None), P("dp", None), P(AXES, None)),
        check_vma=False,
    )
```

```python
import functools

import jax
import jax.numpy as jnp
import numpy as np
from jax import lax
from jax.experimental import pallas as pl
from jax.experimental.pallas import tpu as pltpu
from jax.sharding import PartitionSpec as P

AXES = ("grp", "dp")
BF = jnp.bfloat16
F32 = jnp.float32
OWN_LIMIT = 62 * 2**20
CHUNK_LIMIT = 62 * 2**20
BACK_LIMIT = 36 * 2**20
SMALL_LIMIT = 8 * 2**20


def place(x, y, z, c):
    return ((x // 2) * 2 + c) * 32 + z * 8 + (x % 2) * 4 + y


EVERY = [(x, y, z, c) for x in range(4) for y in range(4) for z in range(4) for c in range(2)]


def partner(i, core, step):
    return (i + (1 if i % 2 == (core + step) % 2 else -1)) % 4


def halving_pairs(axis, step):
    pairs = []
    for x, y, z, c in EVERY:
        at = [x, y, z]
        at[axis] = partner(at[axis], c, step)
        pairs.append((place(x, y, z, c), place(*at, c)))
    return pairs


X0, X1 = halving_pairs(0, 0), halving_pairs(0, 1)
Y0, Y1 = halving_pairs(1, 0), halving_pairs(1, 1)
Z0, Z1 = halving_pairs(2, 0), halving_pairs(2, 1)
CORE_PAIRS = [(place(x, y, z, c), place(x, y, z, 1 - c)) for x, y, z, c in EVERY]
FAR_PAIRS = [(place(x, y, z, c), place((x + 2) % 4, y, z, c)) for x, y, z, c in EVERY]


def owns(x, core):
    return x % 2 == core


LOWER_PAIRS = [
    (
        place(x, y, z, c),
        place((x + 2) % 4, y, z, 1 - c) if owns(x, c) else place((x - 1) % 4, y, z, c),
    )
    for x, y, z, c in EVERY
]
UPPER_PAIRS = [
    (place(x, y, z, c), place((x + 1) % 4, y, z, c)) for x, y, z, c in EVERY if not owns(x, c)
]


def ring_order(i, core):
    first, second = partner(i, core, 0), partner(i, core, 1)
    return [partner(first, core, 1), first, second, i]


CORE, CHUNK, KIND, HALF, XAT, YAT, ZAT = 0, 1, 3, 7, 9, 13, 17
OWN_HALF, X, IS_OWNER, WIDTH = 22, 23, 24, 32


def table():
    rows = np.zeros((len(EVERY), WIDTH), np.int32)
    for x, y, z, c in EVERY:
        row = rows[place(x, y, z, c)]
        row[CORE] = c
        xs, ys, zs = ring_order(x, c), ring_order(y, c), ring_order(z, c)
        row[CHUNK], row[CHUNK + 1] = 1 - z % 2, z % 2
        row[KIND : KIND + 4] = [zs[1] // 2, zs[2] // 2, zs[0] // 2, zs[3] // 2]
        labels = {i: (i % 2, i // 2 if c == 0 else (i // 2) ^ (i % 2)) for i in range(4)}
        for k in range(2):
            (row[HALF + k],) = [labels[i][0] for i in xs[2:] if labels[i][1] == row[CHUNK + k]]
        for at, order in ((XAT, xs), (YAT, ys), (ZAT, zs)):
            for rank, i in enumerate(order):
                row[at + rank] = i
        row[OWN_HALF] = labels[x][1]
        row[X] = x
        row[IS_OWNER] = int(owns(x, c))
    return rows


TWO_BITS = [*range(XAT, ZAT + 4), X]
FIELDS = {at: (0, 2 * i, 3) for i, at in enumerate(TWO_BITS)}
ONE_BIT = [CORE, CHUNK, CHUNK + 1, *range(KIND, KIND + 4), HALF, HALF + 1, OWN_HALF, IS_OWNER]
FIELDS.update({at: (1, i, 1) for i, at in enumerate(ONE_BIT)})


def packed():
    rows = table()
    words = np.zeros((len(EVERY), 2), np.int32)
    for at, (word, shift, _) in FIELDS.items():
        words[:, word] |= rows[:, at] << shift
    return words


TABLE = packed()


def field(index, table, at):
    word, shift, mask = FIELDS[at]
    return (table[index[0] * 2 + word] >> shift) & mask


NT = (((1,), (1,)), ((), ()))
TN = (((0,), (0,)), ((), ()))


def row_of(index, table):
    class Row:
        def __getitem__(self, at):
            return field(index, table, at)

    return Row()


def gated(value, gate, dact):
    cdf = 0.5 * (1.0 + lax.erf(gate * (2.0 ** -0.5)))
    density = jnp.exp(-0.5 * gate * gate) * ((2.0 * jnp.pi) ** -0.5)
    share = gate * cdf
    return (
        (value * share).astype(BF),
        (dact * share).astype(BF),
        (dact * value * (cdf + gate * density)).astype(BF),
    )


class Copies:
    def __init__(self, sems):
        self.sems, self.used = sems, 0

    def start(self, source, target):
        copy = pltpu.make_async_copy(source, target, self.sems.at[self.used])
        self.used += 1
        copy.start()
        return copy


def own_kernel(index, table, win, wout, n_in, c_in, d_out, act_out, w, wo, n, c, d, act, sems):
    tab = row_of(index, table)
    width = w.shape[2]
    copies = Copies(sems)
    load_w, load_wo = [], []
    for k in range(2):
        block, core = tab[CHUNK + k], tab[CORE]
        column = pl.multiple_of((block * 2 + core) * width, 128)
        load_wo.append(copies.start(wout.at[:, pl.ds(column, width)], wo.at[k]))
        if k == 0:
            load_c = copies.start(c_in, c)
        load_w.append([copies.start(win.at[i, block, core], w.at[k, i]) for i in range(2)])
        if k == 0:
            load_n = copies.start(n_in, n)
    stores = []
    for k in range(2):
        load_wo[k].wait()
        if k == 0:
            load_c.wait()
        dact = jnp.dot(c[...], wo[k], preferred_element_type=F32)
        for copy in load_w[k]:
            copy.wait()
        if k == 0:
            load_n.wait()
        proj = lax.dot_general(
            n[...], w[k].reshape(2 * width, w.shape[3]), NT, preferred_element_type=F32
        )
        act[k], d[k, 0], d[k, 1] = gated(proj[:, :width], proj[:, width:], dact)
        stores.append(copies.start(act.at[k], act_out.at[k]))
        stores.append(copies.start(d.at[k], d_out.at[k]))
    for copy in stores:
        copy.wait()


def own_call(place_at, win, wout, normed, cot):
    count, dim = normed.shape
    width = win.shape[3]
    anywhere = pl.BlockSpec(memory_space=pl.ANY)
    return pl.pallas_call(
        own_kernel,
        grid_spec=pltpu.PrefetchScalarGridSpec(
            num_scalar_prefetch=2,
            grid=(1,),
            in_specs=[anywhere] * 4,
            out_specs=[anywhere] * 2,
            scratch_shapes=[
                pltpu.VMEM((2, 2, width, dim), BF),
                pltpu.VMEM((2, dim, width), BF),
                pltpu.VMEM((count, dim), BF),
                pltpu.VMEM((count, dim), BF),
                pltpu.VMEM((2, 2, count, width), BF),
                pltpu.VMEM((2, count, width), BF),
                pltpu.SemaphoreType.DMA((12,)),
            ],
        ),
        out_shape=[
            jax.ShapeDtypeStruct((2, 2, count, width), BF),
            jax.ShapeDtypeStruct((2, count, width), BF),
        ],
        compiler_params=pltpu.CompilerParams(vmem_limit_bytes=OWN_LIMIT),
        cost_estimate=pl.CostEstimate(
            flops=12 * count * dim * width, bytes_accessed=16 * 2**20, transcendentals=0
        ),
        name="own_terms",
    )(*place_at, win, wout, normed, cot)


def chunk_kernel(
    chunk, index, table, win, wout, n_in, c_in, n_own, c_own, d_own, act_own,
    a_send, a_keep, b_send, b_keep, c_send, c_keep, d_out,
    w, wo, nb, cb, d, act, gin, gout, load_sems, sems,
):
    tab = row_of(index, table)
    width, dim = w.shape[1:]
    count = n_in.shape[0]
    half = dim // 2
    core, block = tab[CORE], tab[CHUNK + chunk]
    own, oth = pl.ds(count, count), pl.ds(0, count)
    loads = Copies(load_sems)
    column = pl.multiple_of((block * 2 + core) * width, 128)
    load_wo = loads.start(wout.at[:, pl.ds(column, width)], wo)
    lanes = [pl.ds(part * half, half) for part in range(2)]
    raw = gin.at[:, :, oth]
    load_c = [loads.start(c_in.at[:, lanes[i]], raw.at[0, i]) for i in range(2)]
    load_w = [loads.start(win.at[i, block, core], w.at[i]) for i in range(2)]
    load_n = [loads.start(n_in.at[:, lanes[i]], raw.at[1, i]) for i in range(2)]
    load_own = [loads.start(c_own, cb.at[own]), loads.start(act_own.at[chunk], act.at[own])]
    load_own += [loads.start(d_own.at[chunk, i], d.at[i, own]) for i in range(2)]
    load_own += [loads.start(n_own, nb.at[own])]

    def store(source, target, sem):
        pltpu.make_async_copy(source, target, sems.at[sem]).start()

    load_wo.wait()
    for i in range(2):
        load_c[i].wait()
        cb[oth, i * half : (i + 1) * half] = raw[0, i].astype(BF)
    dact = jnp.dot(cb[oth], wo[...], preferred_element_type=F32)
    for i in range(2):
        load_n[i].wait()
        nb[oth, i * half : (i + 1) * half] = raw[1, i].astype(BF)
    for copy in load_w:
        copy.wait()
    proj = lax.dot_general(
        nb[oth], w[...].reshape(2 * width, dim), NT, preferred_element_type=F32
    )
    act[oth], d[0, oth], d[1, oth] = gated(proj[:, :width], proj[:, width:], dact)
    for i in range(2):
        store(d.at[i, oth], d_out.at[i], 0)
    for copy in load_own:
        copy.wait()

    gout[...] = lax.dot_general(cb[...], act[...], TN, preferred_element_type=F32)
    tiny = dim // 32
    kept = tab[HALF + chunk]
    for out, x, sem in ((c_send, 1 - kept, 1), (c_keep, kept, 2)):
        for z in range(4):
            for y in range(4):
                at = ((tab[ZAT + z] * 2 + x) * 4 + tab[YAT + y]) * tiny
                store(gout.at[pl.ds(pl.multiple_of(at, 8), tiny)], out.at[z, y], sem)
    small = width // 16
    for slot, out in enumerate((a_send, a_keep)):
        kind = tab[KIND + 2 * chunk + slot]
        for part in range(2):
            cut = slice(part * half, (part + 1) * half)
            gin[slot, part] = lax.dot_general(
                d[kind], nb[:, cut], TN, preferred_element_type=F32
            )
            for y in range(4):
                for x in range(4):
                    at = (tab[YAT + y] * 4 + tab[XAT + x]) * small
                    rows = gin.at[slot, part, pl.ds(pl.multiple_of(at, 8), small)]
                    if part == 0:
                        store(rows, out.at[y, x], 3 + slot)
                    else:
                        store(rows, (b_send, b_keep)[y // 2].at[y % 2, x, slot], 5 + y // 2)
    outs = (d_out, c_send, c_keep, a_send, a_keep, b_send, b_keep)
    for i, out in enumerate(outs):
        pltpu.make_async_copy(out, out, sems.at[i]).wait()


def chunk_call(place_at, win, wout, other, own, terms, chunk):
    count, dim = own[0].shape
    width = win.shape[3]
    a = jax.ShapeDtypeStruct((4, 4, width // 16, dim // 2), F32)
    b = jax.ShapeDtypeStruct((2, 4, 2, width // 16, dim // 2), F32)
    c = jax.ShapeDtypeStruct((4, 4, dim // 32, width), F32)
    outs = [a, a, b, b, c, c, jax.ShapeDtypeStruct((2, count, width), BF)]
    operands = [win, wout, *other, *own, *terms]
    anywhere = pl.BlockSpec(memory_space=pl.ANY)
    return pl.pallas_call(
        functools.partial(chunk_kernel, chunk),
        grid_spec=pltpu.PrefetchScalarGridSpec(
            num_scalar_prefetch=2,
            grid=(1,),
            in_specs=[anywhere] * len(operands),
            out_specs=[anywhere] * len(outs),
            scratch_shapes=[
                pltpu.VMEM((2, width, dim), BF),
                pltpu.VMEM((dim, width), BF),
                pltpu.VMEM((2 * count, dim), BF),
                pltpu.VMEM((2 * count, dim), BF),
                pltpu.VMEM((2, 2 * count, width), BF),
                pltpu.VMEM((2 * count, width), BF),
                pltpu.VMEM((2, 2, width, dim // 2), F32),
                pltpu.VMEM((dim, width), F32),
                pltpu.SemaphoreType.DMA((12,)),
                pltpu.SemaphoreType.DMA((7,)),
            ],
        ),
        out_shape=outs,
        compiler_params=pltpu.CompilerParams(vmem_limit_bytes=CHUNK_LIMIT),
        cost_estimate=pl.CostEstimate(
            flops=16 * count * dim * width, bytes_accessed=16 * 2**20, transcendentals=0
        ),
        name="chunk",
    )(*place_at, *operands)


def back_kernel(index, table, own_ref, oth0_ref, oth1_ref, w_ref, oth_out, own_out):
    tab = row_of(index, table)
    w = w_ref[...].reshape(2 * w_ref.shape[1], w_ref.shape[2])
    straight = tab[CHUNK] == 0
    for d0, d1, out in (
        (oth0_ref[...], oth1_ref[...], oth_out),
        (own_ref[0], own_ref[1], own_out),
    ):
        low = jnp.where(straight, d0, d1)
        high = jnp.where(straight, d1, d0)
        part = jnp.dot(jnp.concatenate([low, high], axis=1), w, preferred_element_type=F32)

        @pl.when(pl.program_id(0) == 0)
        def _():
            out[...] = part

        @pl.when(pl.program_id(0) == 1)
        def _():
            out[...] += part


def back(place_at, own, oth0, oth1, win):
    _, count, width = oth0.shape
    dim = win.shape[4]
    whole = pl.BlockSpec((count, dim), lambda k, i, t: (0, 0))
    d_spec = pl.BlockSpec((None, count, width), lambda k, i, t: (k, 0, 0))
    return pl.pallas_call(
        back_kernel,
        grid_spec=pltpu.PrefetchScalarGridSpec(
            num_scalar_prefetch=2,
            grid=(2,),
            in_specs=[
                pl.BlockSpec((2, None, count, width), lambda k, i, t: (0, k, 0, 0)),
                d_spec,
                d_spec,
                pl.BlockSpec(
                    (None, 2, None, width, dim),
                    lambda k, i, t: (k, 0, field(i, t, CORE), 0, 0),
                ),
            ],
            out_specs=[whole, whole],
        ),
        out_shape=[jax.ShapeDtypeStruct((count, dim), F32)] * 2,
        compiler_params=pltpu.CompilerParams(vmem_limit_bytes=BACK_LIMIT),
        cost_estimate=pl.CostEstimate(
            flops=16 * count * dim * width, bytes_accessed=16 * 2**20, transcendentals=0
        ),
        name="back",
    )(*place_at, own, oth0, oth1, win)


def small_call(kernel, out_shape, name, place_at, *operands):
    return pl.pallas_call(
        kernel,
        grid_spec=pltpu.PrefetchScalarGridSpec(
            num_scalar_prefetch=2,
            grid=(1,),
            in_specs=[
                pl.BlockSpec(o.shape, functools.partial(lambda n, *_: (0,) * n, o.ndim))
                for o in operands
            ],
            out_specs=[
                pl.BlockSpec(o.shape, functools.partial(lambda n, *_: (0,) * n, len(o.shape)))
                for o in out_shape
            ],
        ),
        out_shape=out_shape,
        compiler_params=pltpu.CompilerParams(vmem_limit_bytes=SMALL_LIMIT),
        cost_estimate=pl.CostEstimate(flops=2**20, bytes_accessed=2**20, transcendentals=0),
        name=name,
    )(*place_at, *operands)


def sums_kernel(sizes, *refs):
    out = refs[-1]
    at = 0
    for i, size in enumerate(sizes):
        out[i, 0] = functools.reduce(lambda p, q: p + q, [r[0] for r in refs[at : at + size]])
        at += size


def sums(groups, rows, count, stride=1):
    lanes = groups[0][0][0].shape[-1]
    tile = min(rows, 160)
    operands, specs = [], []
    for group in groups:
        for array, first in group:
            operands.append(array.reshape(-1, rows, lanes))
            specs.append(
                pl.BlockSpec((1, tile, lanes), functools.partial(lambda f, i, j: (f + i * stride, j, 0), first))
            )
    return pl.pallas_call(
        functools.partial(sums_kernel, [len(group) for group in groups]),
        grid=(count, rows // tile),
        in_specs=specs,
        out_specs=pl.BlockSpec((len(groups), 1, tile, lanes), lambda i, j: (0, i, j, 0)),
        out_shape=jax.ShapeDtypeStruct((len(groups), count, rows, lanes), F32),
        compiler_params=pltpu.CompilerParams(vmem_limit_bytes=SMALL_LIMIT),
        cost_estimate=pl.CostEstimate(
            flops=2**20, bytes_accessed=4 * 2**20, transcendentals=0
        ),
        name="sums",
    )(*operands)


def gather_kernel(factor, index, table, both_ref, c_ref, first_ref, second_ref, far_ref, out):
    tab = row_of(index, table)
    rows, half = c_ref.shape
    x, owner = tab[X], tab[IS_OWNER]
    for ref, offset in ((both_ref, 2), (both_ref, 0), (second_ref, 3), (first_ref, 2 - owner)):
        here = pl.ds(pl.multiple_of(lax.rem(x + offset, 4) * rows, 8), rows)
        out[here] = ref[...] * factor
    low = tab[OWN_HALF] == 0
    c, far = c_ref[...] * factor, far_ref[...] * factor
    out[4 * rows :, :half] = jnp.where(low, c, far)
    out[4 * rows :, half:] = jnp.where(low, far, c)


def last_kernel(index, table, own_ref, oth_ref, in_ref, out_ref):
    tab = row_of(index, table)
    count, half = in_ref.shape[0], in_ref.shape[1] // 2
    rows = count // 4
    owner, zero = tab[IS_OWNER] == 1, tab[CORE] == 0
    far = lax.rem(tab[X] + 2, 4)
    for i in range(4):
        here = slice(i * rows, (i + 1) * rows)
        mine = (far == i) != owner
        in_ref[here] = jnp.where(mine, own_ref[here], oth_ref[here])
    own, oth = own_ref[count:], oth_ref[count:]
    for i in range(2):
        cut = slice(i * half, (i + 1) * half)
        out_ref[:, 2 * i * half : (2 * i + 1) * half] = jnp.where(zero, own[:, cut], oth[:, cut])
        out_ref[:, (2 * i + 1) * half : (2 * i + 2) * half] = jnp.where(
            zero, oth[:, cut], own[:, cut]
        )


def widen_kernel(n_ref, c_ref, n_out, c_out):
    n_out[...] = n_ref[...].astype(F32)
    c_out[...] = c_ref[...].astype(F32)


def widen(normed, cot):
    count, dim = normed.shape
    tile = pl.BlockSpec((count // 4, dim), lambda i: (i, 0))
    return pl.pallas_call(
        widen_kernel,
        grid=(4,),
        in_specs=[tile, tile],
        out_specs=[tile, tile],
        out_shape=[jax.ShapeDtypeStruct((count, dim), F32)] * 2,
        compiler_params=pltpu.CompilerParams(vmem_limit_bytes=OWN_LIMIT),
        cost_estimate=pl.CostEstimate(flops=2**20, bytes_accessed=8 * 2**20, transcendentals=0),
        name="widen",
    )(normed, cot)


def move(array, pairs):
    return lax.ppermute(array, AXES, pairs)


def total(terms):
    return functools.reduce(lambda p, q: p + q, terms)


def settle(array):
    return lax.optimization_barrier(array)


def after(array, other):
    return lax.optimization_barrier((array, other))[0]


def local(normed, w_in, w_out, cotangent):
    dim = normed.shape[1]
    width = w_out.shape[1] // 4
    factor = (normed.shape[0] * lax.axis_size("dp") * lax.axis_size("grp")) ** (-0.5)
    index = lax.axis_index(AXES).reshape(1)
    place_at = index, jnp.asarray(TABLE.reshape(-1))
    win = w_in.reshape(2, 2, 2, width, dim)

    wide = widen(normed, cotangent)
    own = normed, cotangent
    other = move(wide[0], CORE_PAIRS), move(wide[1], CORE_PAIRS)
    terms = own_call(place_at, win, w_out, normed, cotangent)
    *first, oth0 = chunk_call(place_at, win, w_out, other, own, terms, 0)
    got_a0, got_b0, got_c0 = move(first[0], Z0), move(first[2], Y0), move(first[4], X0)
    index, _ = lax.optimization_barrier((index, first[0]))
    place_at = index, place_at[1]
    *second, oth1 = chunk_call(place_at, win, w_out, other, own, terms, 1)
    got_a1, got_b1, got_c1 = move(second[0], Z0), move(second[2], Y0), move(second[4], X0)

    oth0, index, got_a0, got_b0, early_c = lax.optimization_barrier(
        (oth0, index, got_a0, got_b0, first[5] + got_c0)
    )
    back_oth, back_own = back(place_at, terms[0], oth0, oth1, win)
    got_a1, got_b1, got_c1, back_own = lax.optimization_barrier(
        (got_a1, got_b1, got_c1, back_own)
    )
    grad_normed = (back_own + move(back_oth, CORE_PAIRS)).astype(BF)

    grp, dp = lax.axis_index("grp"), lax.axis_index("dp")
    own_first = ((dp >> 3) & 1) != ((grp >> 1) ^ (grp & (dp >> 2) & 1))

    rows = width // 2
    a = [second[1], got_a0]
    b = [first[3], got_b0], [second[3], got_b1]
    c = [early_c], [second[5], got_c1]
    to_b = sums([[(t, 0) for t in chunk] for chunk in b], rows, 1)
    got_b = move(to_b, Y1)
    to_c = jnp.where(own_first, total([after(second[5], to_b), got_c1]), early_c)
    got_c = move(to_c, X1)
    to_a = total([first[1], after(got_a1, to_c)])
    got_a = move(to_a, Z1)
    a = [settle(total(a)), got_a]
    b = [[(t, 4) for t in chunk] + [(got_b, 4 * k)] for k, chunk in enumerate(b)]
    c = [settle(jnp.where(own_first, total(c[0]), total(c[1]))), got_c]

    rows = width // 8
    to_b = sums(b, rows, 2)
    got_b = move(to_b, X0)
    b = [sums([[(t, at + 2) for t, at in chunk] for chunk in b], rows, 2), got_b]
    c[-1] = after(c[-1], to_b)
    to_c = total([t[:2] for t in c])
    got_c = move(to_c, Z0)
    c = [settle(total([t[2:] for t in c])), got_c]
    a[-1] = after(a[-1], to_c)
    to_a = total([t[:2] for t in a])
    got_a = move(to_a, Y0)
    kept, grad_normed = settle((total([t[2:] for t in a]), grad_normed))
    a = [kept, got_a]

    b[-1] = after(b[-1], to_a)
    to_b = sums([[(t, 0) for t in b]], rows, 2, 2)
    got_b = move(to_b, X1)
    b = [sums([[(t, 1) for t in b]], rows, 2, 2), got_b]
    c[-1] = after(c[-1], to_b)
    to_c = total([t[0] for t in c])
    got_c = move(to_c, Z1)
    c = [t[1] for t in c] + [got_c]
    a[-1] = after(a[-1], to_c)
    to_a = total([t[0] for t in a])
    got_a = move(to_a, Y1)
    a = [t[1] for t in a] + [got_a]

    rows = width // 16
    b[-1] = after(b[-1], to_a)
    to_b = sums([[(t, 2) for t in b]], rows, 2, -2)
    got_b = move(to_b, Z0)
    b = [sums([[(t, 1) for t in b]], rows, 2, 2)[0], got_b[0]]
    c[-1] = after(c[-1], to_b)
    to_c = total([t[:2] for t in c])
    got_c = move(to_c, Y0)
    c = [t[2:] for t in c] + [got_c]
    a[-1] = after(a[-1], to_c)
    to_a = total([t[:2] for t in a])
    got_a = move(to_a, X0)
    a = [t[2:] for t in a] + [got_a]

    b[-1] = after(b[-1], to_a)
    to_b = total([t[0] for t in b])
    got_b = move(to_b, Z1)
    c[-1] = after(c[-1], to_b)
    to_c = total([t[0] for t in c])
    got_c = move(to_c, Y1)
    a[-1] = after(a[-1], to_c)
    to_a = total([t[0] for t in a])
    got_a = move(to_a, X1)

    b = total([t[1] for t in b] + [got_b])
    c = total([t[1] for t in c] + [after(got_c, to_a)])
    c_far = move(c, FAR_PAIRS)
    a = total([t[1] for t in a] + [after(got_a, c)])
    both = jnp.concatenate([a, b], axis=1)
    (rows,) = small_call(
        functools.partial(gather_kernel, factor),
        [jax.ShapeDtypeStruct((5 * (dim // 32), dim), F32)],
        "gather",
        place_at,
        both,
        c,
        move(both, LOWER_PAIRS),
        move(both, UPPER_PAIRS),
        c_far,
    )
    grad_in, grad_out = small_call(
        last_kernel,
        [
            jax.ShapeDtypeStruct((width // 4, dim), F32),
            jax.ShapeDtypeStruct((dim // 32, 4 * width), F32),
        ],
        "last",
        place_at,
        rows,
        move(rows, CORE_PAIRS),
    )
    return (grad_in, grad_out, grad_normed)


def solution(mesh):
    placed = (P(AXES, None), P(), P(), P(AXES, None))
    return jax.shard_map(
        local,
        mesh=mesh,
        in_specs=placed,
        out_specs=(P("dp", None), P("dp", None), P(AXES, None)),
        check_vma=False,
    )
```

```python
import functools

import jax
import jax.numpy as jnp
import numpy as np
from jax import lax
from jax.experimental import pallas as pl
from jax.experimental.pallas import tpu as pltpu
from jax.sharding import PartitionSpec as P

AXES = ("grp", "dp")
BF = jnp.bfloat16
F32 = jnp.float32
OWN_LIMIT = 62 * 2**20
CHUNK_LIMIT = 62 * 2**20
BACK_LIMIT = 36 * 2**20
SMALL_LIMIT = 8 * 2**20


def place(x, y, z, c):
    return ((x // 2) * 2 + c) * 32 + z * 8 + (x % 2) * 4 + y


EVERY = [(x, y, z, c) for x in range(4) for y in range(4) for z in range(4) for c in range(2)]


def partner(i, core, step):
    return (i + (1 if i % 2 == (core + step) % 2 else -1)) % 4


def halving_pairs(axis, step):
    pairs = []
    for x, y, z, c in EVERY:
        at = [x, y, z]
        at[axis] = partner(at[axis], c, step)
        pairs.append((place(x, y, z, c), place(*at, c)))
    return pairs


X0, X1 = halving_pairs(0, 0), halving_pairs(0, 1)
Y0, Y1 = halving_pairs(1, 0), halving_pairs(1, 1)
Z0, Z1 = halving_pairs(2, 0), halving_pairs(2, 1)
CORE_PAIRS = [(place(x, y, z, c), place(x, y, z, 1 - c)) for x, y, z, c in EVERY]
FAR_PAIRS = [(place(x, y, z, c), place((x + 2) % 4, y, z, c)) for x, y, z, c in EVERY]


def owns(x, core):
    return x % 2 == core


def owner_pairs(shift):
    return [
        (place((x + shift) % 4, y, z, c), place(x, y, z, c)) for x, y, z, c in EVERY if owns(x, c)
    ]


def ring_order(i, core):
    first, second = partner(i, core, 0), partner(i, core, 1)
    return [partner(first, core, 1), first, second, i]


CORE, CHUNK, KIND, HALF, XAT, YAT, ZAT = 0, 1, 3, 7, 9, 13, 17
OWN_HALF, X, IS_OWNER, WIDTH = 22, 23, 24, 32


def table():
    rows = np.zeros((len(EVERY), WIDTH), np.int32)
    for x, y, z, c in EVERY:
        row = rows[place(x, y, z, c)]
        row[CORE] = c
        xs, ys, zs = ring_order(x, c), ring_order(y, c), ring_order(z, c)
        row[CHUNK], row[CHUNK + 1] = 1 - z % 2, z % 2
        row[KIND : KIND + 4] = [zs[1] // 2, zs[2] // 2, zs[0] // 2, zs[3] // 2]
        labels = {i: (i % 2, i // 2 if c == 0 else (i // 2) ^ (i % 2)) for i in range(4)}
        for k in range(2):
            (row[HALF + k],) = [labels[i][0] for i in xs[2:] if labels[i][1] == row[CHUNK + k]]
        for at, order in ((XAT, xs), (YAT, ys), (ZAT, zs)):
            for rank, i in enumerate(order):
                row[at + rank] = i
        row[OWN_HALF] = labels[x][1]
        row[X] = x
        row[IS_OWNER] = int(owns(x, c))
    return rows


TWO_BITS = [*range(XAT, ZAT + 4), X]
FIELDS = {at: (0, 2 * i, 3) for i, at in enumerate(TWO_BITS)}
ONE_BIT = [CORE, CHUNK, CHUNK + 1, *range(KIND, KIND + 4), HALF, HALF + 1, OWN_HALF, IS_OWNER]
FIELDS.update({at: (1, i, 1) for i, at in enumerate(ONE_BIT)})


def packed():
    rows = table()
    words = np.zeros((len(EVERY), 2), np.int32)
    for at, (word, shift, _) in FIELDS.items():
        words[:, word] |= rows[:, at] << shift
    return words


TABLE = packed()


def field(index, table, at):
    word, shift, mask = FIELDS[at]
    return (table[index[0] * 2 + word] >> shift) & mask


NT = (((1,), (1,)), ((), ()))
TN = (((0,), (0,)), ((), ()))


def row_of(index, table):
    class Row:
        def __getitem__(self, at):
            return field(index, table, at)

    return Row()


def gated(value, gate, dact):
    cdf = 0.5 * (1.0 + lax.erf(gate * (2.0 ** -0.5)))
    density = jnp.exp(-0.5 * gate * gate) * ((2.0 * jnp.pi) ** -0.5)
    share = gate * cdf
    return (
        (value * share).astype(BF),
        (dact * share).astype(BF),
        (dact * value * (cdf + gate * density)).astype(BF),
    )


class Copies:
    def __init__(self, sems):
        self.sems, self.used = sems, 0

    def start(self, source, target):
        copy = pltpu.make_async_copy(source, target, self.sems.at[self.used])
        self.used += 1
        copy.start()
        return copy


def own_kernel(index, table, win, wout, n_in, c_in, d_out, act_out, w, wo, n, c, d, act, sems):
    tab = row_of(index, table)
    width = w.shape[2]
    copies = Copies(sems)
    load_w, load_wo = [], []
    for k in range(2):
        block, core = tab[CHUNK + k], tab[CORE]
        column = pl.multiple_of((block * 2 + core) * width, 128)
        load_wo.append(copies.start(wout.at[:, pl.ds(column, width)], wo.at[k]))
        if k == 0:
            load_c = copies.start(c_in, c)
        load_w.append([copies.start(win.at[i, block, core], w.at[k, i]) for i in range(2)])
        if k == 0:
            load_n = copies.start(n_in, n)
    stores = []
    for k in range(2):
        load_wo[k].wait()
        if k == 0:
            load_c.wait()
        dact = jnp.dot(c[...], wo[k], preferred_element_type=F32)
        for copy in load_w[k]:
            copy.wait()
        if k == 0:
            load_n.wait()
        proj = lax.dot_general(
            n[...], w[k].reshape(2 * width, w.shape[3]), NT, preferred_element_type=F32
        )
        act[k], d[k, 0], d[k, 1] = gated(proj[:, :width], proj[:, width:], dact)
        stores.append(copies.start(act.at[k], act_out.at[k]))
        stores.append(copies.start(d.at[k], d_out.at[k]))
    for copy in stores:
        copy.wait()


def own_call(place_at, win, wout, normed, cot):
    count, dim = normed.shape
    width = win.shape[3]
    anywhere = pl.BlockSpec(memory_space=pl.ANY)
    return pl.pallas_call(
        own_kernel,
        grid_spec=pltpu.PrefetchScalarGridSpec(
            num_scalar_prefetch=2,
            grid=(1,),
            in_specs=[anywhere] * 4,
            out_specs=[anywhere] * 2,
            scratch_shapes=[
                pltpu.VMEM((2, 2, width, dim), BF),
                pltpu.VMEM((2, dim, width), BF),
                pltpu.VMEM((count, dim), BF),
                pltpu.VMEM((count, dim), BF),
                pltpu.VMEM((2, 2, count, width), BF),
                pltpu.VMEM((2, count, width), BF),
                pltpu.SemaphoreType.DMA((12,)),
            ],
        ),
        out_shape=[
            jax.ShapeDtypeStruct((2, 2, count, width), BF),
            jax.ShapeDtypeStruct((2, count, width), BF),
        ],
        compiler_params=pltpu.CompilerParams(vmem_limit_bytes=OWN_LIMIT),
        cost_estimate=pl.CostEstimate(
            flops=12 * count * dim * width, bytes_accessed=16 * 2**20, transcendentals=0
        ),
        name="own_terms",
    )(*place_at, win, wout, normed, cot)


def chunk_kernel(
    chunk, index, table, win, wout, n_in, c_in, n_own, c_own, d_own, act_own,
    a_send, a_keep, b_send, b_keep, c_send, c_keep, d_out,
    w, wo, nb, cb, d, act, gin, gout, load_sems, sems,
):
    tab = row_of(index, table)
    width, dim = w.shape[1:]
    count = n_in.shape[0]
    half = dim // 2
    core, block = tab[CORE], tab[CHUNK + chunk]
    own, oth = pl.ds(count, count), pl.ds(0, count)
    loads = Copies(load_sems)
    column = pl.multiple_of((block * 2 + core) * width, 128)
    load_wo = loads.start(wout.at[:, pl.ds(column, width)], wo)
    lanes = [pl.ds(part * half, half) for part in range(2)]
    raw = gin.at[:, :, oth]
    load_c = [loads.start(c_in.at[:, lanes[i]], raw.at[0, i]) for i in range(2)]
    load_w = [loads.start(win.at[i, block, core], w.at[i]) for i in range(2)]
    load_n = [loads.start(n_in.at[:, lanes[i]], raw.at[1, i]) for i in range(2)]
    load_own = [loads.start(c_own, cb.at[own]), loads.start(act_own.at[chunk], act.at[own])]
    load_own += [loads.start(d_own.at[chunk, i], d.at[i, own]) for i in range(2)]
    load_own += [loads.start(n_own, nb.at[own])]

    def store(source, target, sem):
        pltpu.make_async_copy(source, target, sems.at[sem]).start()

    load_wo.wait()
    for i in range(2):
        load_c[i].wait()
        cb[oth, i * half : (i + 1) * half] = raw[0, i].astype(BF)
    dact = jnp.dot(cb[oth], wo[...], preferred_element_type=F32)
    for i in range(2):
        load_n[i].wait()
        nb[oth, i * half : (i + 1) * half] = raw[1, i].astype(BF)
    for copy in load_w:
        copy.wait()
    proj = lax.dot_general(
        nb[oth], w[...].reshape(2 * width, dim), NT, preferred_element_type=F32
    )
    act[oth], d[0, oth], d[1, oth] = gated(proj[:, :width], proj[:, width:], dact)
    for i in range(2):
        store(d.at[i, oth], d_out.at[i], 0)
    for copy in load_own:
        copy.wait()

    gout[...] = lax.dot_general(cb[...], act[...], TN, preferred_element_type=F32)
    tiny = dim // 32
    kept = tab[HALF + chunk]
    for out, x, sem in ((c_send, 1 - kept, 1), (c_keep, kept, 2)):
        for z in range(4):
            for y in range(4):
                at = ((tab[ZAT + z] * 2 + x) * 4 + tab[YAT + y]) * tiny
                store(gout.at[pl.ds(pl.multiple_of(at, 8), tiny)], out.at[z, y], sem)
    small = width // 16
    for slot, out in enumerate((a_send, a_keep)):
        kind = tab[KIND + 2 * chunk + slot]
        for part in range(2):
            cut = slice(part * half, (part + 1) * half)
            gin[slot, part] = lax.dot_general(
                d[kind], nb[:, cut], TN, preferred_element_type=F32
            )
            for y in range(4):
                for x in range(4):
                    at = (tab[YAT + y] * 4 + tab[XAT + x]) * small
                    rows = gin.at[slot, part, pl.ds(pl.multiple_of(at, 8), small)]
                    if part == 0:
                        store(rows, out.at[y, x], 3 + slot)
                    else:
                        store(rows, (b_send, b_keep)[y // 2].at[y % 2, x, slot], 5 + y // 2)
    outs = (d_out, c_send, c_keep, a_send, a_keep, b_send, b_keep)
    for i, out in enumerate(outs):
        pltpu.make_async_copy(out, out, sems.at[i]).wait()


def chunk_call(place_at, win, wout, other, own, terms, chunk):
    count, dim = own[0].shape
    width = win.shape[3]
    a = jax.ShapeDtypeStruct((4, 4, width // 16, dim // 2), F32)
    b = jax.ShapeDtypeStruct((2, 4, 2, width // 16, dim // 2), F32)
    c = jax.ShapeDtypeStruct((4, 4, dim // 32, width), F32)
    outs = [a, a, b, b, c, c, jax.ShapeDtypeStruct((2, count, width), BF)]
    operands = [win, wout, *other, *own, *terms]
    anywhere = pl.BlockSpec(memory_space=pl.ANY)
    return pl.pallas_call(
        functools.partial(chunk_kernel, chunk),
        grid_spec=pltpu.PrefetchScalarGridSpec(
            num_scalar_prefetch=2,
            grid=(1,),
            in_specs=[anywhere] * len(operands),
            out_specs=[anywhere] * len(outs),
            scratch_shapes=[
                pltpu.VMEM((2, width, dim), BF),
                pltpu.VMEM((dim, width), BF),
                pltpu.VMEM((2 * count, dim), BF),
                pltpu.VMEM((2 * count, dim), BF),
                pltpu.VMEM((2, 2 * count, width), BF),
                pltpu.VMEM((2 * count, width), BF),
                pltpu.VMEM((2, 2, width, dim // 2), F32),
                pltpu.VMEM((dim, width), F32),
                pltpu.SemaphoreType.DMA((12,)),
                pltpu.SemaphoreType.DMA((7,)),
            ],
        ),
        out_shape=outs,
        compiler_params=pltpu.CompilerParams(vmem_limit_bytes=CHUNK_LIMIT),
        cost_estimate=pl.CostEstimate(
            flops=16 * count * dim * width, bytes_accessed=16 * 2**20, transcendentals=0
        ),
        name="chunk",
    )(*place_at, *operands)


def back_kernel(index, table, own_ref, oth0_ref, oth1_ref, w_ref, oth_out, own_out):
    tab = row_of(index, table)
    w = w_ref[...].reshape(2 * w_ref.shape[1], w_ref.shape[2])
    straight = tab[CHUNK] == 0
    for d0, d1, out in (
        (oth0_ref[...], oth1_ref[...], oth_out),
        (own_ref[0], own_ref[1], own_out),
    ):
        low = jnp.where(straight, d0, d1)
        high = jnp.where(straight, d1, d0)
        part = jnp.dot(jnp.concatenate([low, high], axis=1), w, preferred_element_type=F32)

        @pl.when(pl.program_id(0) == 0)
        def _():
            out[...] = part

        @pl.when(pl.program_id(0) == 1)
        def _():
            out[...] += part


def back(place_at, own, oth0, oth1, win):
    _, count, width = oth0.shape
    dim = win.shape[4]
    whole = pl.BlockSpec((count, dim), lambda k, i, t: (0, 0))
    d_spec = pl.BlockSpec((None, count, width), lambda k, i, t: (k, 0, 0))
    return pl.pallas_call(
        back_kernel,
        grid_spec=pltpu.PrefetchScalarGridSpec(
            num_scalar_prefetch=2,
            grid=(2,),
            in_specs=[
                pl.BlockSpec((2, None, count, width), lambda k, i, t: (0, k, 0, 0)),
                d_spec,
                d_spec,
                pl.BlockSpec(
                    (None, 2, None, width, dim),
                    lambda k, i, t: (k, 0, field(i, t, CORE), 0, 0),
                ),
            ],
            out_specs=[whole, whole],
        ),
        out_shape=[jax.ShapeDtypeStruct((count, dim), F32)] * 2,
        compiler_params=pltpu.CompilerParams(vmem_limit_bytes=BACK_LIMIT),
        cost_estimate=pl.CostEstimate(
            flops=16 * count * dim * width, bytes_accessed=16 * 2**20, transcendentals=0
        ),
        name="back",
    )(*place_at, own, oth0, oth1, win)


def small_call(kernel, out_shape, name, place_at, *operands):
    return pl.pallas_call(
        kernel,
        grid_spec=pltpu.PrefetchScalarGridSpec(
            num_scalar_prefetch=2,
            grid=(1,),
            in_specs=[
                pl.BlockSpec(o.shape, functools.partial(lambda n, *_: (0,) * n, o.ndim))
                for o in operands
            ],
            out_specs=[
                pl.BlockSpec(o.shape, functools.partial(lambda n, *_: (0,) * n, len(o.shape)))
                for o in out_shape
            ],
        ),
        out_shape=out_shape,
        compiler_params=pltpu.CompilerParams(vmem_limit_bytes=SMALL_LIMIT),
        cost_estimate=pl.CostEstimate(flops=2**20, bytes_accessed=2**20, transcendentals=0),
        name=name,
    )(*place_at, *operands)


def sums_kernel(sizes, *refs):
    out = refs[-1]
    at = 0
    for i, size in enumerate(sizes):
        out[i, 0] = functools.reduce(lambda p, q: p + q, [r[0] for r in refs[at : at + size]])
        at += size


def sums(groups, rows, count, stride=1):
    lanes = groups[0][0][0].shape[-1]
    tile = min(rows, 160)
    operands, specs = [], []
    for group in groups:
        for array, first in group:
            operands.append(array.reshape(-1, rows, lanes))
            specs.append(
                pl.BlockSpec((1, tile, lanes), functools.partial(lambda f, i, j: (f + i * stride, j, 0), first))
            )
    return pl.pallas_call(
        functools.partial(sums_kernel, [len(group) for group in groups]),
        grid=(count, rows // tile),
        in_specs=specs,
        out_specs=pl.BlockSpec((len(groups), 1, tile, lanes), lambda i, j: (0, i, j, 0)),
        out_shape=jax.ShapeDtypeStruct((len(groups), count, rows, lanes), F32),
        compiler_params=pltpu.CompilerParams(vmem_limit_bytes=SMALL_LIMIT),
        cost_estimate=pl.CostEstimate(
            flops=2**20, bytes_accessed=4 * 2**20, transcendentals=0
        ),
        name="sums",
    )(*operands)


def gather_kernel(factor, index, table, *refs):
    tab = row_of(index, table)
    *both_refs, c_ref, far_ref, out = refs
    rows, half = c_ref.shape
    for i, ref in enumerate(both_refs):
        here = pl.ds(pl.multiple_of(lax.rem(tab[X] + i, 4) * rows, 8), rows)
        out[here] = ref[...] * factor
    low = tab[OWN_HALF] == 0
    c, far = c_ref[...] * factor, far_ref[...] * factor
    out[4 * rows :, :half] = jnp.where(low, c, far)
    out[4 * rows :, half:] = jnp.where(low, far, c)


def last_kernel(index, table, own_ref, oth_ref, in_ref, out_ref):
    tab = row_of(index, table)
    count, half = in_ref.shape[0], in_ref.shape[1] // 2
    owner, zero = tab[IS_OWNER] == 1, tab[CORE] == 0
    in_ref[...] = jnp.where(owner, own_ref[:count], oth_ref[:count])
    own, oth = own_ref[count:], oth_ref[count:]
    for i in range(2):
        cut = slice(i * half, (i + 1) * half)
        out_ref[:, 2 * i * half : (2 * i + 1) * half] = jnp.where(zero, own[:, cut], oth[:, cut])
        out_ref[:, (2 * i + 1) * half : (2 * i + 2) * half] = jnp.where(
            zero, oth[:, cut], own[:, cut]
        )


def widen_kernel(n_ref, c_ref, n_out, c_out):
    n_out[...] = n_ref[...].astype(F32)
    c_out[...] = c_ref[...].astype(F32)


def widen(normed, cot):
    count, dim = normed.shape
    tile = pl.BlockSpec((count // 4, dim), lambda i: (i, 0))
    return pl.pallas_call(
        widen_kernel,
        grid=(4,),
        in_specs=[tile, tile],
        out_specs=[tile, tile],
        out_shape=[jax.ShapeDtypeStruct((count, dim), F32)] * 2,
        compiler_params=pltpu.CompilerParams(vmem_limit_bytes=OWN_LIMIT),
        cost_estimate=pl.CostEstimate(flops=2**20, bytes_accessed=8 * 2**20, transcendentals=0),
        name="widen",
    )(normed, cot)


def move(array, pairs):
    return lax.ppermute(array, AXES, pairs)


def total(terms):
    return functools.reduce(lambda p, q: p + q, terms)


def settle(array):
    return lax.optimization_barrier(array)


def after(array, other):
    return lax.optimization_barrier((array, other))[0]


def local(normed, w_in, w_out, cotangent):
    dim = normed.shape[1]
    width = w_out.shape[1] // 4
    factor = (normed.shape[0] * lax.axis_size("dp") * lax.axis_size("grp")) ** (-0.5)
    index = lax.axis_index(AXES).reshape(1)
    place_at = index, jnp.asarray(TABLE.reshape(-1))
    win = w_in.reshape(2, 2, 2, width, dim)

    wide = widen(normed, cotangent)
    own = normed, cotangent
    other = move(wide[0], CORE_PAIRS), move(wide[1], CORE_PAIRS)
    terms = own_call(place_at, win, w_out, normed, cotangent)
    *first, oth0 = chunk_call(place_at, win, w_out, other, own, terms, 0)
    got_a0, got_b0, got_c0 = move(first[0], Z0), move(first[2], Y0), move(first[4], X0)
    index, _ = lax.optimization_barrier((index, first[0]))
    place_at = index, place_at[1]
    *second, oth1 = chunk_call(place_at, win, w_out, other, own, terms, 1)
    got_a1, got_b1, got_c1 = move(second[0], Z0), move(second[2], Y0), move(second[4], X0)

    oth0, index, got_a0, got_b0, early_c = lax.optimization_barrier(
        (oth0, index, got_a0, got_b0, first[5] + got_c0)
    )
    back_oth, back_own = back(place_at, terms[0], oth0, oth1, win)
    got_b1, back_own = lax.optimization_barrier((got_b1, back_own))
    grad_normed = (back_own + move(back_oth, CORE_PAIRS)).astype(BF)

    grp, dp = lax.axis_index("grp"), lax.axis_index("dp")
    own_first = ((dp >> 3) & 1) != ((grp >> 1) ^ (grp & (dp >> 2) & 1))

    rows = width // 2
    a = [second[1], got_a0]
    b = [first[3], got_b0], [second[3], got_b1]
    c = [early_c], [second[5], got_c1]
    to_b = sums([[(t, 0) for t in chunk] for chunk in b], rows, 1)
    got_b = move(to_b, Y1)
    c[1][1] = got_c1 = after(got_c1, to_b)
    to_c = jnp.where(own_first, total([second[5], got_c1]), early_c)
    got_c = move(to_c, X1)
    to_a = total([first[1], after(got_a1, to_c)])
    got_a = move(to_a, Z1)
    a = [settle(total(a)), got_a]
    b = [[(t, 4) for t in chunk] + [(got_b, 4 * k)] for k, chunk in enumerate(b)]
    c = [settle(jnp.where(own_first, total(c[0]), total(c[1]))), got_c]

    rows = width // 8
    to_b = sums(b, rows, 2)
    got_b = move(to_b, X0)
    b = [sums([[(t, at + 2) for t, at in chunk] for chunk in b], rows, 2), got_b]
    c[-1] = after(c[-1], to_b)
    to_c = total([t[:2] for t in c])
    got_c = move(to_c, Z0)
    c = [settle(total([t[2:] for t in c])), got_c]
    a[-1] = after(a[-1], to_c)
    to_a = total([t[:2] for t in a])
    got_a = move(to_a, Y0)
    kept, grad_normed = settle((total([t[2:] for t in a]), grad_normed))
    a = [kept, got_a]

    b[-1] = after(b[-1], to_a)
    to_b = sums([[(t, 0) for t in b]], rows, 2, 2)
    got_b = move(to_b, X1)
    b = [sums([[(t, 1) for t in b]], rows, 2, 2), got_b]
    c[-1] = after(c[-1], to_b)
    to_c = total([t[0] for t in c])
    got_c = move(to_c, Z1)
    c = [t[1] for t in c] + [got_c]
    a[-1] = after(a[-1], to_c)
    to_a = total([t[0] for t in a])
    got_a = move(to_a, Y1)
    a = [t[1] for t in a] + [got_a]

    rows = width // 16
    b[-1] = after(b[-1], to_a)
    to_b = sums([[(t, 2) for t in b]], rows, 2, -2)
    got_b = move(to_b, Z0)
    b = [sums([[(t, 1) for t in b]], rows, 2, 2)[0], got_b[0]]
    c[-1] = after(c[-1], to_b)
    to_c = total([t[:2] for t in c])
    got_c = move(to_c, Y0)
    c = [t[2:] for t in c] + [got_c]
    a[-1] = after(a[-1], to_c)
    to_a = total([t[:2] for t in a])
    got_a = move(to_a, X0)
    a = [t[2:] for t in a] + [got_a]

    b[-1] = after(b[-1], to_a)
    to_b = total([t[0] for t in b])
    got_b = move(to_b, Z1)
    c[-1] = after(c[-1], to_b)
    to_c = total([t[0] for t in c])
    got_c = move(to_c, Y1)
    a[-1] = after(a[-1], to_c)
    to_a = total([t[0] for t in a])
    got_a = move(to_a, X1)

    b = total([t[1] for t in b] + [got_b])
    c = total([t[1] for t in c] + [after(got_c, to_a)])
    c_far = move(c, FAR_PAIRS)
    a = total([t[1] for t in a] + [after(got_a, c_far)])
    both = jnp.concatenate([a, b], axis=1)
    (rows,) = small_call(
        functools.partial(gather_kernel, factor),
        [jax.ShapeDtypeStruct((5 * (dim // 32), dim), F32)],
        "gather",
        place_at,
        both,
        *(move(both, owner_pairs(shift)) for shift in (1, 2, 3)),
        c,
        c_far,
    )
    grad_in, grad_out = small_call(
        last_kernel,
        [
            jax.ShapeDtypeStruct((width // 4, dim), F32),
            jax.ShapeDtypeStruct((dim // 32, 4 * width), F32),
        ],
        "last",
        place_at,
        rows,
        move(rows, CORE_PAIRS),
    )
    return (grad_in, grad_out, grad_normed)


def solution(mesh):
    placed = (P(AXES, None), P(), P(), P(AXES, None))
    return jax.shard_map(
        local,
        mesh=mesh,
        in_specs=placed,
        out_specs=(P("dp", None), P("dp", None), P(AXES, None)),
        check_vma=False,
    )
```

```python
import functools

import jax
import jax.numpy as jnp
import numpy as np
from jax import lax
from jax.experimental import pallas as pl
from jax.experimental.pallas import tpu as pltpu
from jax.sharding import PartitionSpec as P

AXES = ("grp", "dp")
BF = jnp.bfloat16
F32 = jnp.float32
OWN_LIMIT = 62 * 2**20
CHUNK_LIMIT = 62 * 2**20
BACK_LIMIT = 36 * 2**20
SMALL_LIMIT = 8 * 2**20


def place(x, y, z, c):
    return ((x // 2) * 2 + c) * 32 + z * 8 + (x % 2) * 4 + y


EVERY = [(x, y, z, c) for x in range(4) for y in range(4) for z in range(4) for c in range(2)]


def partner(i, core, step):
    return (i + (1 if i % 2 == (core + step) % 2 else -1)) % 4


def halving_pairs(axis, step):
    pairs = []
    for x, y, z, c in EVERY:
        at = [x, y, z]
        at[axis] = partner(at[axis], c, step)
        pairs.append((place(x, y, z, c), place(*at, c)))
    return pairs


X0, X1 = halving_pairs(0, 0), halving_pairs(0, 1)
Y0, Y1 = halving_pairs(1, 0), halving_pairs(1, 1)
Z0, Z1 = halving_pairs(2, 0), halving_pairs(2, 1)
CORE_PAIRS = [(place(x, y, z, c), place(x, y, z, 1 - c)) for x, y, z, c in EVERY]
FAR_PAIRS = [(place(x, y, z, c), place((x + 2) % 4, y, z, c)) for x, y, z, c in EVERY]


def owns(x, core):
    return x % 2 == core


def owner_pairs(shift):
    return [
        (place((x + shift) % 4, y, z, c), place(x, y, z, c)) for x, y, z, c in EVERY if owns(x, c)
    ]


def ring_order(i, core):
    first, second = partner(i, core, 0), partner(i, core, 1)
    return [partner(first, core, 1), first, second, i]


CORE, CHUNK, KIND, HALF, XAT, YAT, ZAT = 0, 1, 3, 7, 9, 13, 17
OWN_HALF, X, IS_OWNER, WIDTH = 22, 23, 24, 32


def table():
    rows = np.zeros((len(EVERY), WIDTH), np.int32)
    for x, y, z, c in EVERY:
        row = rows[place(x, y, z, c)]
        row[CORE] = c
        xs, ys, zs = ring_order(x, c), ring_order(y, c), ring_order(z, c)
        row[CHUNK], row[CHUNK + 1] = 1 - z % 2, z % 2
        row[KIND : KIND + 4] = [zs[1] // 2, zs[2] // 2, zs[0] // 2, zs[3] // 2]
        labels = {i: (i % 2, i // 2 if c == 0 else (i // 2) ^ (i % 2)) for i in range(4)}
        for k in range(2):
            (row[HALF + k],) = [labels[i][0] for i in xs[2:] if labels[i][1] == row[CHUNK + k]]
        for at, order in ((XAT, xs), (YAT, ys), (ZAT, zs)):
            for rank, i in enumerate(order):
                row[at + rank] = i
        row[OWN_HALF] = labels[x][1]
        row[X] = x
        row[IS_OWNER] = int(owns(x, c))
    return rows


TWO_BITS = [*range(XAT, ZAT + 4), X]
FIELDS = {at: (0, 2 * i, 3) for i, at in enumerate(TWO_BITS)}
ONE_BIT = [CORE, CHUNK, CHUNK + 1, *range(KIND, KIND + 4), HALF, HALF + 1, OWN_HALF, IS_OWNER]
FIELDS.update({at: (1, i, 1) for i, at in enumerate(ONE_BIT)})


def packed():
    rows = table()
    words = np.zeros((len(EVERY), 2), np.int32)
    for at, (word, shift, _) in FIELDS.items():
        words[:, word] |= rows[:, at] << shift
    return words


TABLE = packed()


def field(index, table, at):
    word, shift, mask = FIELDS[at]
    return (table[index[0] * 2 + word] >> shift) & mask


NT = (((1,), (1,)), ((), ()))
TN = (((0,), (0,)), ((), ()))


def row_of(index, table):
    class Row:
        def __getitem__(self, at):
            return field(index, table, at)

    return Row()


def gated(value, gate, dact):
    cdf = 0.5 * (1.0 + lax.erf(gate * (2.0 ** -0.5)))
    density = jnp.exp(-0.5 * gate * gate) * ((2.0 * jnp.pi) ** -0.5)
    share = gate * cdf
    return (
        (value * share).astype(BF),
        (dact * share).astype(BF),
        (dact * value * (cdf + gate * density)).astype(BF),
    )


class Copies:
    def __init__(self, sems):
        self.sems, self.used = sems, 0

    def start(self, source, target):
        copy = pltpu.make_async_copy(source, target, self.sems.at[self.used])
        self.used += 1
        copy.start()
        return copy


def own_kernel(index, table, win, wout, n_in, c_in, d_out, act_out, w, wo, n, c, d, act, sems):
    tab = row_of(index, table)
    width = w.shape[2]
    copies = Copies(sems)
    load_w, load_wo = [], []
    for k in range(2):
        block, core = tab[CHUNK + k], tab[CORE]
        column = pl.multiple_of((block * 2 + core) * width, 128)
        load_wo.append(copies.start(wout.at[:, pl.ds(column, width)], wo.at[k]))
        if k == 0:
            load_c = copies.start(c_in, c)
        load_w.append([copies.start(win.at[i, block, core], w.at[k, i]) for i in range(2)])
        if k == 0:
            load_n = copies.start(n_in, n)
    stores = []
    for k in range(2):
        load_wo[k].wait()
        if k == 0:
            load_c.wait()
        dact = jnp.dot(c[...], wo[k], preferred_element_type=F32)
        for copy in load_w[k]:
            copy.wait()
        if k == 0:
            load_n.wait()
        proj = lax.dot_general(
            n[...], w[k].reshape(2 * width, w.shape[3]), NT, preferred_element_type=F32
        )
        act[k], d[k, 0], d[k, 1] = gated(proj[:, :width], proj[:, width:], dact)
        stores.append(copies.start(act.at[k], act_out.at[k]))
        stores.append(copies.start(d.at[k], d_out.at[k]))
    for copy in stores:
        copy.wait()


def own_call(place_at, win, wout, normed, cot):
    count, dim = normed.shape
    width = win.shape[3]
    anywhere = pl.BlockSpec(memory_space=pl.ANY)
    return pl.pallas_call(
        own_kernel,
        grid_spec=pltpu.PrefetchScalarGridSpec(
            num_scalar_prefetch=2,
            grid=(1,),
            in_specs=[anywhere] * 4,
            out_specs=[anywhere] * 2,
            scratch_shapes=[
                pltpu.VMEM((2, 2, width, dim), BF),
                pltpu.VMEM((2, dim, width), BF),
                pltpu.VMEM((count, dim), BF),
                pltpu.VMEM((count, dim), BF),
                pltpu.VMEM((2, 2, count, width), BF),
                pltpu.VMEM((2, count, width), BF),
                pltpu.SemaphoreType.DMA((12,)),
            ],
        ),
        out_shape=[
            jax.ShapeDtypeStruct((2, 2, count, width), BF),
            jax.ShapeDtypeStruct((2, count, width), BF),
        ],
        compiler_params=pltpu.CompilerParams(vmem_limit_bytes=OWN_LIMIT),
        cost_estimate=pl.CostEstimate(
            flops=12 * count * dim * width, bytes_accessed=16 * 2**20, transcendentals=0
        ),
        name="own_terms",
    )(*place_at, win, wout, normed, cot)


def chunk_kernel(
    chunk, index, table, win, wout, n_in, c_in, n_own, c_own, d_own, act_own,
    a_send, a_keep, b_send, b_keep, c_send, c_keep, d_out,
    w, wo, nb, cb, d, act, gin, gout, load_sems, sems,
):
    tab = row_of(index, table)
    width, dim = w.shape[1:]
    count = n_in.shape[0]
    half = dim // 2
    core, block = tab[CORE], tab[CHUNK + chunk]
    own, oth = pl.ds(count, count), pl.ds(0, count)
    loads = Copies(load_sems)
    column = pl.multiple_of((block * 2 + core) * width, 128)
    load_wo = loads.start(wout.at[:, pl.ds(column, width)], wo)
    lanes = [pl.ds(part * half, half) for part in range(2)]
    raw = gin.at[:, :, oth]
    load_c = [loads.start(c_in.at[:, lanes[i]], raw.at[0, i]) for i in range(2)]
    load_w = [loads.start(win.at[i, block, core], w.at[i]) for i in range(2)]
    load_n = [loads.start(n_in.at[:, lanes[i]], raw.at[1, i]) for i in range(2)]
    load_own = [loads.start(c_own, cb.at[own]), loads.start(act_own.at[chunk], act.at[own])]
    load_own += [loads.start(d_own.at[chunk, i], d.at[i, own]) for i in range(2)]
    load_own += [loads.start(n_own, nb.at[own])]

    def store(source, target, sem):
        pltpu.make_async_copy(source, target, sems.at[sem]).start()

    load_wo.wait()
    for i in range(2):
        load_c[i].wait()
        cb[oth, i * half : (i + 1) * half] = raw[0, i].astype(BF)
    dact = jnp.dot(cb[oth], wo[...], preferred_element_type=F32)
    for i in range(2):
        load_n[i].wait()
        nb[oth, i * half : (i + 1) * half] = raw[1, i].astype(BF)
    for copy in load_w:
        copy.wait()
    proj = lax.dot_general(
        nb[oth], w[...].reshape(2 * width, dim), NT, preferred_element_type=F32
    )
    act[oth], d[0, oth], d[1, oth] = gated(proj[:, :width], proj[:, width:], dact)
    for i in range(2):
        store(d.at[i, oth], d_out.at[i], 0)
    for copy in load_own:
        copy.wait()

    gout[...] = lax.dot_general(cb[...], act[...], TN, preferred_element_type=F32)
    tiny = dim // 32
    kept = tab[HALF + chunk]
    for out, x, sem in ((c_send, 1 - kept, 1), (c_keep, kept, 2)):
        for z in range(4):
            for y in range(4):
                at = ((tab[ZAT + z] * 2 + x) * 4 + tab[YAT + y]) * tiny
                store(gout.at[pl.ds(pl.multiple_of(at, 8), tiny)], out.at[z, y], sem)
    small = width // 16
    for slot, out in enumerate((a_send, a_keep)):
        kind = tab[KIND + 2 * chunk + slot]
        for part in range(2):
            cut = slice(part * half, (part + 1) * half)
            gin[slot, part] = lax.dot_general(
                d[kind], nb[:, cut], TN, preferred_element_type=F32
            )
            for y in range(4):
                for x in range(4):
                    at = (tab[YAT + y] * 4 + tab[XAT + x]) * small
                    rows = gin.at[slot, part, pl.ds(pl.multiple_of(at, 8), small)]
                    if part == 0:
                        store(rows, out.at[y, x], 3 + slot)
                    else:
                        store(rows, (b_send, b_keep)[y // 2].at[y % 2, x, slot], 5 + y // 2)
    outs = (d_out, c_send, c_keep, a_send, a_keep, b_send, b_keep)
    for i, out in enumerate(outs):
        pltpu.make_async_copy(out, out, sems.at[i]).wait()


def chunk_call(place_at, win, wout, other, own, terms, chunk):
    count, dim = own[0].shape
    width = win.shape[3]
    a = jax.ShapeDtypeStruct((4, 4, width // 16, dim // 2), F32)
    b = jax.ShapeDtypeStruct((2, 4, 2, width // 16, dim // 2), F32)
    c = jax.ShapeDtypeStruct((4, 4, dim // 32, width), F32)
    outs = [a, a, b, b, c, c, jax.ShapeDtypeStruct((2, count, width), BF)]
    operands = [win, wout, *other, *own, *terms]
    anywhere = pl.BlockSpec(memory_space=pl.ANY)
    return pl.pallas_call(
        functools.partial(chunk_kernel, chunk),
        grid_spec=pltpu.PrefetchScalarGridSpec(
            num_scalar_prefetch=2,
            grid=(1,),
            in_specs=[anywhere] * len(operands),
            out_specs=[anywhere] * len(outs),
            scratch_shapes=[
                pltpu.VMEM((2, width, dim), BF),
                pltpu.VMEM((dim, width), BF),
                pltpu.VMEM((2 * count, dim), BF),
                pltpu.VMEM((2 * count, dim), BF),
                pltpu.VMEM((2, 2 * count, width), BF),
                pltpu.VMEM((2 * count, width), BF),
                pltpu.VMEM((2, 2, width, dim // 2), F32),
                pltpu.VMEM((dim, width), F32),
                pltpu.SemaphoreType.DMA((12,)),
                pltpu.SemaphoreType.DMA((7,)),
            ],
        ),
        out_shape=outs,
        compiler_params=pltpu.CompilerParams(vmem_limit_bytes=CHUNK_LIMIT),
        cost_estimate=pl.CostEstimate(
            flops=16 * count * dim * width, bytes_accessed=16 * 2**20, transcendentals=0
        ),
        name="chunk",
    )(*place_at, *operands)


def back_kernel(index, table, own_ref, oth0_ref, oth1_ref, w_ref, oth_out, own_out):
    tab = row_of(index, table)
    w = w_ref[...].reshape(2 * w_ref.shape[1], w_ref.shape[2])
    straight = tab[CHUNK] == 0
    for d0, d1, out in (
        (oth0_ref[...], oth1_ref[...], oth_out),
        (own_ref[0], own_ref[1], own_out),
    ):
        low = jnp.where(straight, d0, d1)
        high = jnp.where(straight, d1, d0)
        part = jnp.dot(jnp.concatenate([low, high], axis=1), w, preferred_element_type=F32)

        @pl.when(pl.program_id(0) == 0)
        def _():
            out[...] = part

        @pl.when(pl.program_id(0) == 1)
        def _():
            out[...] += part


def back(place_at, own, oth0, oth1, win):
    _, count, width = oth0.shape
    dim = win.shape[4]
    whole = pl.BlockSpec((count, dim), lambda k, i, t: (0, 0))
    d_spec = pl.BlockSpec((None, count, width), lambda k, i, t: (k, 0, 0))
    return pl.pallas_call(
        back_kernel,
        grid_spec=pltpu.PrefetchScalarGridSpec(
            num_scalar_prefetch=2,
            grid=(2,),
            in_specs=[
                pl.BlockSpec((2, None, count, width), lambda k, i, t: (0, k, 0, 0)),
                d_spec,
                d_spec,
                pl.BlockSpec(
                    (None, 2, None, width, dim),
                    lambda k, i, t: (k, 0, field(i, t, CORE), 0, 0),
                ),
            ],
            out_specs=[whole, whole],
        ),
        out_shape=[jax.ShapeDtypeStruct((count, dim), F32)] * 2,
        compiler_params=pltpu.CompilerParams(vmem_limit_bytes=BACK_LIMIT),
        cost_estimate=pl.CostEstimate(
            flops=16 * count * dim * width, bytes_accessed=16 * 2**20, transcendentals=0
        ),
        name="back",
    )(*place_at, own, oth0, oth1, win)


def small_call(kernel, out_shape, name, place_at, *operands):
    return pl.pallas_call(
        kernel,
        grid_spec=pltpu.PrefetchScalarGridSpec(
            num_scalar_prefetch=2,
            grid=(1,),
            in_specs=[
                pl.BlockSpec(o.shape, functools.partial(lambda n, *_: (0,) * n, o.ndim))
                for o in operands
            ],
            out_specs=[
                pl.BlockSpec(o.shape, functools.partial(lambda n, *_: (0,) * n, len(o.shape)))
                for o in out_shape
            ],
        ),
        out_shape=out_shape,
        compiler_params=pltpu.CompilerParams(vmem_limit_bytes=SMALL_LIMIT),
        cost_estimate=pl.CostEstimate(flops=2**20, bytes_accessed=2**20, transcendentals=0),
        name=name,
    )(*place_at, *operands)


def sums_kernel(sizes, *refs):
    out = refs[-1]
    at = 0
    for i, size in enumerate(sizes):
        out[i, 0] = functools.reduce(lambda p, q: p + q, [r[0] for r in refs[at : at + size]])
        at += size


def sums(groups, rows, count, order=lambda i: i):
    lanes = groups[0][0][0].shape[-1]
    tile = min(rows, 160)
    operands, specs = [], []
    for group in groups:
        for array, first in group:
            operands.append(array.reshape(-1, rows, lanes))
            specs.append(
                pl.BlockSpec((1, tile, lanes), functools.partial(lambda f, i, j: (f + order(i), j, 0), first))
            )
    return pl.pallas_call(
        functools.partial(sums_kernel, [len(group) for group in groups]),
        grid=(count, rows // tile),
        in_specs=specs,
        out_specs=pl.BlockSpec((len(groups), 1, tile, lanes), lambda i, j: (0, i, j, 0)),
        out_shape=jax.ShapeDtypeStruct((len(groups), count, rows, lanes), F32),
        compiler_params=pltpu.CompilerParams(vmem_limit_bytes=SMALL_LIMIT),
        cost_estimate=pl.CostEstimate(
            flops=2**20, bytes_accessed=4 * 2**20, transcendentals=0
        ),
        name="sums",
    )(*operands)


def gather_kernel(factor, index, table, a0, a1, a2, b0, b1, b2, b3, c_ref, far_ref, out):
    tab = row_of(index, table)
    rows, half = c_ref.shape
    for i, ref in enumerate((b0, b1, b2, b3)):
        here = pl.ds(pl.multiple_of(tab[XAT + i] * rows, 8), rows)
        out[here, :half] = (a0[i] + a1[i] + a2[i]) * factor
        here = pl.ds(pl.multiple_of(lax.rem(tab[X] + i, 4) * rows, 8), rows)
        out[here, half:] = ref[...] * factor
    low = tab[OWN_HALF] == 0
    c, far = c_ref[...] * factor, far_ref[...] * factor
    out[4 * rows :, :half] = jnp.where(low, c, far)
    out[4 * rows :, half:] = jnp.where(low, far, c)


def last_kernel(index, table, own_ref, oth_ref, in_ref, out_ref):
    tab = row_of(index, table)
    count, half = in_ref.shape[0], in_ref.shape[1] // 2
    owner, zero = tab[IS_OWNER] == 1, tab[CORE] == 0
    in_ref[...] = jnp.where(owner, own_ref[:count], oth_ref[:count])
    own, oth = own_ref[count:], oth_ref[count:]
    for i in range(2):
        cut = slice(i * half, (i + 1) * half)
        out_ref[:, 2 * i * half : (2 * i + 1) * half] = jnp.where(zero, own[:, cut], oth[:, cut])
        out_ref[:, (2 * i + 1) * half : (2 * i + 2) * half] = jnp.where(
            zero, oth[:, cut], own[:, cut]
        )


def widen_kernel(n_ref, c_ref, n_out, c_out):
    n_out[...] = n_ref[...].astype(F32)
    c_out[...] = c_ref[...].astype(F32)


def widen(normed, cot):
    count, dim = normed.shape
    tile = pl.BlockSpec((count // 4, dim), lambda i: (i, 0))
    return pl.pallas_call(
        widen_kernel,
        grid=(4,),
        in_specs=[tile, tile],
        out_specs=[tile, tile],
        out_shape=[jax.ShapeDtypeStruct((count, dim), F32)] * 2,
        compiler_params=pltpu.CompilerParams(vmem_limit_bytes=OWN_LIMIT),
        cost_estimate=pl.CostEstimate(flops=2**20, bytes_accessed=8 * 2**20, transcendentals=0),
        name="widen",
    )(normed, cot)


def move(array, pairs):
    return lax.ppermute(array, AXES, pairs)


def total(terms):
    return functools.reduce(lambda p, q: p + q, terms)


def settle(array):
    return lax.optimization_barrier(array)


def twice(i):
    return 2 * i


def after(array, other):
    return lax.optimization_barrier((array, other))[0]


def local(normed, w_in, w_out, cotangent):
    dim = normed.shape[1]
    width = w_out.shape[1] // 4
    factor = (normed.shape[0] * lax.axis_size("dp") * lax.axis_size("grp")) ** (-0.5)
    index = lax.axis_index(AXES).reshape(1)
    place_at = index, jnp.asarray(TABLE.reshape(-1))
    win = w_in.reshape(2, 2, 2, width, dim)

    wide = widen(normed, cotangent)
    own = normed, cotangent
    other = move(wide[0], CORE_PAIRS), move(wide[1], CORE_PAIRS)
    terms = own_call(place_at, win, w_out, normed, cotangent)
    *first, oth0 = chunk_call(place_at, win, w_out, other, own, terms, 0)
    got_a0, got_b0, got_c0 = move(first[0], Z0), move(first[2], Y0), move(first[4], X0)
    index, _ = lax.optimization_barrier((index, first[0]))
    place_at = index, place_at[1]
    *second, oth1 = chunk_call(place_at, win, w_out, other, own, terms, 1)
    got_a1, got_b1, got_c1 = move(second[0], Z0), move(second[2], Y0), move(second[4], X0)

    oth0, index, got_a0, got_b0, early_c = lax.optimization_barrier(
        (oth0, index, got_a0, got_b0, first[5] + got_c0)
    )
    back_oth, back_own = back(place_at, terms[0], oth0, oth1, win)
    got_b1, back_own = lax.optimization_barrier((got_b1, back_own))
    grad_normed = (back_own + move(back_oth, CORE_PAIRS)).astype(BF)

    grp, dp = lax.axis_index("grp"), lax.axis_index("dp")
    own_first = ((dp >> 3) & 1) != ((grp >> 1) ^ (grp & (dp >> 2) & 1))

    rows = width // 2
    a = [second[1], got_a0]
    b = [first[3], got_b0], [second[3], got_b1]
    c = [early_c], [second[5], got_c1]
    to_b = sums([[(t, 0) for t in chunk] for chunk in b], rows, 1)
    got_b = move(to_b, Y1)
    c[1][1] = got_c1 = after(got_c1, to_b)
    to_c = jnp.where(own_first, total([second[5], got_c1]), early_c)
    got_c = move(to_c, X1)
    to_a = total([first[1], after(got_a1, to_c)])
    got_a = move(to_a, Z1)
    a = [settle(total(a)), got_a]
    b = [[(t, 4) for t in chunk] + [(got_b, 4 * k)] for k, chunk in enumerate(b)]
    c = [settle(jnp.where(own_first, total(c[0]), total(c[1]))), got_c]

    rows = width // 8
    to_b = sums(b, rows, 2)
    got_b = move(to_b, X0)
    b = [sums([[(t, at + 2) for t, at in chunk] for chunk in b], rows, 2), got_b]
    c[-1] = after(c[-1], to_b)
    to_c = total([t[:2] for t in c])
    got_c = move(to_c, Z0)
    c = [settle(total([t[2:] for t in c])), got_c]
    a[-1] = after(a[-1], to_c)
    to_a = total([t[:2] for t in a])
    got_a = move(to_a, Y0)
    kept, grad_normed = settle((total([t[2:] for t in a]), grad_normed))
    a = [kept, got_a]

    b[-1] = after(b[-1], to_a)
    to_b = sums([[(t, 0) for t in b]], rows, 2, twice)
    got_b = move(to_b, X1)
    b = [sums([[(t, 1) for t in b]], rows, 2, twice), got_b]
    c[-1] = after(c[-1], to_b)
    to_c = total([t[0] for t in c])
    got_c = move(to_c, Z1)
    c = [t[1] for t in c] + [got_c]
    a[-1] = after(a[-1], to_c)
    to_a = total([t[0] for t in a])
    got_a = move(to_a, Y1)

    rows = width // 16
    b[-1] = after(b[-1], to_a)
    to_b = sums([[(t, 2) for t in b]], rows, 2, lambda i: -2 * i)
    got_b = move(to_b, Z0)
    b = [sums([[(t, 1) for t in b]], rows, 2, twice)[0], got_b[0]]
    c[-1] = after(c[-1], to_b)
    to_c = total([t[:2] for t in c])
    got_c = move(to_c, Y0)
    c = [t[2:] for t in c] + [got_c]
    a = [(t, 4) for t in a] + [(after(got_a, to_c), 0)]
    to_a = sums([a], rows, 4, lambda i: (i + 2) % 4)
    got_a = move(to_a, X0)
    a = [(sums([a], rows, 4), 0), (got_a, 0)]

    b[-1] = after(b[-1], to_a)
    to_b = total([t[0] for t in b])
    got_b = move(to_b, Z1)
    c[-1] = after(c[-1], to_b)
    to_c = total([t[0] for t in c])
    got_c = move(to_c, Y1)
    a[1] = after(got_a, to_c), 0
    to_a = sums([a], rows, 4, lambda i: i + 1 - 2 * (i % 2))
    got_a = move(to_a, X1)

    b = total([t[1] for t in b] + [after(got_b, to_a)])
    c = total([t[1] for t in c] + [after(got_c, to_a)])
    c_far = move(c, FAR_PAIRS)
    (packed_rows,) = small_call(
        functools.partial(gather_kernel, factor),
        [jax.ShapeDtypeStruct((5 * (dim // 32), dim), F32)],
        "gather",
        place_at,
        *(t[0] for t, _ in a),
        got_a[0],
        b,
        *(move(b, owner_pairs(shift)) for shift in (1, 2, 3)),
        c,
        c_far,
    )
    grad_in, grad_out = small_call(
        last_kernel,
        [
            jax.ShapeDtypeStruct((width // 4, dim), F32),
            jax.ShapeDtypeStruct((dim // 32, 4 * width), F32),
        ],
        "last",
        place_at,
        packed_rows,
        move(packed_rows, CORE_PAIRS),
    )
    return (grad_in, grad_out, grad_normed)


def solution(mesh):
    placed = (P(AXES, None), P(), P(), P(AXES, None))
    return jax.shard_map(
        local,
        mesh=mesh,
        in_specs=placed,
        out_specs=(P("dp", None), P("dp", None), P(AXES, None)),
        check_vma=False,
    )
```

```python
import functools

import jax
import jax.numpy as jnp
import numpy as np
from jax import lax
from jax.experimental import pallas as pl
from jax.experimental.pallas import tpu as pltpu
from jax.sharding import PartitionSpec as P

AXES = ("grp", "dp")
BF = jnp.bfloat16
F32 = jnp.float32
OWN_LIMIT = 62 * 2**20
CHUNK_LIMIT = 62 * 2**20
BACK_LIMIT = 36 * 2**20
SMALL_LIMIT = 8 * 2**20


def place(x, y, z, c):
    return ((x // 2) * 2 + c) * 32 + z * 8 + (x % 2) * 4 + y


EVERY = [(x, y, z, c) for x in range(4) for y in range(4) for z in range(4) for c in range(2)]


def partner(i, core, step):
    return (i + (1 if i % 2 == (core + step) % 2 else -1)) % 4


def halving_pairs(axis, step):
    pairs = []
    for x, y, z, c in EVERY:
        at = [x, y, z]
        at[axis] = partner(at[axis], c, step)
        pairs.append((place(x, y, z, c), place(*at, c)))
    return pairs


X0, X1 = halving_pairs(0, 0), halving_pairs(0, 1)
Y0, Y1 = halving_pairs(1, 0), halving_pairs(1, 1)
Z0, Z1 = halving_pairs(2, 0), halving_pairs(2, 1)
CORE_PAIRS = [(place(x, y, z, c), place(x, y, z, 1 - c)) for x, y, z, c in EVERY]
FAR_PAIRS = [(place(x, y, z, c), place((x + 2) % 4, y, z, c)) for x, y, z, c in EVERY]


def owns(x, core):
    return x % 2 == core


def owner_pairs(shift):
    return [
        (place((x + shift) % 4, y, z, c), place(x, y, z, c)) for x, y, z, c in EVERY if owns(x, c)
    ]


def ring_order(i, core):
    first, second = partner(i, core, 0), partner(i, core, 1)
    return [partner(first, core, 1), first, second, i]


CORE, CHUNK, KIND, HALF, XAT, YAT, ZAT = 0, 1, 3, 7, 9, 13, 17
OWN_HALF, X, IS_OWNER, WIDTH = 22, 23, 24, 32


def table():
    rows = np.zeros((len(EVERY), WIDTH), np.int32)
    for x, y, z, c in EVERY:
        row = rows[place(x, y, z, c)]
        row[CORE] = c
        xs, ys, zs = ring_order(x, c), ring_order(y, c), ring_order(z, c)
        row[CHUNK], row[CHUNK + 1] = 1 - z % 2, z % 2
        row[KIND : KIND + 4] = [zs[1] // 2, zs[2] // 2, zs[0] // 2, zs[3] // 2]
        labels = {i: (i % 2, i // 2 if c == 0 else (i // 2) ^ (i % 2)) for i in range(4)}
        for k in range(2):
            (row[HALF + k],) = [labels[i][0] for i in xs[2:] if labels[i][1] == row[CHUNK + k]]
        for at, order in ((XAT, xs), (YAT, ys), (ZAT, zs)):
            for rank, i in enumerate(order):
                row[at + rank] = i
        row[OWN_HALF] = labels[x][1]
        row[X] = x
        row[IS_OWNER] = int(owns(x, c))
    return rows


TWO_BITS = [*range(XAT, ZAT + 4), X]
FIELDS = {at: (0, 2 * i, 3) for i, at in enumerate(TWO_BITS)}
ONE_BIT = [CORE, CHUNK, CHUNK + 1, *range(KIND, KIND + 4), HALF, HALF + 1, OWN_HALF, IS_OWNER]
FIELDS.update({at: (1, i, 1) for i, at in enumerate(ONE_BIT)})


def packed():
    rows = table()
    words = np.zeros((len(EVERY), 2), np.int32)
    for at, (word, shift, _) in FIELDS.items():
        words[:, word] |= rows[:, at] << shift
    return words


TABLE = packed()


def field(index, table, at):
    word, shift, mask = FIELDS[at]
    return (table[index[0] * 2 + word] >> shift) & mask


NT = (((1,), (1,)), ((), ()))
TN = (((0,), (0,)), ((), ()))


def row_of(index, table):
    class Row:
        def __getitem__(self, at):
            return field(index, table, at)

    return Row()


def gated(value, gate, dact):
    cdf = 0.5 * (1.0 + lax.erf(gate * (2.0 ** -0.5)))
    density = jnp.exp(-0.5 * gate * gate) * ((2.0 * jnp.pi) ** -0.5)
    share = gate * cdf
    return (
        (value * share).astype(BF),
        (dact * share).astype(BF),
        (dact * value * (cdf + gate * density)).astype(BF),
    )


class Copies:
    def __init__(self, sems):
        self.sems, self.used = sems, 0

    def start(self, source, target):
        copy = pltpu.make_async_copy(source, target, self.sems.at[self.used])
        self.used += 1
        copy.start()
        return copy


def own_kernel(index, table, win, wout, n_in, c_in, d_out, act_out, w, wo, n, c, d, act, sems):
    tab = row_of(index, table)
    width = w.shape[2]
    copies = Copies(sems)
    load_w, load_wo = [], []
    for k in range(2):
        block, core = tab[CHUNK + k], tab[CORE]
        column = pl.multiple_of((block * 2 + core) * width, 128)
        load_wo.append(copies.start(wout.at[:, pl.ds(column, width)], wo.at[k]))
        if k == 0:
            load_c = copies.start(c_in, c)
        load_w.append([copies.start(win.at[i, block, core], w.at[k, i]) for i in range(2)])
        if k == 0:
            load_n = copies.start(n_in, n)
    stores = []
    for k in range(2):
        load_wo[k].wait()
        if k == 0:
            load_c.wait()
        dact = jnp.dot(c[...], wo[k], preferred_element_type=F32)
        for copy in load_w[k]:
            copy.wait()
        if k == 0:
            load_n.wait()
        proj = lax.dot_general(
            n[...], w[k].reshape(2 * width, w.shape[3]), NT, preferred_element_type=F32
        )
        act[k], d[k, 0], d[k, 1] = gated(proj[:, :width], proj[:, width:], dact)
        stores.append(copies.start(act.at[k], act_out.at[k]))
        stores.append(copies.start(d.at[k], d_out.at[k]))
    for copy in stores:
        copy.wait()


def own_call(place_at, win, wout, normed, cot):
    count, dim = normed.shape
    width = win.shape[3]
    anywhere = pl.BlockSpec(memory_space=pl.ANY)
    return pl.pallas_call(
        own_kernel,
        grid_spec=pltpu.PrefetchScalarGridSpec(
            num_scalar_prefetch=2,
            grid=(1,),
            in_specs=[anywhere] * 4,
            out_specs=[anywhere] * 2,
            scratch_shapes=[
                pltpu.VMEM((2, 2, width, dim), BF),
                pltpu.VMEM((2, dim, width), BF),
                pltpu.VMEM((count, dim), BF),
                pltpu.VMEM((count, dim), BF),
                pltpu.VMEM((2, 2, count, width), BF),
                pltpu.VMEM((2, count, width), BF),
                pltpu.SemaphoreType.DMA((12,)),
            ],
        ),
        out_shape=[
            jax.ShapeDtypeStruct((2, 2, count, width), BF),
            jax.ShapeDtypeStruct((2, count, width), BF),
        ],
        compiler_params=pltpu.CompilerParams(vmem_limit_bytes=OWN_LIMIT),
        cost_estimate=pl.CostEstimate(
            flops=12 * count * dim * width, bytes_accessed=16 * 2**20, transcendentals=0
        ),
        name="own_terms",
    )(*place_at, win, wout, normed, cot)


def chunk_kernel(
    chunk, index, table, win, wout, n_in, c_in, n_own, c_own, d_own, act_own,
    a_send, a_keep, b_send, b_keep, c_send, c_keep, d_out,
    w, wo, nb, cb, d, act, gin, gout, load_sems, sems,
):
    tab = row_of(index, table)
    width, dim = w.shape[1:]
    count = n_in.shape[0]
    half = dim // 2
    core, block = tab[CORE], tab[CHUNK + chunk]
    own, oth = pl.ds(count, count), pl.ds(0, count)
    loads = Copies(load_sems)
    column = pl.multiple_of((block * 2 + core) * width, 128)
    load_wo = loads.start(wout.at[:, pl.ds(column, width)], wo)
    lanes = [pl.ds(part * half, half) for part in range(2)]
    raw = gin.at[:, :, oth]
    load_c = [loads.start(c_in.at[:, lanes[i]], raw.at[0, i]) for i in range(2)]
    load_w = [loads.start(win.at[i, block, core], w.at[i]) for i in range(2)]
    load_n = [loads.start(n_in.at[:, lanes[i]], raw.at[1, i]) for i in range(2)]
    load_own = [loads.start(c_own, cb.at[own]), loads.start(act_own.at[chunk], act.at[own])]
    load_own += [loads.start(d_own.at[chunk, i], d.at[i, own]) for i in range(2)]
    load_own += [loads.start(n_own, nb.at[own])]

    def store(source, target, sem):
        pltpu.make_async_copy(source, target, sems.at[sem]).start()

    load_wo.wait()
    for i in range(2):
        load_c[i].wait()
        cb[oth, i * half : (i + 1) * half] = raw[0, i].astype(BF)
    dact = jnp.dot(cb[oth], wo[...], preferred_element_type=F32)
    for i in range(2):
        load_n[i].wait()
        nb[oth, i * half : (i + 1) * half] = raw[1, i].astype(BF)
    for copy in load_w:
        copy.wait()
    proj = lax.dot_general(
        nb[oth], w[...].reshape(2 * width, dim), NT, preferred_element_type=F32
    )
    act[oth], d[0, oth], d[1, oth] = gated(proj[:, :width], proj[:, width:], dact)
    for i in range(2):
        store(d.at[i, oth], d_out.at[i], 0)
    for copy in load_own:
        copy.wait()

    gout[...] = lax.dot_general(cb[...], act[...], TN, preferred_element_type=F32)
    tiny = dim // 32
    kept = tab[HALF + chunk]
    for out, x, sem in ((c_send, 1 - kept, 1), (c_keep, kept, 2)):
        for z in range(4):
            for y in range(4):
                at = ((tab[ZAT + z] * 2 + x) * 4 + tab[YAT + y]) * tiny
                store(gout.at[pl.ds(pl.multiple_of(at, 8), tiny)], out.at[z, y], sem)
    small = width // 16
    for slot, out in enumerate((a_send, a_keep)):
        kind = tab[KIND + 2 * chunk + slot]
        for part in range(2):
            cut = slice(part * half, (part + 1) * half)
            gin[slot, part] = lax.dot_general(
                d[kind], nb[:, cut], TN, preferred_element_type=F32
            )
            for y in range(4):
                for x in range(4):
                    at = (tab[YAT + y] * 4 + tab[XAT + x]) * small
                    rows = gin.at[slot, part, pl.ds(pl.multiple_of(at, 8), small)]
                    if part == 0:
                        store(rows, out.at[y, x], 3 + slot)
                    else:
                        store(rows, (b_send, b_keep)[y // 2].at[y % 2, x, slot], 5 + y // 2)
    outs = (d_out, c_send, c_keep, a_send, a_keep, b_send, b_keep)
    for i, out in enumerate(outs):
        pltpu.make_async_copy(out, out, sems.at[i]).wait()


def chunk_call(place_at, win, wout, other, own, terms, chunk):
    count, dim = own[0].shape
    width = win.shape[3]
    a = jax.ShapeDtypeStruct((4, 4, width // 16, dim // 2), F32)
    b = jax.ShapeDtypeStruct((2, 4, 2, width // 16, dim // 2), F32)
    c = jax.ShapeDtypeStruct((4, 4, dim // 32, width), F32)
    outs = [a, a, b, b, c, c, jax.ShapeDtypeStruct((2, count, width), BF)]
    operands = [win, wout, *other, *own, *terms]
    anywhere = pl.BlockSpec(memory_space=pl.ANY)
    return pl.pallas_call(
        functools.partial(chunk_kernel, chunk),
        grid_spec=pltpu.PrefetchScalarGridSpec(
            num_scalar_prefetch=2,
            grid=(1,),
            in_specs=[anywhere] * len(operands),
            out_specs=[anywhere] * len(outs),
            scratch_shapes=[
                pltpu.VMEM((2, width, dim), BF),
                pltpu.VMEM((dim, width), BF),
                pltpu.VMEM((2 * count, dim), BF),
                pltpu.VMEM((2 * count, dim), BF),
                pltpu.VMEM((2, 2 * count, width), BF),
                pltpu.VMEM((2 * count, width), BF),
                pltpu.VMEM((2, 2, width, dim // 2), F32),
                pltpu.VMEM((dim, width), F32),
                pltpu.SemaphoreType.DMA((12,)),
                pltpu.SemaphoreType.DMA((7,)),
            ],
        ),
        out_shape=outs,
        compiler_params=pltpu.CompilerParams(vmem_limit_bytes=CHUNK_LIMIT),
        cost_estimate=pl.CostEstimate(
            flops=16 * count * dim * width, bytes_accessed=16 * 2**20, transcendentals=0
        ),
        name="chunk",
    )(*place_at, *operands)


def back_kernel(index, table, own_ref, oth0_ref, oth1_ref, w_ref, oth_out, own_out):
    tab = row_of(index, table)
    w = w_ref[...].reshape(2 * w_ref.shape[1], w_ref.shape[2])
    straight = tab[CHUNK] == 0
    for d0, d1, out in (
        (oth0_ref[...], oth1_ref[...], oth_out),
        (own_ref[0], own_ref[1], own_out),
    ):
        low = jnp.where(straight, d0, d1)
        high = jnp.where(straight, d1, d0)
        part = jnp.dot(jnp.concatenate([low, high], axis=1), w, preferred_element_type=F32)

        @pl.when(pl.program_id(0) == 0)
        def _():
            out[...] = part

        @pl.when(pl.program_id(0) == 1)
        def _():
            out[...] += part


def back(place_at, own, oth0, oth1, win):
    _, count, width = oth0.shape
    dim = win.shape[4]
    whole = pl.BlockSpec((count, dim), lambda k, i, t: (0, 0))
    d_spec = pl.BlockSpec((None, count, width), lambda k, i, t: (k, 0, 0))
    return pl.pallas_call(
        back_kernel,
        grid_spec=pltpu.PrefetchScalarGridSpec(
            num_scalar_prefetch=2,
            grid=(2,),
            in_specs=[
                pl.BlockSpec((2, None, count, width), lambda k, i, t: (0, k, 0, 0)),
                d_spec,
                d_spec,
                pl.BlockSpec(
                    (None, 2, None, width, dim),
                    lambda k, i, t: (k, 0, field(i, t, CORE), 0, 0),
                ),
            ],
            out_specs=[whole, whole],
        ),
        out_shape=[jax.ShapeDtypeStruct((count, dim), F32)] * 2,
        compiler_params=pltpu.CompilerParams(vmem_limit_bytes=BACK_LIMIT),
        cost_estimate=pl.CostEstimate(
            flops=16 * count * dim * width, bytes_accessed=16 * 2**20, transcendentals=0
        ),
        name="back",
    )(*place_at, own, oth0, oth1, win)


def small_call(kernel, out_shape, name, place_at, *operands):
    return pl.pallas_call(
        kernel,
        grid_spec=pltpu.PrefetchScalarGridSpec(
            num_scalar_prefetch=2,
            grid=(1,),
            in_specs=[
                pl.BlockSpec(o.shape, functools.partial(lambda n, *_: (0,) * n, o.ndim))
                for o in operands
            ],
            out_specs=[
                pl.BlockSpec(o.shape, functools.partial(lambda n, *_: (0,) * n, len(o.shape)))
                for o in out_shape
            ],
        ),
        out_shape=out_shape,
        compiler_params=pltpu.CompilerParams(vmem_limit_bytes=SMALL_LIMIT),
        cost_estimate=pl.CostEstimate(flops=2**20, bytes_accessed=2**20, transcendentals=0),
        name=name,
    )(*place_at, *operands)


def sums_kernel(sizes, *refs):
    out = refs[-1]
    at = 0
    for i, size in enumerate(sizes):
        out[i, 0] = functools.reduce(lambda p, q: p + q, [r[0] for r in refs[at : at + size]])
        at += size


def sums(groups, rows, count, order=lambda i: i):
    lanes = groups[0][0][0].shape[-1]
    tile = min(rows, 160)
    operands, specs = [], []
    for group in groups:
        for array, first in group:
            operands.append(array.reshape(-1, rows, lanes))
            specs.append(
                pl.BlockSpec((1, tile, lanes), functools.partial(lambda f, i, j: (f + order(i), j, 0), first))
            )
    return pl.pallas_call(
        functools.partial(sums_kernel, [len(group) for group in groups]),
        grid=(count, rows // tile),
        in_specs=specs,
        out_specs=pl.BlockSpec((len(groups), 1, tile, lanes), lambda i, j: (0, i, j, 0)),
        out_shape=jax.ShapeDtypeStruct((len(groups), count, rows, lanes), F32),
        compiler_params=pltpu.CompilerParams(vmem_limit_bytes=SMALL_LIMIT),
        cost_estimate=pl.CostEstimate(
            flops=2**20, bytes_accessed=4 * 2**20, transcendentals=0
        ),
        name="sums",
    )(*operands)


def gather_kernel(factor, index, table, a0, a1, a2, b0, b1, b2, b3, c_ref, far_ref, out):
    tab = row_of(index, table)
    rows, half = c_ref.shape
    for i, ref in enumerate((b0, b1, b2, b3)):
        here = pl.ds(pl.multiple_of(tab[XAT + i] * rows, 8), rows)
        out[here, :half] = (a0[i] + a1[i] + a2[i]) * factor
        here = pl.ds(pl.multiple_of(lax.rem(tab[X] + i, 4) * rows, 8), rows)
        out[here, half:] = ref[...] * factor
    low = tab[OWN_HALF] == 0
    c, far = c_ref[...] * factor, far_ref[...] * factor
    out[4 * rows :, :half] = jnp.where(low, c, far)
    out[4 * rows :, half:] = jnp.where(low, far, c)


def last_kernel(index, table, own_ref, oth_ref, in_ref, out_ref):
    tab = row_of(index, table)
    count, half = in_ref.shape[0], in_ref.shape[1] // 2
    owner, zero = tab[IS_OWNER] == 1, tab[CORE] == 0
    in_ref[...] = jnp.where(owner, own_ref[:count], oth_ref[:count])
    own, oth = own_ref[count:], oth_ref[count:]
    for i in range(2):
        cut = slice(i * half, (i + 1) * half)
        out_ref[:, 2 * i * half : (2 * i + 1) * half] = jnp.where(zero, own[:, cut], oth[:, cut])
        out_ref[:, (2 * i + 1) * half : (2 * i + 2) * half] = jnp.where(
            zero, oth[:, cut], own[:, cut]
        )


def widen_kernel(n_ref, c_ref, n_out, c_out):
    n_out[...] = n_ref[...].astype(F32)
    c_out[...] = c_ref[...].astype(F32)


def widen(normed, cot):
    count, dim = normed.shape
    tile = pl.BlockSpec((count // 4, dim), lambda i: (i, 0))
    return pl.pallas_call(
        widen_kernel,
        grid=(4,),
        in_specs=[tile, tile],
        out_specs=[tile, tile],
        out_shape=[jax.ShapeDtypeStruct((count, dim), F32)] * 2,
        compiler_params=pltpu.CompilerParams(vmem_limit_bytes=OWN_LIMIT),
        cost_estimate=pl.CostEstimate(flops=2**20, bytes_accessed=8 * 2**20, transcendentals=0),
        name="widen",
    )(normed, cot)


def move(array, pairs):
    return lax.ppermute(array, AXES, pairs)


def total(terms):
    return functools.reduce(lambda p, q: p + q, terms)


def settle(array):
    return lax.optimization_barrier(array)


def twice(i):
    return 2 * i


def after(array, other):
    return lax.optimization_barrier((array, other))[0]


def local(normed, w_in, w_out, cotangent):
    dim = normed.shape[1]
    width = w_out.shape[1] // 4
    factor = (normed.shape[0] * lax.axis_size("dp") * lax.axis_size("grp")) ** (-0.5)
    index = lax.axis_index(AXES).reshape(1)
    place_at = index, jnp.asarray(TABLE.reshape(-1))
    win = w_in.reshape(2, 2, 2, width, dim)

    wide = widen(normed, cotangent)
    own = normed, cotangent
    other = move(wide[0], CORE_PAIRS), move(wide[1], CORE_PAIRS)
    terms = own_call(place_at, win, w_out, normed, cotangent)
    *first, oth0 = chunk_call(place_at, win, w_out, other, own, terms, 0)
    got_a0, got_b0, got_c0 = move(first[0], Z0), move(first[2], Y0), move(first[4], X0)
    index, _ = lax.optimization_barrier((index, first[0]))
    place_at = index, place_at[1]
    *second, oth1 = chunk_call(place_at, win, w_out, other, own, terms, 1)
    got_a1, got_b1, got_c1 = move(second[0], Z0), move(second[2], Y0), move(second[4], X0)

    oth0, index, got_a0, got_b0, early_c = lax.optimization_barrier(
        (oth0, index, got_a0, got_b0, first[5] + got_c0)
    )
    back_oth, back_own = back(place_at, terms[0], oth0, oth1, win)
    got_b1, back_own = lax.optimization_barrier((got_b1, back_own))
    grad_normed = (back_own + move(back_oth, CORE_PAIRS)).astype(BF)

    grp, dp = lax.axis_index("grp"), lax.axis_index("dp")
    own_first = ((dp >> 3) & 1) != ((grp >> 1) ^ (grp & (dp >> 2) & 1))

    rows = width // 2
    a = [second[1], got_a0]
    b = [first[3], got_b0], [second[3], got_b1]
    c = [early_c], [second[5], got_c1]
    to_b = sums([[(t, 0) for t in chunk] for chunk in b], rows, 1)
    got_b = move(to_b, Y1)
    c[1][1] = got_c1 = after(got_c1, to_b)
    to_c = jnp.where(own_first, total([second[5], got_c1]), early_c)
    got_c = move(to_c, X1)
    to_a = total([first[1], after(got_a1, to_c)])
    got_a = move(to_a, Z1)
    a = [settle(total(a)), got_a]
    b = [[(t, 4) for t in chunk] + [(got_b, 4 * k)] for k, chunk in enumerate(b)]
    c = [settle(jnp.where(own_first, total(c[0]), total(c[1]))), got_c]

    rows = width // 8
    to_b = sums(b, rows, 2)
    got_b = move(to_b, X0)
    b = [sums([[(t, at + 2) for t, at in chunk] for chunk in b], rows, 2), got_b]
    c[-1] = after(c[-1], to_b)
    to_c = total([t[:2] for t in c])
    got_c = move(to_c, Z0)
    c = [settle(total([t[2:] for t in c])), got_c]
    a[-1] = after(a[-1], to_c)
    to_a = total([t[:2] for t in a])
    got_a = move(to_a, Y0)
    a = [settle(total([t[2:] for t in a])), got_a]

    b[-1] = after(b[-1], to_a)
    to_b = sums([[(t, 0) for t in b]], rows, 2, twice)
    got_b = move(to_b, X1)
    b = [sums([[(t, 1) for t in b]], rows, 2, twice), got_b]
    c[-1] = after(c[-1], to_b)
    to_c = total([t[0] for t in c])
    got_c = move(to_c, Z1)
    c = [t[1] for t in c] + [got_c]
    a[-1] = after(a[-1], to_c)
    to_a = total([t[0] for t in a])
    got_a = move(to_a, Y1)

    rows = width // 16
    b[-1] = after(b[-1], to_a)
    to_b = sums([[(t, 2) for t in b]], rows, 2, lambda i: -2 * i)
    got_b = move(to_b, Z0)
    b = [sums([[(t, 1) for t in b]], rows, 2, twice)[0], got_b[0]]
    c[-1] = after(c[-1], to_b)
    to_c = total([t[:2] for t in c])
    got_c = move(to_c, Y0)
    c = [t[2:] for t in c] + [got_c]
    a = [(t, 4) for t in a] + [(after(got_a, to_c), 0)]
    to_a = sums([a], rows, 4, lambda i: (i + 2) % 4)
    got_a = move(to_a, X0)
    kept, grad_normed = settle((sums([a], rows, 4), grad_normed))
    a = [(kept, 0), (got_a, 0)]

    b[-1] = after(b[-1], to_a)
    to_b = total([t[0] for t in b])
    got_b = move(to_b, Z1)
    c[-1] = after(c[-1], to_b)
    to_c = total([t[0] for t in c])
    got_c = move(to_c, Y1)
    b = total([t[1] for t in b] + [after(got_b, to_c)])
    b_rest = [move(b, owner_pairs(shift)) for shift in (1, 2, 3)]
    a[1] = after(got_a, b_rest[:2]), 0
    to_a = sums([a], rows, 4, lambda i: i + 1 - 2 * (i % 2))
    got_a = move(to_a, X1)

    c = total([t[1] for t in c] + [after(got_c, to_a)])
    c_far = move(c, FAR_PAIRS)
    (packed_rows,) = small_call(
        functools.partial(gather_kernel, factor),
        [jax.ShapeDtypeStruct((5 * (dim // 32), dim), F32)],
        "gather",
        place_at,
        *(t[0] for t, _ in a),
        got_a[0],
        b,
        *b_rest,
        c,
        c_far,
    )
    grad_in, grad_out = small_call(
        last_kernel,
        [
            jax.ShapeDtypeStruct((width // 4, dim), F32),
            jax.ShapeDtypeStruct((dim // 32, 4 * width), F32),
        ],
        "last",
        place_at,
        packed_rows,
        move(packed_rows, CORE_PAIRS),
    )
    return (grad_in, grad_out, grad_normed)


def solution(mesh):
    placed = (P(AXES, None), P(), P(), P(AXES, None))
    return jax.shard_map(
        local,
        mesh=mesh,
        in_specs=placed,
        out_specs=(P("dp", None), P("dp", None), P(AXES, None)),
        check_vma=False,
    )
```

```python
import functools

import jax
import jax.numpy as jnp
import numpy as np
from jax import lax
from jax.experimental import pallas as pl
from jax.experimental.pallas import tpu as pltpu
from jax.sharding import PartitionSpec as P

AXES = ("grp", "dp")
BF = jnp.bfloat16
F32 = jnp.float32
OWN_LIMIT = 62 * 2**20
CHUNK_LIMIT = 62 * 2**20
BACK_LIMIT = 36 * 2**20
SMALL_LIMIT = 8 * 2**20


def place(x, y, z, c):
    return ((x // 2) * 2 + c) * 32 + z * 8 + (x % 2) * 4 + y


EVERY = [(x, y, z, c) for x in range(4) for y in range(4) for z in range(4) for c in range(2)]


def partner(i, core, step):
    return (i + (1 if i % 2 == (core + step) % 2 else -1)) % 4


def halving_pairs(axis, step):
    pairs = []
    for x, y, z, c in EVERY:
        at = [x, y, z]
        at[axis] = partner(at[axis], c, step)
        pairs.append((place(x, y, z, c), place(*at, c)))
    return pairs


X0, X1 = halving_pairs(0, 0), halving_pairs(0, 1)
Y0, Y1 = halving_pairs(1, 0), halving_pairs(1, 1)
Z0, Z1 = halving_pairs(2, 0), halving_pairs(2, 1)
CORE_PAIRS = [(place(x, y, z, c), place(x, y, z, 1 - c)) for x, y, z, c in EVERY]
FAR_PAIRS = [(place(x, y, z, c), place((x + 2) % 4, y, z, c)) for x, y, z, c in EVERY]


def owns(x, core):
    return x % 2 == core


def owner_pairs(shift):
    return [
        (place((x + shift) % 4, y, z, c), place(x, y, z, c)) for x, y, z, c in EVERY if owns(x, c)
    ]


def ring_order(i, core):
    first, second = partner(i, core, 0), partner(i, core, 1)
    return [partner(first, core, 1), first, second, i]


CORE, CHUNK, KIND, HALF, XAT, YAT, ZAT = 0, 1, 3, 7, 9, 13, 17
OWN_HALF, X, IS_OWNER, WIDTH = 22, 23, 24, 32


def table():
    rows = np.zeros((len(EVERY), WIDTH), np.int32)
    for x, y, z, c in EVERY:
        row = rows[place(x, y, z, c)]
        row[CORE] = c
        xs, ys, zs = ring_order(x, c), ring_order(y, c), ring_order(z, c)
        row[CHUNK], row[CHUNK + 1] = 1 - z % 2, z % 2
        row[KIND : KIND + 4] = [zs[1] // 2, zs[2] // 2, zs[0] // 2, zs[3] // 2]
        labels = {i: (i % 2, i // 2 if c == 0 else (i // 2) ^ (i % 2)) for i in range(4)}
        for k in range(2):
            (row[HALF + k],) = [labels[i][0] for i in xs[2:] if labels[i][1] == row[CHUNK + k]]
        for at, order in ((XAT, xs), (YAT, ys), (ZAT, zs)):
            for rank, i in enumerate(order):
                row[at + rank] = i
        row[OWN_HALF] = labels[x][1]
        row[X] = x
        row[IS_OWNER] = int(owns(x, c))
    return rows


TWO_BITS = [*range(XAT, ZAT + 4), X]
FIELDS = {at: (0, 2 * i, 3) for i, at in enumerate(TWO_BITS)}
ONE_BIT = [CORE, CHUNK, CHUNK + 1, *range(KIND, KIND + 4), HALF, HALF + 1, OWN_HALF, IS_OWNER]
FIELDS.update({at: (1, i, 1) for i, at in enumerate(ONE_BIT)})


def packed():
    rows = table()
    words = np.zeros((len(EVERY), 2), np.int32)
    for at, (word, shift, _) in FIELDS.items():
        words[:, word] |= rows[:, at] << shift
    return words


TABLE = packed()


def field(index, table, at):
    word, shift, mask = FIELDS[at]
    return (table[index[0] * 2 + word] >> shift) & mask


NT = (((1,), (1,)), ((), ()))
TN = (((0,), (0,)), ((), ()))


def row_of(index, table):
    class Row:
        def __getitem__(self, at):
            return field(index, table, at)

    return Row()


def gated(value, gate, dact):
    cdf = 0.5 * (1.0 + lax.erf(gate * (2.0 ** -0.5)))
    density = jnp.exp(-0.5 * gate * gate) * ((2.0 * jnp.pi) ** -0.5)
    share = gate * cdf
    return (
        (value * share).astype(BF),
        (dact * share).astype(BF),
        (dact * value * (cdf + gate * density)).astype(BF),
    )


class Copies:
    def __init__(self, sems):
        self.sems, self.used = sems, 0

    def start(self, source, target):
        copy = pltpu.make_async_copy(source, target, self.sems.at[self.used])
        self.used += 1
        copy.start()
        return copy


def own_kernel(index, table, win, wout, n_in, c_in, d_out, act_out, w, wo, n, c, d, act, sems):
    tab = row_of(index, table)
    width = w.shape[2]
    copies = Copies(sems)
    load_w, load_wo = [], []
    for k in range(2):
        block, core = tab[CHUNK + k], tab[CORE]
        column = pl.multiple_of((block * 2 + core) * width, 128)
        load_wo.append(copies.start(wout.at[:, pl.ds(column, width)], wo.at[k]))
        if k == 0:
            load_c = copies.start(c_in, c)
        load_w.append([copies.start(win.at[i, block, core], w.at[k, i]) for i in range(2)])
        if k == 0:
            load_n = copies.start(n_in, n)
    stores = []
    for k in range(2):
        load_wo[k].wait()
        if k == 0:
            load_c.wait()
        dact = jnp.dot(c[...], wo[k], preferred_element_type=F32)
        for copy in load_w[k]:
            copy.wait()
        if k == 0:
            load_n.wait()
        proj = lax.dot_general(
            n[...], w[k].reshape(2 * width, w.shape[3]), NT, preferred_element_type=F32
        )
        act[k], d[k, 0], d[k, 1] = gated(proj[:, :width], proj[:, width:], dact)
        stores.append(copies.start(act.at[k], act_out.at[k]))
        stores.append(copies.start(d.at[k], d_out.at[k]))
    for copy in stores:
        copy.wait()


def own_call(place_at, win, wout, normed, cot):
    count, dim = normed.shape
    width = win.shape[3]
    anywhere = pl.BlockSpec(memory_space=pl.ANY)
    return pl.pallas_call(
        own_kernel,
        grid_spec=pltpu.PrefetchScalarGridSpec(
            num_scalar_prefetch=2,
            grid=(1,),
            in_specs=[anywhere] * 4,
            out_specs=[anywhere] * 2,
            scratch_shapes=[
                pltpu.VMEM((2, 2, width, dim), BF),
                pltpu.VMEM((2, dim, width), BF),
                pltpu.VMEM((count, dim), BF),
                pltpu.VMEM((count, dim), BF),
                pltpu.VMEM((2, 2, count, width), BF),
                pltpu.VMEM((2, count, width), BF),
                pltpu.SemaphoreType.DMA((12,)),
            ],
        ),
        out_shape=[
            jax.ShapeDtypeStruct((2, 2, count, width), BF),
            jax.ShapeDtypeStruct((2, count, width), BF),
        ],
        compiler_params=pltpu.CompilerParams(vmem_limit_bytes=OWN_LIMIT),
        cost_estimate=pl.CostEstimate(
            flops=12 * count * dim * width, bytes_accessed=16 * 2**20, transcendentals=0
        ),
        name="own_terms",
    )(*place_at, win, wout, normed, cot)


def chunk_kernel(
    chunk, index, table, win, wout, n_in, c_in, n_own, c_own, d_own, act_own,
    a_send, a_keep, b_send, b_keep, c_send, c_keep, d_out,
    w, wo, nb, cb, d, act, gin, gout, load_sems, sems,
):
    tab = row_of(index, table)
    width, dim = w.shape[1:]
    count = n_in.shape[0]
    half = dim // 2
    core, block = tab[CORE], tab[CHUNK + chunk]
    own, oth = pl.ds(count, count), pl.ds(0, count)
    loads = Copies(load_sems)
    column = pl.multiple_of((block * 2 + core) * width, 128)
    load_wo = loads.start(wout.at[:, pl.ds(column, width)], wo)
    lanes = [pl.ds(part * half, half) for part in range(2)]
    raw = gin.at[:, :, oth]
    load_c = [loads.start(c_in.at[:, lanes[i]], raw.at[0, i]) for i in range(2)]
    load_w = [loads.start(win.at[i, block, core], w.at[i]) for i in range(2)]
    load_n = [loads.start(n_in.at[:, lanes[i]], raw.at[1, i]) for i in range(2)]
    load_own = [loads.start(c_own, cb.at[own]), loads.start(act_own.at[chunk], act.at[own])]
    load_own += [loads.start(d_own.at[chunk, i], d.at[i, own]) for i in range(2)]
    load_own += [loads.start(n_own, nb.at[own])]

    def store(source, target, sem):
        pltpu.make_async_copy(source, target, sems.at[sem]).start()

    load_wo.wait()
    for i in range(2):
        load_c[i].wait()
        cb[oth, i * half : (i + 1) * half] = raw[0, i].astype(BF)
    dact = jnp.dot(cb[oth], wo[...], preferred_element_type=F32)
    for i in range(2):
        load_n[i].wait()
        nb[oth, i * half : (i + 1) * half] = raw[1, i].astype(BF)
    for copy in load_w:
        copy.wait()
    proj = lax.dot_general(
        nb[oth], w[...].reshape(2 * width, dim), NT, preferred_element_type=F32
    )
    act[oth], d[0, oth], d[1, oth] = gated(proj[:, :width], proj[:, width:], dact)
    for i in range(2):
        store(d.at[i, oth], d_out.at[i], 0)
    for copy in load_own:
        copy.wait()

    gout[...] = lax.dot_general(cb[...], act[...], TN, preferred_element_type=F32)
    tiny = dim // 32
    kept = tab[HALF + chunk]
    for out, x, sem in ((c_send, 1 - kept, 1), (c_keep, kept, 2)):
        for z in range(4):
            for y in range(4):
                at = ((tab[ZAT + z] * 2 + x) * 4 + tab[YAT + y]) * tiny
                store(gout.at[pl.ds(pl.multiple_of(at, 8), tiny)], out.at[z, y], sem)
    small = width // 16
    for slot, out in enumerate((a_send, a_keep)):
        kind = tab[KIND + 2 * chunk + slot]
        for part in range(2):
            cut = slice(part * half, (part + 1) * half)
            gin[slot, part] = lax.dot_general(
                d[kind], nb[:, cut], TN, preferred_element_type=F32
            )
            for y in range(4):
                for x in range(4):
                    at = (tab[YAT + y] * 4 + tab[XAT + x]) * small
                    rows = gin.at[slot, part, pl.ds(pl.multiple_of(at, 8), small)]
                    if part == 0:
                        store(rows, out.at[y, x], 3 + slot)
                    else:
                        store(rows, (b_send, b_keep)[y // 2].at[y % 2, x, slot], 5 + y // 2)
    outs = (d_out, c_send, c_keep, a_send, a_keep, b_send, b_keep)
    for i, out in enumerate(outs):
        pltpu.make_async_copy(out, out, sems.at[i]).wait()


def chunk_call(place_at, win, wout, other, own, terms, chunk):
    count, dim = own[0].shape
    width = win.shape[3]
    a = jax.ShapeDtypeStruct((4, 4, width // 16, dim // 2), F32)
    b = jax.ShapeDtypeStruct((2, 4, 2, width // 16, dim // 2), F32)
    c = jax.ShapeDtypeStruct((4, 4, dim // 32, width), F32)
    outs = [a, a, b, b, c, c, jax.ShapeDtypeStruct((2, count, width), BF)]
    operands = [win, wout, *other, *own, *terms]
    anywhere = pl.BlockSpec(memory_space=pl.ANY)
    return pl.pallas_call(
        functools.partial(chunk_kernel, chunk),
        grid_spec=pltpu.PrefetchScalarGridSpec(
            num_scalar_prefetch=2,
            grid=(1,),
            in_specs=[anywhere] * len(operands),
            out_specs=[anywhere] * len(outs),
            scratch_shapes=[
                pltpu.VMEM((2, width, dim), BF),
                pltpu.VMEM((dim, width), BF),
                pltpu.VMEM((2 * count, dim), BF),
                pltpu.VMEM((2 * count, dim), BF),
                pltpu.VMEM((2, 2 * count, width), BF),
                pltpu.VMEM((2 * count, width), BF),
                pltpu.VMEM((2, 2, width, dim // 2), F32),
                pltpu.VMEM((dim, width), F32),
                pltpu.SemaphoreType.DMA((12,)),
                pltpu.SemaphoreType.DMA((7,)),
            ],
        ),
        out_shape=outs,
        compiler_params=pltpu.CompilerParams(vmem_limit_bytes=CHUNK_LIMIT),
        cost_estimate=pl.CostEstimate(
            flops=16 * count * dim * width, bytes_accessed=16 * 2**20, transcendentals=0
        ),
        name="chunk",
    )(*place_at, *operands)


def back_kernel(index, table, own_ref, oth0_ref, oth1_ref, w_ref, oth_out, own_out):
    tab = row_of(index, table)
    w = w_ref[...].reshape(2 * w_ref.shape[1], w_ref.shape[2])
    straight = tab[CHUNK] == 0
    for d0, d1, out in (
        (oth0_ref[...], oth1_ref[...], oth_out),
        (own_ref[0], own_ref[1], own_out),
    ):
        low = jnp.where(straight, d0, d1)
        high = jnp.where(straight, d1, d0)
        part = jnp.dot(jnp.concatenate([low, high], axis=1), w, preferred_element_type=F32)

        @pl.when(pl.program_id(0) == 0)
        def _():
            out[...] = part

        @pl.when(pl.program_id(0) == 1)
        def _():
            out[...] += part


def back(place_at, own, oth0, oth1, win):
    _, count, width = oth0.shape
    dim = win.shape[4]
    whole = pl.BlockSpec((count, dim), lambda k, i, t: (0, 0))
    d_spec = pl.BlockSpec((None, count, width), lambda k, i, t: (k, 0, 0))
    return pl.pallas_call(
        back_kernel,
        grid_spec=pltpu.PrefetchScalarGridSpec(
            num_scalar_prefetch=2,
            grid=(2,),
            in_specs=[
                pl.BlockSpec((2, None, count, width), lambda k, i, t: (0, k, 0, 0)),
                d_spec,
                d_spec,
                pl.BlockSpec(
                    (None, 2, None, width, dim),
                    lambda k, i, t: (k, 0, field(i, t, CORE), 0, 0),
                ),
            ],
            out_specs=[whole, whole],
        ),
        out_shape=[jax.ShapeDtypeStruct((count, dim), F32)] * 2,
        compiler_params=pltpu.CompilerParams(vmem_limit_bytes=BACK_LIMIT),
        cost_estimate=pl.CostEstimate(
            flops=16 * count * dim * width, bytes_accessed=16 * 2**20, transcendentals=0
        ),
        name="back",
    )(*place_at, own, oth0, oth1, win)


def small_call(kernel, out_shape, name, place_at, *operands):
    return pl.pallas_call(
        kernel,
        grid_spec=pltpu.PrefetchScalarGridSpec(
            num_scalar_prefetch=2,
            grid=(1,),
            in_specs=[
                pl.BlockSpec(o.shape, functools.partial(lambda n, *_: (0,) * n, o.ndim))
                for o in operands
            ],
            out_specs=[
                pl.BlockSpec(o.shape, functools.partial(lambda n, *_: (0,) * n, len(o.shape)))
                for o in out_shape
            ],
        ),
        out_shape=out_shape,
        compiler_params=pltpu.CompilerParams(vmem_limit_bytes=SMALL_LIMIT),
        cost_estimate=pl.CostEstimate(flops=2**20, bytes_accessed=2**20, transcendentals=0),
        name=name,
    )(*place_at, *operands)


def sums_kernel(sizes, *refs):
    out = refs[-1]
    at = 0
    for i, size in enumerate(sizes):
        out[i, 0] = functools.reduce(lambda p, q: p + q, [r[0] for r in refs[at : at + size]])
        at += size


def sums(groups, rows, count, order=lambda i: i):
    lanes = groups[0][0][0].shape[-1]
    tile = min(rows, 160)
    operands, specs = [], []
    for group in groups:
        for array, first in group:
            operands.append(array.reshape(-1, rows, lanes))
            specs.append(
                pl.BlockSpec((1, tile, lanes), functools.partial(lambda f, i, j: (f + order(i), j, 0), first))
            )
    return pl.pallas_call(
        functools.partial(sums_kernel, [len(group) for group in groups]),
        grid=(count, rows // tile),
        in_specs=specs,
        out_specs=pl.BlockSpec((len(groups), 1, tile, lanes), lambda i, j: (0, i, j, 0)),
        out_shape=jax.ShapeDtypeStruct((len(groups), count, rows, lanes), F32),
        compiler_params=pltpu.CompilerParams(vmem_limit_bytes=SMALL_LIMIT),
        cost_estimate=pl.CostEstimate(
            flops=2**20, bytes_accessed=4 * 2**20, transcendentals=0
        ),
        name="sums",
    )(*operands)


def gather_kernel(factor, index, table, a0, a1, a2, b0, b1, b2, b3, c_ref, far_ref, out):
    tab = row_of(index, table)
    rows, half = c_ref.shape
    for i, ref in enumerate((b0, b1, b2, b3)):
        here = pl.ds(pl.multiple_of(tab[XAT + i] * rows, 8), rows)
        out[here, :half] = (a0[i] + a1[i] + a2[i]) * factor
        here = pl.ds(pl.multiple_of(lax.rem(tab[X] + i, 4) * rows, 8), rows)
        out[here, half:] = ref[...] * factor
    low = tab[OWN_HALF] == 0
    c, far = c_ref[...] * factor, far_ref[...] * factor
    out[4 * rows :, :half] = jnp.where(low, c, far)
    out[4 * rows :, half:] = jnp.where(low, far, c)


def last_kernel(index, table, own_ref, oth_ref, in_ref, out_ref):
    tab = row_of(index, table)
    count, half = in_ref.shape[0], in_ref.shape[1] // 2
    owner, zero = tab[IS_OWNER] == 1, tab[CORE] == 0
    in_ref[...] = jnp.where(owner, own_ref[:count], oth_ref[:count])
    own, oth = own_ref[count:], oth_ref[count:]
    for i in range(2):
        cut = slice(i * half, (i + 1) * half)
        out_ref[:, 2 * i * half : (2 * i + 1) * half] = jnp.where(zero, own[:, cut], oth[:, cut])
        out_ref[:, (2 * i + 1) * half : (2 * i + 2) * half] = jnp.where(
            zero, oth[:, cut], own[:, cut]
        )


def widen_kernel(n_ref, c_ref, n_out, c_out):
    n_out[...] = n_ref[...].astype(F32)
    c_out[...] = c_ref[...].astype(F32)


def widen(normed, cot):
    count, dim = normed.shape
    tile = pl.BlockSpec((count // 4, dim), lambda i: (i, 0))
    return pl.pallas_call(
        widen_kernel,
        grid=(4,),
        in_specs=[tile, tile],
        out_specs=[tile, tile],
        out_shape=[jax.ShapeDtypeStruct((count, dim), F32)] * 2,
        compiler_params=pltpu.CompilerParams(vmem_limit_bytes=OWN_LIMIT),
        cost_estimate=pl.CostEstimate(flops=2**20, bytes_accessed=8 * 2**20, transcendentals=0),
        name="widen",
    )(normed, cot)


def move(array, pairs):
    return lax.ppermute(array, AXES, pairs)


def total(terms):
    return functools.reduce(lambda p, q: p + q, terms)


def settle(array):
    return lax.optimization_barrier(array)


def twice(i):
    return 2 * i


def after(array, other):
    return lax.optimization_barrier((array, other))[0]


def local(normed, w_in, w_out, cotangent):
    dim = normed.shape[1]
    width = w_out.shape[1] // 4
    factor = (normed.shape[0] * lax.axis_size("dp") * lax.axis_size("grp")) ** (-0.5)
    index = lax.axis_index(AXES).reshape(1)
    place_at = index, jnp.asarray(TABLE.reshape(-1))
    win = w_in.reshape(2, 2, 2, width, dim)

    wide = widen(normed, cotangent)
    own = normed, cotangent
    other = move(wide[0], CORE_PAIRS), move(wide[1], CORE_PAIRS)
    terms = own_call(place_at, win, w_out, normed, cotangent)
    *first, oth0 = chunk_call(place_at, win, w_out, other, own, terms, 0)
    got_a0, got_b0, got_c0 = move(first[0], Z0), move(first[2], Y0), move(first[4], X0)
    index, _ = lax.optimization_barrier((index, first[0]))
    place_at = index, place_at[1]
    *second, oth1 = chunk_call(place_at, win, w_out, other, own, terms, 1)
    got_a1, got_b1, got_c1 = move(second[0], Z0), move(second[2], Y0), move(second[4], X0)

    oth0, index, got_a0, got_b0, early_c = lax.optimization_barrier(
        (oth0, index, got_a0, got_b0, first[5] + got_c0)
    )
    back_oth, back_own = back(place_at, terms[0], oth0, oth1, win)
    got_a1, back_own = lax.optimization_barrier((got_a1, back_own))
    grad_normed = (back_own + move(back_oth, CORE_PAIRS)).astype(BF)

    grp, dp = lax.axis_index("grp"), lax.axis_index("dp")
    own_first = ((dp >> 3) & 1) != ((grp >> 1) ^ (grp & (dp >> 2) & 1))

    rows = width // 2
    a = [second[1], got_a0]
    b = [first[3], got_b0], [second[3], got_b1]
    c = [early_c], [second[5], got_c1]
    to_a = total([first[1], got_a1])
    got_a = move(to_a, Z1)
    b[1][1] = after(got_b1, to_a)
    to_b = sums([[(t, 0) for t in chunk] for chunk in b], rows, 1)
    got_b = move(to_b, Y1)
    c[1][1] = got_c1 = after(got_c1, to_b)
    to_c = jnp.where(own_first, total([second[5], got_c1]), early_c)
    got_c = move(to_c, X1)
    a = [settle(total(a)), after(got_a, to_c)]
    b = [[(t, 4) for t in chunk] + [(got_b, 4 * k)] for k, chunk in enumerate(b)]
    c = [settle(jnp.where(own_first, total(c[0]), total(c[1]))), got_c]

    rows = width // 8
    to_a = total([t[:2] for t in a])
    got_a = move(to_a, Y0)
    a = [settle(total([t[2:] for t in a])), got_a]
    got_b = after(got_b, to_a)
    b = [chunk[:-1] + [(got_b, 4 * k)] for k, chunk in enumerate(b)]
    to_b = sums(b, rows, 2)
    got_b = move(to_b, X0)
    b = [sums([[(t, at + 2) for t, at in chunk] for chunk in b], rows, 2), got_b]
    c[-1] = after(c[-1], to_b)
    to_c = total([t[:2] for t in c])
    got_c = move(to_c, Z0)
    c = [settle(total([t[2:] for t in c])), got_c]

    a[-1] = after(a[-1], to_c)
    to_a = total([t[0] for t in a])
    got_a = move(to_a, Y1)
    b[-1] = after(b[-1], to_a)
    to_b = sums([[(t, 0) for t in b]], rows, 2, twice)
    got_b = move(to_b, X1)
    b = [sums([[(t, 1) for t in b]], rows, 2, twice), got_b]
    c[-1] = after(c[-1], to_b)
    to_c = total([t[0] for t in c])
    got_c = move(to_c, Z1)
    c = [t[1] for t in c] + [got_c]

    rows = width // 16
    a = [(t, 4) for t in a] + [(after(got_a, to_c), 0)]
    to_a = sums([a], rows, 4, lambda i: (i + 2) % 4)
    got_a = move(to_a, X0)
    kept, grad_normed = settle((sums([a], rows, 4), grad_normed))
    a = [(kept, 0), (got_a, 0)]
    b[-1] = after(b[-1], to_a)
    to_b = sums([[(t, 2) for t in b]], rows, 2, lambda i: -2 * i)
    got_b = move(to_b, Z0)
    b = [sums([[(t, 1) for t in b]], rows, 2, twice)[0], got_b[0]]
    c[-1] = after(c[-1], to_b)
    to_c = total([t[:2] for t in c])
    got_c = move(to_c, Y0)
    c = [t[2:] for t in c] + [got_c]

    a[1] = after(got_a, to_c), 0
    to_a = sums([a], rows, 4, lambda i: i + 1 - 2 * (i % 2))
    got_a = move(to_a, X1)
    b[-1] = after(b[-1], to_a)
    to_b = total([t[0] for t in b])
    got_b = move(to_b, Z1)
    c[-1] = after(c[-1], to_b)
    to_c = total([t[0] for t in c])
    got_c = move(to_c, Y1)

    b = total([t[1] for t in b] + [after(got_b, to_c)])
    b_rest = [move(b, owner_pairs(shift)) for shift in (1, 2, 3)]
    c = total([t[1] for t in c] + [after(got_c, b)])
    c_far = move(c, FAR_PAIRS)
    (packed_rows,) = small_call(
        functools.partial(gather_kernel, factor),
        [jax.ShapeDtypeStruct((5 * (dim // 32), dim), F32)],
        "gather",
        place_at,
        *(t[0] for t, _ in a),
        got_a[0],
        b,
        *b_rest,
        c,
        c_far,
    )
    grad_in, grad_out = small_call(
        last_kernel,
        [
            jax.ShapeDtypeStruct((width // 4, dim), F32),
            jax.ShapeDtypeStruct((dim // 32, 4 * width), F32),
        ],
        "last",
        place_at,
        packed_rows,
        move(packed_rows, CORE_PAIRS),
    )
    return (grad_in, grad_out, grad_normed)


def solution(mesh):
    placed = (P(AXES, None), P(), P(), P(AXES, None))
    return jax.shard_map(
        local,
        mesh=mesh,
        in_specs=placed,
        out_specs=(P("dp", None), P("dp", None), P(AXES, None)),
        check_vma=False,
    )
```

```python
import functools

import jax
import jax.numpy as jnp
import numpy as np
from jax import lax
from jax.experimental import pallas as pl
from jax.experimental.pallas import tpu as pltpu
from jax.sharding import PartitionSpec as P

AXES = ("grp", "dp")
BF = jnp.bfloat16
F32 = jnp.float32
OWN_LIMIT = 62 * 2**20
CHUNK_LIMIT = 62 * 2**20
BACK_LIMIT = 36 * 2**20
SMALL_LIMIT = 8 * 2**20


def place(x, y, z, c):
    return ((x // 2) * 2 + c) * 32 + z * 8 + (x % 2) * 4 + y


EVERY = [(x, y, z, c) for x in range(4) for y in range(4) for z in range(4) for c in range(2)]


def partner(i, core, step):
    return (i + (1 if i % 2 == (core + step) % 2 else -1)) % 4


def halving_pairs(axis, step):
    pairs = []
    for x, y, z, c in EVERY:
        at = [x, y, z]
        at[axis] = partner(at[axis], 1 - c if axis == 1 else c, step)
        pairs.append((place(x, y, z, c), place(*at, c)))
    return pairs


X0, X1 = halving_pairs(0, 0), halving_pairs(0, 1)
Y0, Y1 = halving_pairs(1, 0), halving_pairs(1, 1)
Z0, Z1 = halving_pairs(2, 0), halving_pairs(2, 1)
CORE_PAIRS = [(place(x, y, z, c), place(x, y, z, 1 - c)) for x, y, z, c in EVERY]
FAR_PAIRS = [(place(x, y, z, c), place((x + 2) % 4, y, z, c)) for x, y, z, c in EVERY]


def owns(x, core):
    return x % 2 == core


def owner_pairs(shift):
    return [
        (place((x + shift) % 4, y, z, c), place(x, y, z, c)) for x, y, z, c in EVERY if owns(x, c)
    ]


def ring_order(i, core):
    first, second = partner(i, core, 0), partner(i, core, 1)
    return [partner(first, core, 1), first, second, i]


CORE, CHUNK, KIND, HALF, XAT, YAT, ZAT = 0, 1, 3, 7, 9, 13, 17
OWN_HALF, X, IS_OWNER, WIDTH = 22, 23, 24, 32


def table():
    rows = np.zeros((len(EVERY), WIDTH), np.int32)
    for x, y, z, c in EVERY:
        row = rows[place(x, y, z, c)]
        row[CORE] = c
        xs, ys, zs = ring_order(x, c), ring_order(y, 1 - c), ring_order(z, c)
        row[CHUNK], row[CHUNK + 1] = 1 - z % 2, z % 2
        row[KIND : KIND + 4] = [zs[1] // 2, zs[2] // 2, zs[0] // 2, zs[3] // 2]
        labels = {i: (i % 2, i // 2 if c == 0 else (i // 2) ^ (i % 2)) for i in range(4)}
        for k in range(2):
            (row[HALF + k],) = [labels[i][0] for i in xs[2:] if labels[i][1] == row[CHUNK + k]]
        for at, order in ((XAT, xs), (YAT, ys), (ZAT, zs)):
            for rank, i in enumerate(order):
                row[at + rank] = i
        row[OWN_HALF] = labels[x][1]
        row[X] = x
        row[IS_OWNER] = int(owns(x, c))
    return rows


TWO_BITS = [*range(XAT, ZAT + 4), X]
FIELDS = {at: (0, 2 * i, 3) for i, at in enumerate(TWO_BITS)}
ONE_BIT = [CORE, CHUNK, CHUNK + 1, *range(KIND, KIND + 4), HALF, HALF + 1, OWN_HALF, IS_OWNER]
FIELDS.update({at: (1, i, 1) for i, at in enumerate(ONE_BIT)})


def packed():
    rows = table()
    words = np.zeros((len(EVERY), 2), np.int32)
    for at, (word, shift, _) in FIELDS.items():
        words[:, word] |= rows[:, at] << shift
    return words


TABLE = packed()


def field(index, table, at):
    word, shift, mask = FIELDS[at]
    return (table[index[0] * 2 + word] >> shift) & mask


NT = (((1,), (1,)), ((), ()))
TN = (((0,), (0,)), ((), ()))


def row_of(index, table):
    class Row:
        def __getitem__(self, at):
            return field(index, table, at)

    return Row()


def gated(value, gate, dact):
    cdf = 0.5 * (1.0 + lax.erf(gate * (2.0 ** -0.5)))
    density = jnp.exp(-0.5 * gate * gate) * ((2.0 * jnp.pi) ** -0.5)
    share = gate * cdf
    return (
        (value * share).astype(BF),
        (dact * share).astype(BF),
        (dact * value * (cdf + gate * density)).astype(BF),
    )


class Copies:
    def __init__(self, sems):
        self.sems, self.used = sems, 0

    def start(self, source, target):
        copy = pltpu.make_async_copy(source, target, self.sems.at[self.used])
        self.used += 1
        copy.start()
        return copy


def own_kernel(index, table, win, wout, n_in, c_in, d_out, act_out, w, wo, n, c, d, act, sems):
    tab = row_of(index, table)
    width = w.shape[2]
    copies = Copies(sems)
    load_w, load_wo = [], []
    for k in range(2):
        block, core = tab[CHUNK + k], tab[CORE]
        column = pl.multiple_of((block * 2 + core) * width, 128)
        load_wo.append(copies.start(wout.at[:, pl.ds(column, width)], wo.at[k]))
        if k == 0:
            load_c = copies.start(c_in, c)
        load_w.append([copies.start(win.at[i, block, core], w.at[k, i]) for i in range(2)])
        if k == 0:
            load_n = copies.start(n_in, n)
    stores = []
    for k in range(2):
        load_wo[k].wait()
        if k == 0:
            load_c.wait()
        dact = jnp.dot(c[...], wo[k], preferred_element_type=F32)
        for copy in load_w[k]:
            copy.wait()
        if k == 0:
            load_n.wait()
        proj = lax.dot_general(
            n[...], w[k].reshape(2 * width, w.shape[3]), NT, preferred_element_type=F32
        )
        act[k], d[k, 0], d[k, 1] = gated(proj[:, :width], proj[:, width:], dact)
        stores.append(copies.start(act.at[k], act_out.at[k]))
        stores.append(copies.start(d.at[k], d_out.at[k]))
    for copy in stores:
        copy.wait()


def own_call(place_at, win, wout, normed, cot):
    count, dim = normed.shape
    width = win.shape[3]
    anywhere = pl.BlockSpec(memory_space=pl.ANY)
    return pl.pallas_call(
        own_kernel,
        grid_spec=pltpu.PrefetchScalarGridSpec(
            num_scalar_prefetch=2,
            grid=(1,),
            in_specs=[anywhere] * 4,
            out_specs=[anywhere] * 2,
            scratch_shapes=[
                pltpu.VMEM((2, 2, width, dim), BF),
                pltpu.VMEM((2, dim, width), BF),
                pltpu.VMEM((count, dim), BF),
                pltpu.VMEM((count, dim), BF),
                pltpu.VMEM((2, 2, count, width), BF),
                pltpu.VMEM((2, count, width), BF),
                pltpu.SemaphoreType.DMA((12,)),
            ],
        ),
        out_shape=[
            jax.ShapeDtypeStruct((2, 2, count, width), BF),
            jax.ShapeDtypeStruct((2, count, width), BF),
        ],
        compiler_params=pltpu.CompilerParams(vmem_limit_bytes=OWN_LIMIT),
        cost_estimate=pl.CostEstimate(
            flops=12 * count * dim * width, bytes_accessed=16 * 2**20, transcendentals=0
        ),
        name="own_terms",
    )(*place_at, win, wout, normed, cot)


def chunk_kernel(
    chunk, index, table, win, wout, n_in, c_in, n_own, c_own, d_own, act_own,
    a_send, a_keep, b_send, b_keep, c_send, c_keep, d_out,
    w, wo, nb, cb, d, act, gin, gout, load_sems, sems,
):
    tab = row_of(index, table)
    width, dim = w.shape[1:]
    count = n_in.shape[0]
    half = dim // 2
    core, block = tab[CORE], tab[CHUNK + chunk]
    own, oth = pl.ds(count, count), pl.ds(0, count)
    loads = Copies(load_sems)
    column = pl.multiple_of((block * 2 + core) * width, 128)
    load_wo = loads.start(wout.at[:, pl.ds(column, width)], wo)
    lanes = [pl.ds(part * half, half) for part in range(2)]
    raw = gin.at[:, :, oth]
    load_c = [loads.start(c_in.at[:, lanes[i]], raw.at[0, i]) for i in range(2)]
    load_w = [loads.start(win.at[i, block, core], w.at[i]) for i in range(2)]
    load_n = [loads.start(n_in.at[:, lanes[i]], raw.at[1, i]) for i in range(2)]
    load_own = [loads.start(c_own, cb.at[own]), loads.start(act_own.at[chunk], act.at[own])]
    load_own += [loads.start(d_own.at[chunk, i], d.at[i, own]) for i in range(2)]
    load_own += [loads.start(n_own, nb.at[own])]

    def store(source, target, sem):
        pltpu.make_async_copy(source, target, sems.at[sem]).start()

    load_wo.wait()
    for i in range(2):
        load_c[i].wait()
        cb[oth, i * half : (i + 1) * half] = raw[0, i].astype(BF)
    dact = jnp.dot(cb[oth], wo[...], preferred_element_type=F32)
    for i in range(2):
        load_n[i].wait()
        nb[oth, i * half : (i + 1) * half] = raw[1, i].astype(BF)
    for copy in load_w:
        copy.wait()
    proj = lax.dot_general(
        nb[oth], w[...].reshape(2 * width, dim), NT, preferred_element_type=F32
    )
    act[oth], d[0, oth], d[1, oth] = gated(proj[:, :width], proj[:, width:], dact)
    for i in range(2):
        store(d.at[i, oth], d_out.at[i], 0)
    for copy in load_own:
        copy.wait()

    gout[...] = lax.dot_general(cb[...], act[...], TN, preferred_element_type=F32)
    tiny = dim // 32
    kept = tab[HALF + chunk]
    for out, x, sem in ((c_send, 1 - kept, 1), (c_keep, kept, 2)):
        for z in range(4):
            for y in range(4):
                at = ((tab[ZAT + z] * 2 + x) * 4 + tab[YAT + y]) * tiny
                store(gout.at[pl.ds(pl.multiple_of(at, 8), tiny)], out.at[z, y], sem)
    small = width // 16
    for slot, out in enumerate((a_send, a_keep)):
        kind = tab[KIND + 2 * chunk + slot]
        for part in range(2):
            cut = slice(part * half, (part + 1) * half)
            gin[slot, part] = lax.dot_general(
                d[kind], nb[:, cut], TN, preferred_element_type=F32
            )
            for y in range(4):
                for x in range(4):
                    at = (tab[YAT + y] * 4 + tab[XAT + x]) * small
                    rows = gin.at[slot, part, pl.ds(pl.multiple_of(at, 8), small)]
                    if part == 0:
                        store(rows, out.at[y, x], 3 + slot)
                    else:
                        store(rows, (b_send, b_keep)[y // 2].at[y % 2, x, slot], 5 + y // 2)
    outs = (d_out, c_send, c_keep, a_send, a_keep, b_send, b_keep)
    for i, out in enumerate(outs):
        pltpu.make_async_copy(out, out, sems.at[i]).wait()


def chunk_call(place_at, win, wout, other, own, terms, chunk):
    count, dim = own[0].shape
    width = win.shape[3]
    a = jax.ShapeDtypeStruct((4, 4, width // 16, dim // 2), F32)
    b = jax.ShapeDtypeStruct((2, 4, 2, width // 16, dim // 2), F32)
    c = jax.ShapeDtypeStruct((4, 4, dim // 32, width), F32)
    outs = [a, a, b, b, c, c, jax.ShapeDtypeStruct((2, count, width), BF)]
    operands = [win, wout, *other, *own, *terms]
    anywhere = pl.BlockSpec(memory_space=pl.ANY)
    return pl.pallas_call(
        functools.partial(chunk_kernel, chunk),
        grid_spec=pltpu.PrefetchScalarGridSpec(
            num_scalar_prefetch=2,
            grid=(1,),
            in_specs=[anywhere] * len(operands),
            out_specs=[anywhere] * len(outs),
            scratch_shapes=[
                pltpu.VMEM((2, width, dim), BF),
                pltpu.VMEM((dim, width), BF),
                pltpu.VMEM((2 * count, dim), BF),
                pltpu.VMEM((2 * count, dim), BF),
                pltpu.VMEM((2, 2 * count, width), BF),
                pltpu.VMEM((2 * count, width), BF),
                pltpu.VMEM((2, 2, width, dim // 2), F32),
                pltpu.VMEM((dim, width), F32),
                pltpu.SemaphoreType.DMA((12,)),
                pltpu.SemaphoreType.DMA((7,)),
            ],
        ),
        out_shape=outs,
        compiler_params=pltpu.CompilerParams(vmem_limit_bytes=CHUNK_LIMIT),
        cost_estimate=pl.CostEstimate(
            flops=16 * count * dim * width, bytes_accessed=16 * 2**20, transcendentals=0
        ),
        name="chunk",
    )(*place_at, *operands)


def back_kernel(index, table, own_ref, oth0_ref, oth1_ref, w_ref, oth_out, own_out):
    tab = row_of(index, table)
    w = w_ref[...].reshape(2 * w_ref.shape[1], w_ref.shape[2])
    straight = tab[CHUNK] == 0
    for d0, d1, out in (
        (oth0_ref[...], oth1_ref[...], oth_out),
        (own_ref[0], own_ref[1], own_out),
    ):
        low = jnp.where(straight, d0, d1)
        high = jnp.where(straight, d1, d0)
        part = jnp.dot(jnp.concatenate([low, high], axis=1), w, preferred_element_type=F32)

        @pl.when(pl.program_id(0) == 0)
        def _():
            out[...] = part

        @pl.when(pl.program_id(0) == 1)
        def _():
            out[...] += part


def back(place_at, own, oth0, oth1, win):
    _, count, width = oth0.shape
    dim = win.shape[4]
    whole = pl.BlockSpec((count, dim), lambda k, i, t: (0, 0))
    d_spec = pl.BlockSpec((None, count, width), lambda k, i, t: (k, 0, 0))
    return pl.pallas_call(
        back_kernel,
        grid_spec=pltpu.PrefetchScalarGridSpec(
            num_scalar_prefetch=2,
            grid=(2,),
            in_specs=[
                pl.BlockSpec((2, None, count, width), lambda k, i, t: (0, k, 0, 0)),
                d_spec,
                d_spec,
                pl.BlockSpec(
                    (None, 2, None, width, dim),
                    lambda k, i, t: (k, 0, field(i, t, CORE), 0, 0),
                ),
            ],
            out_specs=[whole, whole],
        ),
        out_shape=[jax.ShapeDtypeStruct((count, dim), F32)] * 2,
        compiler_params=pltpu.CompilerParams(vmem_limit_bytes=BACK_LIMIT),
        cost_estimate=pl.CostEstimate(
            flops=16 * count * dim * width, bytes_accessed=16 * 2**20, transcendentals=0
        ),
        name="back",
    )(*place_at, own, oth0, oth1, win)


def small_call(kernel, out_shape, name, place_at, *operands):
    return pl.pallas_call(
        kernel,
        grid_spec=pltpu.PrefetchScalarGridSpec(
            num_scalar_prefetch=2,
            grid=(1,),
            in_specs=[
                pl.BlockSpec(o.shape, functools.partial(lambda n, *_: (0,) * n, o.ndim))
                for o in operands
            ],
            out_specs=[
                pl.BlockSpec(o.shape, functools.partial(lambda n, *_: (0,) * n, len(o.shape)))
                for o in out_shape
            ],
        ),
        out_shape=out_shape,
        compiler_params=pltpu.CompilerParams(vmem_limit_bytes=SMALL_LIMIT),
        cost_estimate=pl.CostEstimate(flops=2**20, bytes_accessed=2**20, transcendentals=0),
        name=name,
    )(*place_at, *operands)


def sums_kernel(sizes, *refs):
    out = refs[-1]
    at = 0
    for i, size in enumerate(sizes):
        out[i, 0] = functools.reduce(lambda p, q: p + q, [r[0] for r in refs[at : at + size]])
        at += size


def sums(groups, rows, count, order=lambda i: i):
    lanes = groups[0][0][0].shape[-1]
    tile = min(rows, 160)
    operands, specs = [], []
    for group in groups:
        for array, first in group:
            operands.append(array.reshape(-1, rows, lanes))
            specs.append(
                pl.BlockSpec((1, tile, lanes), functools.partial(lambda f, i, j: (f + order(i), j, 0), first))
            )
    return pl.pallas_call(
        functools.partial(sums_kernel, [len(group) for group in groups]),
        grid=(count, rows // tile),
        in_specs=specs,
        out_specs=pl.BlockSpec((len(groups), 1, tile, lanes), lambda i, j: (0, i, j, 0)),
        out_shape=jax.ShapeDtypeStruct((len(groups), count, rows, lanes), F32),
        compiler_params=pltpu.CompilerParams(vmem_limit_bytes=SMALL_LIMIT),
        cost_estimate=pl.CostEstimate(
            flops=2**20, bytes_accessed=4 * 2**20, transcendentals=0
        ),
        name="sums",
    )(*operands)


def gather_kernel(factor, index, table, a0, a1, a2, b0, b1, b2, b3, c_ref, far_ref, out):
    tab = row_of(index, table)
    rows, half = c_ref.shape
    for i, ref in enumerate((b0, b1, b2, b3)):
        here = pl.ds(pl.multiple_of(tab[XAT + i] * rows, 8), rows)
        out[here, :half] = (a0[i] + a1[i] + a2[i]) * factor
        here = pl.ds(pl.multiple_of(lax.rem(tab[X] + i, 4) * rows, 8), rows)
        out[here, half:] = ref[...] * factor
    low = tab[OWN_HALF] == 0
    c, far = c_ref[...] * factor, far_ref[...] * factor
    out[4 * rows :, :half] = jnp.where(low, c, far)
    out[4 * rows :, half:] = jnp.where(low, far, c)


def last_kernel(index, table, own_ref, oth_ref, in_ref, out_ref):
    tab = row_of(index, table)
    count, half = in_ref.shape[0], in_ref.shape[1] // 2
    owner, zero = tab[IS_OWNER] == 1, tab[CORE] == 0
    in_ref[...] = jnp.where(owner, own_ref[:count], oth_ref[:count])
    own, oth = own_ref[count:], oth_ref[count:]
    for i in range(2):
        cut = slice(i * half, (i + 1) * half)
        out_ref[:, 2 * i * half : (2 * i + 1) * half] = jnp.where(zero, own[:, cut], oth[:, cut])
        out_ref[:, (2 * i + 1) * half : (2 * i + 2) * half] = jnp.where(
            zero, oth[:, cut], own[:, cut]
        )


def widen_kernel(n_ref, c_ref, n_out, c_out):
    n_out[...] = n_ref[...].astype(F32)
    c_out[...] = c_ref[...].astype(F32)


def widen(normed, cot):
    count, dim = normed.shape
    tile = pl.BlockSpec((count // 4, dim), lambda i: (i, 0))
    return pl.pallas_call(
        widen_kernel,
        grid=(4,),
        in_specs=[tile, tile],
        out_specs=[tile, tile],
        out_shape=[jax.ShapeDtypeStruct((count, dim), F32)] * 2,
        compiler_params=pltpu.CompilerParams(vmem_limit_bytes=OWN_LIMIT),
        cost_estimate=pl.CostEstimate(flops=2**20, bytes_accessed=8 * 2**20, transcendentals=0),
        name="widen",
    )(normed, cot)


def move(array, pairs):
    return lax.ppermute(array, AXES, pairs)


def total(terms):
    return functools.reduce(lambda p, q: p + q, terms)


def settle(array):
    return lax.optimization_barrier(array)


def twice(i):
    return 2 * i


def after(array, other):
    return lax.optimization_barrier((array, other))[0]


def local(normed, w_in, w_out, cotangent):
    dim = normed.shape[1]
    width = w_out.shape[1] // 4
    factor = (normed.shape[0] * lax.axis_size("dp") * lax.axis_size("grp")) ** (-0.5)
    index = lax.axis_index(AXES).reshape(1)
    place_at = index, jnp.asarray(TABLE.reshape(-1))
    win = w_in.reshape(2, 2, 2, width, dim)

    wide = widen(normed, cotangent)
    own = normed, cotangent
    other = move(wide[0], CORE_PAIRS), move(wide[1], CORE_PAIRS)
    terms = own_call(place_at, win, w_out, normed, cotangent)
    *first, oth0 = chunk_call(place_at, win, w_out, other, own, terms, 0)
    got_a0, got_b0, got_c0 = move(first[0], Z0), move(first[2], Y0), move(first[4], X0)
    index, _ = lax.optimization_barrier((index, first[0]))
    place_at = index, place_at[1]
    *second, oth1 = chunk_call(place_at, win, w_out, other, own, terms, 1)
    got_a1, got_b1, got_c1 = move(second[0], Z0), move(second[2], Y0), move(second[4], X0)

    oth0, index, got_a0, got_b0, early_c = lax.optimization_barrier(
        (oth0, index, got_a0, got_b0, first[5] + got_c0)
    )
    back_oth, back_own = back(place_at, terms[0], oth0, oth1, win)
    got_b1, back_own = lax.optimization_barrier((got_b1, back_own))
    grad_normed = (back_own + move(back_oth, CORE_PAIRS)).astype(BF)

    grp, dp = lax.axis_index("grp"), lax.axis_index("dp")
    own_first = ((dp >> 3) & 1) != ((grp >> 1) ^ (grp & (dp >> 2) & 1))

    rows = width // 2
    a = [second[1], got_a0]
    b = [first[3], got_b0], [second[3], got_b1]
    c = [early_c], [second[5], got_c1]
    to_b = sums([[(t, 0) for t in chunk] for chunk in b], rows, 1)
    got_b = move(to_b, Y1)
    c[1][1] = got_c1 = after(got_c1, to_b)
    to_c = jnp.where(own_first, total([second[5], got_c1]), early_c)
    got_c = move(to_c, X1)
    to_a = total([first[1], after(got_a1, to_c)])
    got_a = move(to_a, Z1)
    a = [settle(total(a)), got_a]
    b = [[(t, 4) for t in chunk] + [(got_b, 4 * k)] for k, chunk in enumerate(b)]
    c = [settle(jnp.where(own_first, total(c[0]), total(c[1]))), got_c]

    rows = width // 8
    to_b = sums(b, rows, 2)
    got_b = move(to_b, X0)
    b = [sums([[(t, at + 2) for t, at in chunk] for chunk in b], rows, 2), got_b]
    c[-1] = after(c[-1], to_b)
    to_c = total([t[:2] for t in c])
    got_c = move(to_c, Z0)
    c = [settle(total([t[2:] for t in c])), got_c]
    a[-1] = after(a[-1], to_c)
    to_a = total([t[:2] for t in a])
    got_a = move(to_a, Y0)
    kept, grad_normed = settle((total([t[2:] for t in a]), grad_normed))
    a = [kept, got_a]

    b[-1] = after(b[-1], to_a)
    to_b = sums([[(t, 0) for t in b]], rows, 2, twice)
    got_b = move(to_b, X1)
    b = [sums([[(t, 1) for t in b]], rows, 2, twice), got_b]
    c[-1] = after(c[-1], to_b)
    to_c = total([t[0] for t in c])
    got_c = move(to_c, Z1)
    c = [t[1] for t in c] + [got_c]
    a[-1] = after(a[-1], to_c)
    to_a = total([t[0] for t in a])
    got_a = move(to_a, Y1)

    rows = width // 16
    b[-1] = after(b[-1], to_a)
    to_b = sums([[(t, 2) for t in b]], rows, 2, lambda i: -2 * i)
    got_b = move(to_b, Z0)
    b = [sums([[(t, 1) for t in b]], rows, 2, twice)[0], got_b[0]]
    c[-1] = after(c[-1], to_b)
    to_c = total([t[:2] for t in c])
    got_c = move(to_c, Y0)
    c = [t[2:] for t in c] + [got_c]
    a = [(t, 4) for t in a] + [(after(got_a, to_c), 0)]
    to_a = sums([a], rows, 4, lambda i: (i + 2) % 4)
    got_a = move(to_a, X0)
    a = [(sums([a], rows, 4), 0), (got_a, 0)]

    b[-1] = after(b[-1], to_a)
    to_b = total([t[0] for t in b])
    got_b = move(to_b, Z1)
    c[-1] = after(c[-1], to_b)
    to_c = total([t[0] for t in c])
    got_c = move(to_c, Y1)
    a[1] = after(got_a, to_c), 0
    to_a = sums([a], rows, 4, lambda i: i + 1 - 2 * (i % 2))
    got_a = move(to_a, X1)

    b = total([t[1] for t in b] + [after(got_b, to_a)])
    c = total([t[1] for t in c] + [after(got_c, to_a)])
    c_far = move(c, FAR_PAIRS)
    (packed_rows,) = small_call(
        functools.partial(gather_kernel, factor),
        [jax.ShapeDtypeStruct((5 * (dim // 32), dim), F32)],
        "gather",
        place_at,
        *(t[0] for t, _ in a),
        got_a[0],
        b,
        *(move(b, owner_pairs(shift)) for shift in (1, 2, 3)),
        c,
        c_far,
    )
    grad_in, grad_out = small_call(
        last_kernel,
        [
            jax.ShapeDtypeStruct((width // 4, dim), F32),
            jax.ShapeDtypeStruct((dim // 32, 4 * width), F32),
        ],
        "last",
        place_at,
        packed_rows,
        move(packed_rows, CORE_PAIRS),
    )
    return (grad_in, grad_out, grad_normed)


def solution(mesh):
    placed = (P(AXES, None), P(), P(), P(AXES, None))
    return jax.shard_map(
        local,
        mesh=mesh,
        in_specs=placed,
        out_specs=(P("dp", None), P("dp", None), P(AXES, None)),
        check_vma=False,
    )
```

```python
import functools

import jax
import jax.numpy as jnp
import numpy as np
from jax import lax
from jax.experimental import pallas as pl
from jax.experimental.pallas import tpu as pltpu
from jax.sharding import PartitionSpec as P

AXES = ("grp", "dp")
BF = jnp.bfloat16
F32 = jnp.float32
OWN_LIMIT = 62 * 2**20
CHUNK_LIMIT = 62 * 2**20
BACK_LIMIT = 36 * 2**20
SMALL_LIMIT = 8 * 2**20


def place(x, y, z, c):
    return ((x // 2) * 2 + c) * 32 + z * 8 + (x % 2) * 4 + y


EVERY = [(x, y, z, c) for x in range(4) for y in range(4) for z in range(4) for c in range(2)]


def partner(i, core, step):
    return (i + (1 if i % 2 == (core + step) % 2 else -1)) % 4


def halving_pairs(axis, step):
    pairs = []
    for x, y, z, c in EVERY:
        at = [x, y, z]
        at[axis] = partner(at[axis], c, step)
        pairs.append((place(x, y, z, c), place(*at, c)))
    return pairs


X0, X1 = halving_pairs(0, 0), halving_pairs(0, 1)
Y0, Y1 = halving_pairs(1, 0), halving_pairs(1, 1)
Z0, Z1 = halving_pairs(2, 0), halving_pairs(2, 1)
CORE_PAIRS = [(place(x, y, z, c), place(x, y, z, 1 - c)) for x, y, z, c in EVERY]
FAR_PAIRS = [(place(x, y, z, c), place((x + 2) % 4, y, z, c)) for x, y, z, c in EVERY]


def owns(x, core):
    return x % 2 == core


def owner_pairs(shift):
    return [
        (place((x + shift) % 4, y, z, c), place(x, y, z, c)) for x, y, z, c in EVERY if owns(x, c)
    ]


def ring_order(i, core):
    first, second = partner(i, core, 0), partner(i, core, 1)
    return [partner(first, core, 1), first, second, i]


CORE, CHUNK, KIND, HALF, XAT, YAT, ZAT = 0, 1, 3, 7, 9, 13, 17
OWN_HALF, X, IS_OWNER, WIDTH = 22, 23, 24, 32


def table():
    rows = np.zeros((len(EVERY), WIDTH), np.int32)
    for x, y, z, c in EVERY:
        row = rows[place(x, y, z, c)]
        row[CORE] = c
        xs, ys, zs = ring_order(x, c), ring_order(y, c), ring_order(z, c)
        row[CHUNK], row[CHUNK + 1] = 1 - z % 2, z % 2
        row[KIND : KIND + 4] = [zs[1] // 2, zs[2] // 2, zs[0] // 2, zs[3] // 2]
        labels = {i: (i % 2, i // 2 if c == 0 else (i // 2) ^ (i % 2)) for i in range(4)}
        for k in range(2):
            (row[HALF + k],) = [labels[i][0] for i in xs[2:] if labels[i][1] == row[CHUNK + k]]
        for at, order in ((XAT, xs), (YAT, ys), (ZAT, zs)):
            for rank, i in enumerate(order):
                row[at + rank] = i
        row[OWN_HALF] = labels[x][1]
        row[X] = x
        row[IS_OWNER] = int(owns(x, c))
    return rows


TWO_BITS = [*range(XAT, ZAT + 4), X]
FIELDS = {at: (0, 2 * i, 3) for i, at in enumerate(TWO_BITS)}
ONE_BIT = [CORE, CHUNK, CHUNK + 1, *range(KIND, KIND + 4), HALF, HALF + 1, OWN_HALF, IS_OWNER]
FIELDS.update({at: (1, i, 1) for i, at in enumerate(ONE_BIT)})


def packed():
    rows = table()
    words = np.zeros((len(EVERY), 2), np.int32)
    for at, (word, shift, _) in FIELDS.items():
        words[:, word] |= rows[:, at] << shift
    return words


TABLE = packed()


def field(index, table, at):
    word, shift, mask = FIELDS[at]
    return (table[index[0] * 2 + word] >> shift) & mask


NT = (((1,), (1,)), ((), ()))
TN = (((0,), (0,)), ((), ()))


def row_of(index, table):
    class Row:
        def __getitem__(self, at):
            return field(index, table, at)

    return Row()


def gated(value, gate, dact):
    cdf = 0.5 * (1.0 + lax.erf(gate * (2.0 ** -0.5)))
    density = jnp.exp(-0.5 * gate * gate) * ((2.0 * jnp.pi) ** -0.5)
    share = gate * cdf
    return (
        (value * share).astype(BF),
        (dact * share).astype(BF),
        (dact * value * (cdf + gate * density)).astype(BF),
    )


class Copies:
    def __init__(self, sems):
        self.sems, self.used = sems, 0

    def start(self, source, target):
        copy = pltpu.make_async_copy(source, target, self.sems.at[self.used])
        self.used += 1
        copy.start()
        return copy


def own_kernel(index, table, win, wout, n_in, c_in, d_out, act_out, w, wo, n, c, d, act, sems):
    tab = row_of(index, table)
    width = w.shape[2]
    copies = Copies(sems)
    load_w, load_wo = [], []
    for k in range(2):
        block, core = tab[CHUNK + k], tab[CORE]
        column = pl.multiple_of((block * 2 + core) * width, 128)
        load_wo.append(copies.start(wout.at[:, pl.ds(column, width)], wo.at[k]))
        if k == 0:
            load_c = copies.start(c_in, c)
        load_w.append([copies.start(win.at[i, block, core], w.at[k, i]) for i in range(2)])
        if k == 0:
            load_n = copies.start(n_in, n)
    stores = []
    for k in range(2):
        load_wo[k].wait()
        if k == 0:
            load_c.wait()
        dact = jnp.dot(c[...], wo[k], preferred_element_type=F32)
        for copy in load_w[k]:
            copy.wait()
        if k == 0:
            load_n.wait()
        proj = lax.dot_general(
            n[...], w[k].reshape(2 * width, w.shape[3]), NT, preferred_element_type=F32
        )
        act[k], d[k, 0], d[k, 1] = gated(proj[:, :width], proj[:, width:], dact)
        stores.append(copies.start(act.at[k], act_out.at[k]))
        stores.append(copies.start(d.at[k], d_out.at[k]))
    for copy in stores:
        copy.wait()


def own_call(place_at, win, wout, normed, cot):
    count, dim = normed.shape
    width = win.shape[3]
    anywhere = pl.BlockSpec(memory_space=pl.ANY)
    return pl.pallas_call(
        own_kernel,
        grid_spec=pltpu.PrefetchScalarGridSpec(
            num_scalar_prefetch=2,
            grid=(1,),
            in_specs=[anywhere] * 4,
            out_specs=[anywhere] * 2,
            scratch_shapes=[
                pltpu.VMEM((2, 2, width, dim), BF),
                pltpu.VMEM((2, dim, width), BF),
                pltpu.VMEM((count, dim), BF),
                pltpu.VMEM((count, dim), BF),
                pltpu.VMEM((2, 2, count, width), BF),
                pltpu.VMEM((2, count, width), BF),
                pltpu.SemaphoreType.DMA((12,)),
            ],
        ),
        out_shape=[
            jax.ShapeDtypeStruct((2, 2, count, width), BF),
            jax.ShapeDtypeStruct((2, count, width), BF),
        ],
        compiler_params=pltpu.CompilerParams(vmem_limit_bytes=OWN_LIMIT),
        cost_estimate=pl.CostEstimate(
            flops=12 * count * dim * width, bytes_accessed=16 * 2**20, transcendentals=0
        ),
        name="own_terms",
    )(*place_at, win, wout, normed, cot)


def chunk_kernel(
    chunk, index, table, win, wout, n_in, c_in, n_own, c_own, d_own, act_own,
    a_send, a_keep, b_send, b_keep, c_send, c_keep, d_out,
    w, wo, nb, cb, d, act, gin, gout, load_sems, sems,
):
    tab = row_of(index, table)
    width, dim = w.shape[1:]
    count = n_in.shape[0]
    half = dim // 2
    core, block = tab[CORE], tab[CHUNK + chunk]
    own, oth = pl.ds(count, count), pl.ds(0, count)
    loads = Copies(load_sems)
    column = pl.multiple_of((block * 2 + core) * width, 128)
    load_wo = loads.start(wout.at[:, pl.ds(column, width)], wo)
    lanes = [pl.ds(part * half, half) for part in range(2)]
    raw = gin.at[:, :, oth]
    load_c = [loads.start(c_in.at[:, lanes[i]], raw.at[0, i]) for i in range(2)]
    load_w = [loads.start(win.at[i, block, core], w.at[i]) for i in range(2)]
    load_n = [loads.start(n_in.at[:, lanes[i]], raw.at[1, i]) for i in range(2)]
    load_own = [loads.start(c_own, cb.at[own]), loads.start(act_own.at[chunk], act.at[own])]
    load_own += [loads.start(d_own.at[chunk, i], d.at[i, own]) for i in range(2)]
    load_own += [loads.start(n_own, nb.at[own])]

    def store(source, target, sem):
        pltpu.make_async_copy(source, target, sems.at[sem]).start()

    load_wo.wait()
    for i in range(2):
        load_c[i].wait()
        cb[oth, i * half : (i + 1) * half] = raw[0, i].astype(BF)
    dact = jnp.dot(cb[oth], wo[...], preferred_element_type=F32)
    for i in range(2):
        load_n[i].wait()
        nb[oth, i * half : (i + 1) * half] = raw[1, i].astype(BF)
    for copy in load_w:
        copy.wait()
    proj = lax.dot_general(
        nb[oth], w[...].reshape(2 * width, dim), NT, preferred_element_type=F32
    )
    act[oth], d[0, oth], d[1, oth] = gated(proj[:, :width], proj[:, width:], dact)
    for i in range(2):
        store(d.at[i, oth], d_out.at[i], 0)
    for copy in load_own:
        copy.wait()

    gout[...] = lax.dot_general(cb[...], act[...], TN, preferred_element_type=F32)
    tiny = dim // 32
    kept = tab[HALF + chunk]
    for out, x, sem in ((c_send, 1 - kept, 1), (c_keep, kept, 2)):
        for z in range(4):
            for y in range(4):
                at = ((tab[ZAT + z] * 2 + x) * 4 + tab[YAT + y]) * tiny
                store(gout.at[pl.ds(pl.multiple_of(at, 8), tiny)], out.at[z, y], sem)
    small = width // 16
    for slot, out in enumerate((a_send, a_keep)):
        kind = tab[KIND + 2 * chunk + slot]
        for part in range(2):
            cut = slice(part * half, (part + 1) * half)
            gin[slot, part] = lax.dot_general(
                d[kind], nb[:, cut], TN, preferred_element_type=F32
            )
            for y in range(4):
                for x in range(4):
                    at = (tab[YAT + y] * 4 + tab[XAT + x]) * small
                    rows = gin.at[slot, part, pl.ds(pl.multiple_of(at, 8), small)]
                    if part == 0:
                        store(rows, out.at[y, x], 3 + slot)
                    else:
                        store(rows, (b_send, b_keep)[y // 2].at[y % 2, x, slot], 5 + y // 2)
    outs = (d_out, c_send, c_keep, a_send, a_keep, b_send, b_keep)
    for i, out in enumerate(outs):
        pltpu.make_async_copy(out, out, sems.at[i]).wait()


def chunk_call(place_at, win, wout, other, own, terms, chunk):
    count, dim = own[0].shape
    width = win.shape[3]
    a = jax.ShapeDtypeStruct((4, 4, width // 16, dim // 2), F32)
    b = jax.ShapeDtypeStruct((2, 4, 2, width // 16, dim // 2), F32)
    c = jax.ShapeDtypeStruct((4, 4, dim // 32, width), F32)
    outs = [a, a, b, b, c, c, jax.ShapeDtypeStruct((2, count, width), BF)]
    operands = [win, wout, *other, *own, *terms]
    anywhere = pl.BlockSpec(memory_space=pl.ANY)
    return pl.pallas_call(
        functools.partial(chunk_kernel, chunk),
        grid_spec=pltpu.PrefetchScalarGridSpec(
            num_scalar_prefetch=2,
            grid=(1,),
            in_specs=[anywhere] * len(operands),
            out_specs=[anywhere] * len(outs),
            scratch_shapes=[
                pltpu.VMEM((2, width, dim), BF),
                pltpu.VMEM((dim, width), BF),
                pltpu.VMEM((2 * count, dim), BF),
                pltpu.VMEM((2 * count, dim), BF),
                pltpu.VMEM((2, 2 * count, width), BF),
                pltpu.VMEM((2 * count, width), BF),
                pltpu.VMEM((2, 2, width, dim // 2), F32),
                pltpu.VMEM((dim, width), F32),
                pltpu.SemaphoreType.DMA((12,)),
                pltpu.SemaphoreType.DMA((7,)),
            ],
        ),
        out_shape=outs,
        compiler_params=pltpu.CompilerParams(vmem_limit_bytes=CHUNK_LIMIT),
        cost_estimate=pl.CostEstimate(
            flops=16 * count * dim * width, bytes_accessed=16 * 2**20, transcendentals=0
        ),
        name="chunk",
    )(*place_at, *operands)


def back_kernel(index, table, own_ref, oth0_ref, oth1_ref, w_ref, oth_out, own_out):
    tab = row_of(index, table)
    w = w_ref[...].reshape(2 * w_ref.shape[1], w_ref.shape[2])
    straight = tab[CHUNK] == 0
    for d0, d1, out in (
        (oth0_ref[...], oth1_ref[...], oth_out),
        (own_ref[0], own_ref[1], own_out),
    ):
        low = jnp.where(straight, d0, d1)
        high = jnp.where(straight, d1, d0)
        part = jnp.dot(jnp.concatenate([low, high], axis=1), w, preferred_element_type=F32)

        @pl.when(pl.program_id(0) == 0)
        def _():
            out[...] = part

        @pl.when(pl.program_id(0) == 1)
        def _():
            out[...] += part


def back(place_at, own, oth0, oth1, win):
    _, count, width = oth0.shape
    dim = win.shape[4]
    whole = pl.BlockSpec((count, dim), lambda k, i, t: (0, 0))
    d_spec = pl.BlockSpec((None, count, width), lambda k, i, t: (k, 0, 0))
    return pl.pallas_call(
        back_kernel,
        grid_spec=pltpu.PrefetchScalarGridSpec(
            num_scalar_prefetch=2,
            grid=(2,),
            in_specs=[
                pl.BlockSpec((2, None, count, width), lambda k, i, t: (0, k, 0, 0)),
                d_spec,
                d_spec,
                pl.BlockSpec(
                    (None, 2, None, width, dim),
                    lambda k, i, t: (k, 0, field(i, t, CORE), 0, 0),
                ),
            ],
            out_specs=[whole, whole],
        ),
        out_shape=[jax.ShapeDtypeStruct((count, dim), F32)] * 2,
        compiler_params=pltpu.CompilerParams(vmem_limit_bytes=BACK_LIMIT),
        cost_estimate=pl.CostEstimate(
            flops=16 * count * dim * width, bytes_accessed=16 * 2**20, transcendentals=0
        ),
        name="back",
    )(*place_at, own, oth0, oth1, win)


def small_call(kernel, out_shape, name, place_at, *operands):
    return pl.pallas_call(
        kernel,
        grid_spec=pltpu.PrefetchScalarGridSpec(
            num_scalar_prefetch=2,
            grid=(1,),
            in_specs=[
                pl.BlockSpec(o.shape, functools.partial(lambda n, *_: (0,) * n, o.ndim))
                for o in operands
            ],
            out_specs=[
                pl.BlockSpec(o.shape, functools.partial(lambda n, *_: (0,) * n, len(o.shape)))
                for o in out_shape
            ],
        ),
        out_shape=out_shape,
        compiler_params=pltpu.CompilerParams(vmem_limit_bytes=SMALL_LIMIT),
        cost_estimate=pl.CostEstimate(flops=2**20, bytes_accessed=2**20, transcendentals=0),
        name=name,
    )(*place_at, *operands)


def sums_kernel(sizes, *refs):
    out = refs[-1]
    at = 0
    for i, size in enumerate(sizes):
        out[i, 0] = functools.reduce(lambda p, q: p + q, [r[0] for r in refs[at : at + size]])
        at += size


def sums(groups, rows, count, order=lambda i: i):
    lanes = groups[0][0][0].shape[-1]
    tile = min(rows, 160)
    operands, specs = [], []
    for group in groups:
        for array, first in group:
            operands.append(array.reshape(-1, rows, lanes))
            specs.append(
                pl.BlockSpec((1, tile, lanes), functools.partial(lambda f, i, j: (f + order(i), j, 0), first))
            )
    return pl.pallas_call(
        functools.partial(sums_kernel, [len(group) for group in groups]),
        grid=(count, rows // tile),
        in_specs=specs,
        out_specs=pl.BlockSpec((len(groups), 1, tile, lanes), lambda i, j: (0, i, j, 0)),
        out_shape=jax.ShapeDtypeStruct((len(groups), count, rows, lanes), F32),
        compiler_params=pltpu.CompilerParams(vmem_limit_bytes=SMALL_LIMIT),
        cost_estimate=pl.CostEstimate(
            flops=2**20, bytes_accessed=4 * 2**20, transcendentals=0
        ),
        name="sums",
    )(*operands)


def gather_kernel(factor, index, table, a0, a1, a2, b0, b1, b2, b3, c_ref, far_ref, out):
    tab = row_of(index, table)
    rows, half = c_ref.shape
    for i, ref in enumerate((b0, b1, b2, b3)):
        here = pl.ds(pl.multiple_of(tab[XAT + i] * rows, 8), rows)
        out[here, :half] = (a0[i] + a1[i] + a2[i]) * factor
        here = pl.ds(pl.multiple_of(lax.rem(tab[X] + i, 4) * rows, 8), rows)
        out[here, half:] = ref[...] * factor
    low = tab[OWN_HALF] == 0
    c, far = c_ref[...] * factor, far_ref[...] * factor
    out[4 * rows :, :half] = jnp.where(low, c, far)
    out[4 * rows :, half:] = jnp.where(low, far, c)


def last_kernel(index, table, own_ref, oth_ref, in_ref, out_ref):
    tab = row_of(index, table)
    count, half = in_ref.shape[0], in_ref.shape[1] // 2
    owner, zero = tab[IS_OWNER] == 1, tab[CORE] == 0
    in_ref[...] = jnp.where(owner, own_ref[:count], oth_ref[:count])
    own, oth = own_ref[count:], oth_ref[count:]
    for i in range(2):
        cut = slice(i * half, (i + 1) * half)
        out_ref[:, 2 * i * half : (2 * i + 1) * half] = jnp.where(zero, own[:, cut], oth[:, cut])
        out_ref[:, (2 * i + 1) * half : (2 * i + 2) * half] = jnp.where(
            zero, oth[:, cut], own[:, cut]
        )


def widen_kernel(n_ref, c_ref, n_out, c_out):
    n_out[...] = n_ref[...].astype(F32)
    c_out[...] = c_ref[...].astype(F32)


def widen(normed, cot):
    count, dim = normed.shape
    tile = pl.BlockSpec((count // 4, dim), lambda i: (i, 0))
    return pl.pallas_call(
        widen_kernel,
        grid=(4,),
        in_specs=[tile, tile],
        out_specs=[tile, tile],
        out_shape=[jax.ShapeDtypeStruct((count, dim), F32)] * 2,
        compiler_params=pltpu.CompilerParams(vmem_limit_bytes=OWN_LIMIT),
        cost_estimate=pl.CostEstimate(flops=2**20, bytes_accessed=8 * 2**20, transcendentals=0),
        name="widen",
    )(normed, cot)


def move(array, pairs):
    return lax.ppermute(array, AXES, pairs)


def total(terms):
    return functools.reduce(lambda p, q: p + q, terms)


def settle(array):
    return lax.optimization_barrier(array)


def twice(i):
    return 2 * i


def after(array, other):
    return lax.optimization_barrier((array, other))[0]


def local(normed, w_in, w_out, cotangent):
    dim = normed.shape[1]
    width = w_out.shape[1] // 4
    factor = (normed.shape[0] * lax.axis_size("dp") * lax.axis_size("grp")) ** (-0.5)
    index = lax.axis_index(AXES).reshape(1)
    place_at = index, jnp.asarray(TABLE.reshape(-1))
    win = w_in.reshape(2, 2, 2, width, dim)

    wide = widen(normed, cotangent)
    own = normed, cotangent
    other = move(wide[0], CORE_PAIRS), move(wide[1], CORE_PAIRS)
    terms = own_call(place_at, win, w_out, normed, cotangent)
    *first, oth0 = chunk_call(place_at, win, w_out, other, own, terms, 0)
    got_a0, got_b0, got_c0 = move(first[0], Z0), move(first[2], Y0), move(first[4], X0)
    index, _ = lax.optimization_barrier((index, first[0]))
    place_at = index, place_at[1]
    *second, oth1 = chunk_call(place_at, win, w_out, other, own, terms, 1)
    got_a1, got_b1, got_c1 = move(second[0], Z0), move(second[2], Y0), move(second[4], X0)

    oth0, index, got_a0, got_b0, early_c = lax.optimization_barrier(
        (oth0, index, got_a0, got_b0, first[5] + got_c0)
    )
    back_oth, back_own = back(place_at, terms[0], oth0, oth1, win)
    got_b1, back_own = lax.optimization_barrier((got_b1, back_own))
    grad_normed = (back_own + move(back_oth, CORE_PAIRS)).astype(BF)

    grp, dp = lax.axis_index("grp"), lax.axis_index("dp")
    own_first = ((dp >> 3) & 1) != ((grp >> 1) ^ (grp & (dp >> 2) & 1))

    rows = width // 2
    a = [second[1], got_a0]
    b = [first[3], got_b0], [second[3], got_b1]
    c = [early_c], [second[5], got_c1]
    to_b = sums([[(t, 0) for t in chunk] for chunk in b], rows, 1)
    got_b = move(to_b, Y1)
    c[1][1] = got_c1 = after(got_c1, to_b)
    to_c = jnp.where(own_first, total([second[5], got_c1]), early_c)
    got_c = move(to_c, X1)
    to_a = total([first[1], after(got_a1, to_c)])
    got_a = move(to_a, Z1)
    a = [settle(total(a)), got_a]
    b = [[(t, 4) for t in chunk] + [(got_b, 4 * k)] for k, chunk in enumerate(b)]
    c = [settle(jnp.where(own_first, total(c[0]), total(c[1]))), got_c]

    rows = width // 8
    to_b = sums(b, rows, 2)
    got_b = move(to_b, X0)
    b = [sums([[(t, at + 2) for t, at in chunk] for chunk in b], rows, 2), got_b]
    c[-1] = after(c[-1], to_b)
    to_c = total([t[:2] for t in c])
    got_c = move(to_c, Z0)
    c = [settle(total([t[2:] for t in c])), got_c]
    a[-1] = after(a[-1], to_c)
    to_a = total([t[:2] for t in a])
    got_a = move(to_a, Y0)
    a = [settle(total([t[2:] for t in a])), got_a]

    b[-1] = after(b[-1], to_a)
    to_b = sums([[(t, 0) for t in b]], rows, 2, twice)
    got_b = move(to_b, X1)
    b = [sums([[(t, 1) for t in b]], rows, 2, twice), got_b]
    c[-1] = after(c[-1], to_b)
    to_c = total([t[0] for t in c])
    got_c = move(to_c, Z1)
    c = [t[1] for t in c] + [got_c]
    a[-1] = after(a[-1], to_c)
    to_a = total([t[0] for t in a])
    got_a = move(to_a, Y1)

    rows = width // 16
    b[-1] = after(b[-1], to_a)
    to_b = sums([[(t, 2) for t in b]], rows, 2, lambda i: -2 * i)
    got_b = move(to_b, Z0)
    b = [sums([[(t, 1) for t in b]], rows, 2, twice)[0], got_b[0]]
    c[-1] = after(c[-1], to_b)
    to_c = total([t[:2] for t in c])
    got_c = move(to_c, Y0)
    c = [t[2:] for t in c] + [got_c]
    a = [(t, 4) for t in a] + [(after(got_a, to_c), 0)]
    to_a = sums([a], rows, 4, lambda i: (i + 2) % 4)
    got_a = move(to_a, X0)
    kept, grad_normed = settle((sums([a], rows, 4), grad_normed))
    a = [(kept, 0), (got_a, 0)]

    b[-1] = after(b[-1], to_a)
    to_b = total([t[0] for t in b])
    got_b = move(to_b, Z1)
    c[-1] = after(c[-1], to_b)
    to_c = total([t[0] for t in c])
    got_c = move(to_c, Y1)
    a[1] = after(got_a, to_c), 0
    to_a = sums([a], rows, 4, lambda i: i + 1 - 2 * (i % 2))
    got_a = move(to_a, X1)

    b = total([t[1] for t in b] + [after(got_b, to_a)])
    c = total([t[1] for t in c] + [after(got_c, to_a)])
    c_far = move(c, FAR_PAIRS)
    (packed_rows,) = small_call(
        functools.partial(gather_kernel, factor),
        [jax.ShapeDtypeStruct((5 * (dim // 32), dim), F32)],
        "gather",
        place_at,
        *(t[0] for t, _ in a),
        got_a[0],
        b,
        *(move(b, owner_pairs(shift)) for shift in (1, 2, 3)),
        c,
        c_far,
    )
    grad_in, grad_out = small_call(
        last_kernel,
        [
            jax.ShapeDtypeStruct((width // 4, dim), F32),
            jax.ShapeDtypeStruct((dim // 32, 4 * width), F32),
        ],
        "last",
        place_at,
        packed_rows,
        move(packed_rows, CORE_PAIRS),
    )
    return (grad_in, grad_out, grad_normed)


def solution(mesh):
    placed = (P(AXES, None), P(), P(), P(AXES, None))
    return jax.shard_map(
        local,
        mesh=mesh,
        in_specs=placed,
        out_specs=(P("dp", None), P("dp", None), P(AXES, None)),
        check_vma=False,
    )
```
